32 devices in a mesh: dp: 4 (over x, core), ctx: 2 (over y), tensor: 4 (over z).
Axes of the slice: x: 2, y: 2, z: 4, core: 2. Of those that a mesh axis runs over, the one named last changes fastest.
Arguments:
- tokens: bfloat16 [5120, 2304], P(('dp', 'ctx')), may hold values from -6 to 6
- segment: int32 [5120], P('dp'), may hold values from 0 to 2, as said below
- position: int32 [5120], P('dp'), may hold values from 0 to 1151, as said below
- gain_attn: float32 [2304], P('dp'), may hold values from 0.5 to 1.5
- w_query: float32 [2304, 2304], P('dp', 'tensor'), may hold values from -0.1875 to 0.1875
- w_key: float32 [2304, 2304], P('dp', 'tensor'), may hold values from -0.1875 to 0.1875
- w_value: float32 [2304, 2304], P('dp', 'tensor'), may hold values from -0.125 to 0.125
- w_out: float32 [2304, 2304], P('tensor', 'dp'), may hold values from -2 to 2
- gain_ffn: float32 [2304], P('dp'), may hold values from 0.5 to 1.5
- w_gate: float32 [2304, 5760], P('dp', 'tensor'), may hold values from -0.125 to 0.125
- w_up: float32 [2304, 5760], P('dp', 'tensor'), may hold values from -0.125 to 0.125
- w_down: float32 [5760, 2304], P('tensor', 'dp'), may hold values from -0.625 to 0.625
- cotangent: bfloat16 [5120, 2304], P(('dp', 'ctx')), may hold values from -6 to 6
Outputs:
- output: float32 [5120, 2304], P(('dp', 'ctx'))
- grad_tokens: float32 [5120, 2304], P(('dp', 'ctx'))
- grad_gain_attn: float32 [2304], P('dp')
- grad_w_query: float32 [2304, 2304], P('dp', 'tensor')
- grad_w_key: float32 [2304, 2304], P('dp', 'tensor')
- grad_w_value: float32 [2304, 2304], P('dp', 'tensor')
- grad_w_out: float32 [2304, 2304], P('tensor', 'dp')
- grad_gain_ffn: float32 [2304], P('dp')
- grad_w_gate: float32 [2304, 5760], P('dp', 'tensor')
- grad_w_up: float32 [2304, 5760], P('dp', 'tensor')
- grad_w_down: float32 [5760, 2304], P('tensor', 'dp')
The draws below stay inside these ranges and needn't reach their ends.
Inputs may be any that keep to these rules, and one draw needn't show every extreme that they name: Within each group of 1280 consecutive tokens the prompt (segment 0, 1024 tokens) and each continuation 1 to 2 (128 tokens each) fill one contiguous run, in an order drawn from the seed. `position`: positions count up from 0 along the prompt and from 1024 along each continuation.
All inputs are finite; a program needn't handle non-finite values.
Results may differ from the reference program's by a relative error of at most 0.025.
Values may be sent and summed in bfloat16 or wider, within the bound.
No kernel may reach another device: no remote copies, remote signals or barrier semaphores. Data moves between devices by JAX's collectives and lax.ppermute only.
A program may use at most 256 MiB of HBM per device.

```python
import math
import jax
import jax.numpy as jnp
from jax import lax

D = 2304
HEADS = 36
HEAD = 64
FF = 5760
PROMPT = 1024
CONTS = 2
CONT_LEN = 128
HQ = 2304
GROUP = 1280
TOKENS = 5120


def layout(key):
    group = PROMPT + CONTS * CONT_LEN
    count = TOKENS // group

    def one_group(sub):
        order = jax.random.permutation(sub, CONTS + 1).astype(jnp.int32)
        lengths = jnp.where(order == 0, PROMPT, CONT_LEN).astype(jnp.int32)
        ends = jnp.cumsum(lengths).astype(jnp.int32)
        starts = ends - lengths
        place = jnp.arange(group, dtype=jnp.int32)
        run = jnp.sum((place[:, None] >= ends[None, :]).astype(jnp.int32), axis=1)
        match = (run[:, None] == jnp.arange(CONTS + 1, dtype=jnp.int32)[None, :]).astype(jnp.int32)
        seg_ids = jnp.sum(match * order[None, :], axis=1)
        begin = jnp.sum(match * starts[None, :], axis=1)
        spots = place - begin + jnp.where(seg_ids == 0, 0, PROMPT).astype(jnp.int32)
        return (seg_ids, spots)
    seg_all, pos_all = jax.vmap(one_group)(jax.random.split(key, count))
    return (seg_all.reshape(TOKENS).astype(jnp.int32), pos_all.reshape(TOKENS).astype(jnp.int32))


def draw_segment(key, part):
    return layout(key)[0]


def draw_position(key, part):
    return layout(key)[1]


def block_scale(key, shape, pieces, smallest, high):
    def one(dim, parts):
        heights = jax.random.uniform(jax.random.fold_in(jax.random.fold_in(key, 6), dim), (parts,), jnp.float32, smallest / len(pieces), high / len(pieces))
        return jnp.repeat(jnp.exp(heights), shape[dim] // parts).reshape((-1,) + (1,) * (len(shape) - dim - 1))

    level = one(*pieces[0])
    for cut in pieces[1:]:
        level = level * one(*cut)
    return level


def bell_draw(key, shape, scale, bound, pieces=(), kind=jnp.bfloat16):
    array = jax.random.normal(key, shape, jnp.float32) * scale
    if len(pieces) > 0:
        array = block_scale(key, shape, pieces, -0.22, 0.18) * array
    return jnp.clip(array, min=-bound, max=bound).astype(kind)


def setup_inputs(seed: int = 0) -> dict:
    splits = jax.random.split(jax.random.key(seed), 14)
    return {
        "tokens": bell_draw(splits[0], (TOKENS, D), 1.0, 6.0, ((0, 8),)),
        "segment": draw_segment(jax.random.fold_in(splits[13], 71), 0),
        "position": draw_position(jax.random.fold_in(splits[13], 71), 0),
        "gain_attn": jnp.clip(1.0 + 0.1 * jax.random.normal(splits[3], (D,), jnp.float32), 0.5, 1.5),
        "w_query": bell_draw(splits[4], (D, HQ), (D // 2) ** -0.5, 0.1875, ((0, 4), (1, 4)), jnp.float32),
        "w_key": bell_draw(splits[5], (D, HQ), (D // 2) ** -0.5, 0.1875, ((0, 4), (1, 4)), jnp.float32),
        "w_value": bell_draw(splits[6], (D, HQ), D ** -0.5, 0.125, ((0, 4), (1, 4)), jnp.float32),
        "w_out": bell_draw(splits[7], (HQ, D), 8 ** -0.5, 2.0, ((0, 4), (1, 4)), jnp.float32),
        "gain_ffn": jnp.clip(1.0 + 0.1 * jax.random.normal(splits[8], (D,), jnp.float32), 0.5, 1.5),
        "w_gate": bell_draw(splits[9], (D, FF), D ** -0.5, 0.125, ((0, 4), (1, 4)), jnp.float32),
        "w_up": bell_draw(splits[10], (D, FF), D ** -0.5, 0.125, ((0, 4), (1, 4)), jnp.float32),
        "w_down": bell_draw(splits[11], (FF, D), (FF // 64) ** -0.5, 0.625, ((0, 4), (1, 4)), jnp.float32),
        "cotangent": bell_draw(splits[12], (TOKENS, D), 1.0, 6.0, ((0, 8),)),
    }


@jax.custom_vjp
def low(v):
    return lax.optimization_barrier(v.astype(jnp.bfloat16)).astype(jnp.float32)

@jax.custom_vjp
def low_back(v):
    return v

def low_keep(v):
    return (low(v), None)

def low_pass(kept, grad):
    return (grad,)

def back_keep(v):
    return (v, None)

def back_low(kept, grad):
    return (low(grad),)
low.defvjp(low_keep, low_pass)
low_back.defvjp(back_keep, back_low)
norm_eps = 1e-05
branch_scale = 1.4 / math.sqrt(40.0)
highest = lax.Precision.HIGHEST

def rope_tables(positions):
    freq = 10000.0 ** (-(jnp.arange(HEAD // 2, dtype=jnp.float32) * 2.0 / HEAD))
    angle = positions.astype(jnp.float32)[:, None] * freq[None, :]
    return (jnp.cos(angle), jnp.sin(angle))

def rotate(field, cosine, sine):
    heads = field.reshape(field.shape[0], -1, HEAD)
    half = HEAD // 2
    first = heads[:, :, :half]
    second = heads[:, :, half:]
    cos_b = cosine[:, None, :]
    sin_b = sine[:, None, :]
    turned = jnp.concatenate([first * cos_b - second * sin_b, second * cos_b + first * sin_b], axis=-1)
    return turned.reshape(field.shape)

def rms_norm(field, gain):
    inverse = lax.rsqrt(lax.optimization_barrier(jnp.mean(field * field, axis=-1, keepdims=True)) + norm_eps)
    return field * inverse * gain

def project(left, right):
    return jnp.dot(left, right, precision=highest, preferred_element_type=jnp.float32)

def group_attention(query, keys, values, seg_ids, positions):
    block = 512 if GROUP % 512 == 0 else GROUP
    count = GROUP // block

    def one_block(args):
        q_block, s_block, p_block = args
        score = jnp.einsum('qhd,khd->hqk', q_block, keys, precision=highest) * HEAD ** (-0.5)
        score = low_back(score)
        allowed = ((seg_ids[None, :] == s_block[:, None]) | (seg_ids[None, :] == 0)) & (positions[None, :] <= p_block[:, None])
        score = jnp.where(allowed[None, :, :], score, -1e+30)
        prob = low(jax.nn.softmax(score, axis=-1))
        return jnp.einsum('hqk,khd->qhd', prob, values, precision=highest)
    result = lax.map(jax.checkpoint(one_block), (query.reshape(count, block, HEADS, HEAD), seg_ids.reshape(count, block), positions.reshape(count, block)))
    return result.reshape(GROUP, HEADS * HEAD)

def layer(inputs, gain_a, wq, wk, wv, wo, gain_f, wg, wu, wd, segment, position):
    ga = low(gain_a)
    gf = low(gain_f)
    wq_r, wk_r, wv_r, wo_r = (low(wq), low(wk), low(wv), low(wo))
    wg_r, wu_r, wd_r = (low(wg), low(wu), low(wd))
    normed1 = low(rms_norm(inputs, ga))
    cosine, sine = rope_tables(position)
    q_pre = low_back(project(normed1, wq_r))
    k_pre = low_back(project(normed1, wk_r))
    values = low(low_back(project(normed1, wv_r)))
    query = low(rotate(q_pre, cosine, sine))
    keys = low(rotate(k_pre, cosine, sine))
    groups = TOKENS // GROUP
    shape4 = (groups, GROUP, HEADS, HEAD)

    def per_group(args):
        return group_attention(args[0], args[1], args[2], args[3], args[4])
    att = lax.map(per_group, (query.reshape(shape4), keys.reshape(shape4), values.reshape(shape4), segment.reshape(groups, GROUP), position.reshape(groups, GROUP)))
    att = low(low_back(att.reshape(TOKENS, HEADS * HEAD)))
    hidden_in = inputs + branch_scale * low_back(project(att, wo_r))
    normed2 = low(rms_norm(hidden_in, gf))
    gate = low_back(project(normed2, wg_r))
    up_val = low_back(project(normed2, wu_r))
    hidden = low(jax.nn.silu(gate) * up_val)
    return hidden_in + branch_scale * low_back(project(hidden, wd_r))

def reference(tokens, segment, position, gain_attn, w_query, w_key, w_value, w_out, gain_ffn, w_gate, w_up, w_down, cotangent):

    def forward(inputs, gain_a, wq, wk, wv, wo, gain_f, wg, wu, wd):
        return layer(inputs, gain_a, wq, wk, wv, wo, gain_f, wg, wu, wd, segment, position)
    output, pull = jax.vjp(forward, tokens.astype(jnp.float32), gain_attn, w_query, w_key, w_value, w_out, gain_ffn, w_gate, w_up, w_down)
    grads = pull(cotangent.astype(jnp.float32))
    return (output, grads[0], grads[1], grads[2], grads[3], grads[4], grads[5], grads[6], grads[7], grads[8], grads[9])
```

```python
import functools
import math

import jax
import jax.numpy as jnp
from jax import lax
from jax.experimental import pallas as pl
from jax.experimental.pallas import tpu as pltpu
from jax.sharding import PartitionSpec as P

HEAD = 64
LANES = 128
NEG = -1e30
norm_eps = 1e-05
branch_scale = 1.4 / math.sqrt(40.0)
bf = jnp.bfloat16
f32 = jnp.float32
MB = 1 << 20


def rope_tables(positions):
    freq = 10000.0 ** (-(jnp.arange(HEAD // 2, dtype=f32) * 2.0 / HEAD))
    angle = positions.astype(f32)[:, None] * freq[None, :]
    cosine, sine = jnp.cos(angle), jnp.sin(angle)
    cos_t = jnp.concatenate([cosine] * 4, axis=1)
    sin_t = jnp.concatenate([-sine, sine, -sine, sine], axis=1)
    return cos_t, sin_t


def rope_block(u, cos_t, sin_t, sign):
    lane = lax.broadcasted_iota(jnp.int32, u.shape, 1)
    low = (lane % HEAD) < HEAD // 2
    partner = jnp.where(low, pltpu.roll(u, LANES - HEAD // 2, 1), pltpu.roll(u, HEAD // 2, 1))
    return u * cos_t + sign * (partner * sin_t)


def dot(a, b, dims=((1,), (0,))):
    return lax.dot_general(a, b, (dims, ((), ())), preferred_element_type=f32)


def proj_kernel(rotary, n_ref, w_ref, cos_ref, sin_ref, o_ref, y_ref):
    feats = o_ref.shape[1]
    y_ref[:, :feats] = dot(n_ref[...], w_ref[...])
    for first in range(0, feats, LANES):
        size = min(LANES, feats - first)
        y = y_ref[:, first : first + LANES]
        if rotary:
            y = rope_block(y, cos_ref[...], sin_ref[...], 1.0)
        o_ref[:, first : first + size] = y[:, :size].astype(bf)


def project(normed, weight, cos_t, sin_t, rotary):
    rows, depth = normed.shape
    feats = weight.shape[1]
    padded = -(-feats // LANES) * LANES
    vm = pl.BlockSpec(memory_space=pltpu.VMEM)
    return pl.pallas_call(
        functools.partial(proj_kernel, rotary),
        out_shape=jax.ShapeDtypeStruct((rows, feats), bf),
        in_specs=[vm] * 4,
        out_specs=vm,
        scratch_shapes=[pltpu.VMEM((rows, padded), f32)],
        compiler_params=pltpu.CompilerParams(vmem_limit_bytes=40 * MB),
        cost_estimate=pl.CostEstimate(
            flops=2 * rows * depth * feats, bytes_accessed=2 * (rows * depth + depth * feats + rows * feats), transcendentals=0
        ),
    )(normed, weight, cos_t, sin_t)


def fill_bias(qseg_ref, qpos_ref, kseg_ref, kpos_ref, bias_ref):
    kseg = kseg_ref[...]
    allowed = ((kseg == qseg_ref[...]) | (kseg == 0)) & (kpos_ref[...] <= qpos_ref[...])
    bias_ref[...] = jnp.where(allowed, 0.0, NEG)


def attn_fwd_kernel(parts, feats, *refs):
    qseg, qpos = refs[:2]
    kseg, kpos = refs[2 : 2 + parts], refs[2 + parts : 2 + 2 * parts]
    rest = refs[2 + 2 * parts :]
    q_ref = rest[0]
    k_refs, v_refs = rest[1 : 1 + parts], rest[1 + parts : 1 + 2 * parts]
    o_ref, lse_ref = rest[1 + 2 * parts : 3 + 2 * parts]
    bias = rest[3 + 2 * parts : 3 + 3 * parts]
    ot_ref = rest[3 + 3 * parts]
    blk = pl.program_id(0)

    @pl.when(blk == 0)
    def _():
        for i in range(parts):
            fill_bias(qseg, qpos, kseg[i], kpos[i], bias[i])

    left = feats - blk * LANES

    def one(sub):
        lane = lax.broadcasted_iota(jnp.int32, (1, LANES), 1)
        mine = (lane >= sub * HEAD) & (lane < (sub + 1) * HEAD)
        valid = lane < left
        q = jnp.where(mine, q_ref[...] * 0.125, 0.0).astype(bf)
        scores = []
        best = None
        for i in range(parts):
            k = jnp.where(valid, k_refs[i][...], 0.0).astype(bf)
            s = dot(k, q, ((1,), (1,))) + bias[i][...]
            scores.append(s)
            top = jnp.max(s, axis=0, keepdims=True)
            best = top if best is None else jnp.maximum(best, top)
        total, acc = None, None
        for i in range(parts):
            p = jnp.exp(scores[i] - best)
            t = jnp.sum(p, axis=0, keepdims=True)
            v = jnp.where(valid, v_refs[i][...], 0.0).astype(bf)
            a = dot(v, p.astype(bf), ((0,), (0,)))
            total = t if total is None else total + t
            acc = a if acc is None else acc + a
        ot_ref[sub * HEAD : (sub + 1) * HEAD, :] = acc[sub * HEAD : (sub + 1) * HEAD, :] / total
        lse_ref[0, sub : sub + 1, :] = best + jnp.log(total)

    for sub in range(LANES // HEAD):
        pl.when(sub * HEAD < left)(functools.partial(one, sub))
    o_ref[...] = ot_ref[...].T.astype(bf)


def attn_specs(rows, key_rows, feats):
    blocks = -(-feats // LANES)
    row = pl.BlockSpec((1, rows), lambda h: (0, 0))
    cols = [pl.BlockSpec((n, 1), lambda h: (0, 0)) for n in key_rows]
    q = pl.BlockSpec((rows, LANES), lambda h: (0, h))
    ks = [pl.BlockSpec((n, LANES), lambda h: (0, h)) for n in key_rows]
    lse = pl.BlockSpec((1, 8, rows), lambda h: (h, 0, 0))
    return blocks, row, cols, q, ks, lse


def attention_fwd(q, keys, values, q_meta, k_metas):
    rows, feats = q.shape
    parts = len(keys)
    key_rows = [k.shape[0] for k in keys]
    count = sum(key_rows)
    blocks, row, cols, qs, ks, lse = attn_specs(rows, key_rows, feats)
    return pl.pallas_call(
        functools.partial(attn_fwd_kernel, parts, feats),
        grid=(blocks,),
        out_shape=(
            jax.ShapeDtypeStruct((rows, feats), bf),
            jax.ShapeDtypeStruct((blocks, 8, rows), f32),
        ),
        in_specs=[row, row] + cols + cols + [qs] + ks + ks,
        out_specs=(qs, lse),
        scratch_shapes=[pltpu.VMEM((n, rows), f32) for n in key_rows] + [pltpu.VMEM((LANES, rows), f32)],
        compiler_params=pltpu.CompilerParams(vmem_limit_bytes=56 * MB),
        cost_estimate=pl.CostEstimate(
            flops=16 * rows * count * feats, bytes_accessed=4 * (rows + count) * feats, transcendentals=rows * count * feats // HEAD
        ),
    )(
        q_meta[0][None, :], q_meta[1][None, :],
        *[m[0][:, None] for m in k_metas], *[m[1][:, None] for m in k_metas],
        q, *keys, *values,
    )


def attn_bwd_kernel(parts, feats, *refs):
    qseg, qpos, qcos, qsin = refs[:4]
    refs = refs[4:]
    take = lambda n: (refs[:n], refs[n:])
    kseg, refs = take(parts)
    kpos, refs = take(parts)
    kcos, refs = take(parts)
    ksin, refs = take(parts)
    (q_ref, att_ref, do_ref, lse_ref), refs = take(4)
    k_refs, refs = take(parts)
    v_refs, refs = take(parts)
    (dq_ref,), refs = take(1)
    dk_refs, refs = take(parts)
    dv_refs, refs = take(parts)
    bias, refs = take(parts)
    dqt_ref, refs = refs[0], refs[1:]
    dka, refs = take(parts)
    dva, refs = take(parts)
    blk = pl.program_id(0)

    @pl.when(blk == 0)
    def _():
        for i in range(parts):
            fill_bias(qseg, qpos, kseg[i], kpos[i], bias[i])

    left = feats - blk * LANES
    valid = lax.broadcasted_iota(jnp.int32, (1, LANES), 1) < left
    prod = jnp.where(valid, do_ref[...].astype(f32) * att_ref[...].astype(f32), 0.0).T

    def one(sub):
        lane = lax.broadcasted_iota(jnp.int32, (1, LANES), 1)
        mine = (lane >= sub * HEAD) & (lane < (sub + 1) * HEAD)
        q = jnp.where(mine, q_ref[...] * 0.125, 0.0).astype(bf)
        do = jnp.where(mine, do_ref[...], 0.0).astype(bf)
        lse = lse_ref[0, sub : sub + 1, :]
        delta = jnp.sum(prod[sub * HEAD : (sub + 1) * HEAD, :], axis=0, keepdims=True)
        dqt = None
        for i in range(parts):
            k = jnp.where(valid, k_refs[i][...], 0.0).astype(bf)
            v = jnp.where(valid, v_refs[i][...], 0.0).astype(bf)
            p = jnp.exp(dot(k, q, ((1,), (1,))) + bias[i][...] - lse)
            dp = dot(v, do, ((1,), (1,)))
            ds = (p * (dp - delta)).astype(bf)
            dv = dot(p.astype(bf), do)
            dk = dot(ds, q)
            if sub == 0:
                dva[i][...] = dv
                dka[i][...] = dk
            else:
                dva[i][...] += dv
                dka[i][...] += dk
            d = dot(k, ds, ((0,), (0,)))
            dqt = d if dqt is None else dqt + d
        dqt_ref[sub * HEAD : (sub + 1) * HEAD, :] = dqt[sub * HEAD : (sub + 1) * HEAD, :] * 0.125

    for sub in range(LANES // HEAD):
        pl.when(sub * HEAD < left)(functools.partial(one, sub))
    dq_ref[...] = rope_block(dqt_ref[...].T, qcos[...], qsin[...], -1.0).astype(bf)
    for i in range(parts):
        dk_refs[i][...] = rope_block(dka[i][...], kcos[i][...], ksin[i][...], -1.0).astype(bf)
        dv_refs[i][...] = dva[i][...].astype(bf)


def attention_bwd(q, att, grad_att, lse, keys, values, q_meta, k_metas):
    rows, feats = q.shape
    parts = len(keys)
    key_rows = [k.shape[0] for k in keys]
    count = sum(key_rows)
    blocks, row, cols, qs, ks, lses = attn_specs(rows, key_rows, feats)
    tab = pl.BlockSpec((rows, LANES), lambda h: (0, 0))
    tabs = [pl.BlockSpec((n, LANES), lambda h: (0, 0)) for n in key_rows]
    out = pl.pallas_call(
        functools.partial(attn_bwd_kernel, parts, feats),
        grid=(blocks,),
        out_shape=(jax.ShapeDtypeStruct((rows, feats), bf),)
        + tuple(jax.ShapeDtypeStruct((n, feats), bf) for n in key_rows) * 2,
        in_specs=[row, row, tab, tab] + cols + cols + tabs + tabs + [qs, qs, qs, lses] + ks + ks,
        out_specs=(qs,) + tuple(ks) + tuple(ks),
        scratch_shapes=[pltpu.VMEM((n, rows), f32) for n in key_rows]
        + [pltpu.VMEM((LANES, rows), f32)]
        + [pltpu.VMEM((n, LANES), f32) for n in key_rows] * 2,
        compiler_params=pltpu.CompilerParams(vmem_limit_bytes=56 * MB),
        cost_estimate=pl.CostEstimate(
            flops=40 * rows * count * feats, bytes_accessed=10 * (rows + count) * feats, transcendentals=rows * count * feats // HEAD
        ),
    )(
        q_meta[0][None, :], q_meta[1][None, :], q_meta[2], q_meta[3],
        *[m[0][:, None] for m in k_metas], *[m[1][:, None] for m in k_metas],
        *[m[2] for m in k_metas], *[m[3] for m in k_metas],
        q, att, grad_att, lse, *keys, *values,
    )
    return out[0], out[1 : 1 + parts], out[1 + parts :]


def swap(n, bit):
    return [(i, i ^ bit) for i in range(n)]


def power_of_two(n):
    return n & (n - 1) == 0


def sum_all(value, sizes):
    for axis, n in sizes:
        if power_of_two(n):
            bit = 1
            while bit < n:
                value = value + lax.ppermute(value, axis, swap(n, bit))
                bit *= 2
        else:
            value = lax.psum(value, axis)
    return value


def line_scatter(chunk, n, me, axis):
    ahead, behind = None, None
    for step in range(n - 1):
        fore = chunk(jnp.clip(me + (n - 1 - step), 0, n - 1))
        back = chunk(jnp.clip(me - (n - 1 - step), 0, n - 1))
        if step > 0:
            fore, back = fore + ahead.astype(f32), back + behind.astype(f32)
        ahead = lax.ppermute(fore.astype(bf), axis, [(i, i + 1) for i in range(step + 1)])
        behind = lax.ppermute(back.astype(bf), axis, [(i, i - 1) for i in range(n - 1 - step, n)])
    own = chunk(me)
    if n == 1:
        return own
    return own + ahead.astype(f32) + behind.astype(f32)


def line_gather(own, n, me, axis):
    rows = own.shape[0]
    ahead, behind, fores, backs = own, own, [], []
    for step in range(n - 1):
        ahead = lax.ppermute(ahead, axis, [(i, i + 1) for i in range(step, n - 1)])
        behind = lax.ppermute(behind, axis, [(i, i - 1) for i in range(1, n - step)])
        fores.append(ahead)
        backs.append(behind)
    out = jnp.concatenate([own] * n, axis=0)
    for step in range(n - 1):
        out = lax.dynamic_update_slice_in_dim(out, fores[step] + backs[n - 2 - step], ((me + n - 1 - step) % n) * rows, 0)
    return out


def gather_weight(shard, n, me):
    if n != 4:
        return lax.all_gather(shard, "dp", axis=0, tiled=True)
    rows = shard.shape[0]
    far = lax.ppermute(shard, "dp", swap(4, 2))
    near = lax.ppermute(shard, "dp", swap(4, 1))
    cross = lax.ppermute(far, "dp", swap(4, 1))
    out = jnp.concatenate([shard] * n, axis=0)
    for bit, part in ((1, near), (2, far), (3, cross)):
        out = lax.dynamic_update_slice_in_dim(out, part, (me ^ bit) * rows, 0)
    return out


def relative_rows(array, n, me):
    rows = array.shape[0] // n
    return [lax.dynamic_slice_in_dim(array, (me ^ j) * rows, rows, 0) for j in range(n)]


def reduce_weight(left_t, right, n, me, n_ctx):
    if n == 4:
        b0, b1, b2, b3 = [dot(part, right).astype(bf) for part in left_t]
        r1 = lax.ppermute(b1, "dp", swap(4, 1))
        r3 = lax.ppermute(b3, "dp", swap(4, 1))
        a0 = b0.astype(f32) + r1.astype(f32)
        a2 = (b2.astype(f32) + r3.astype(f32)).astype(bf)
        total = a0 + lax.ppermute(a2, "dp", swap(4, 2)).astype(f32)
    else:
        total = lax.psum_scatter(dot(left_t, right).astype(bf), "dp", scatter_dimension=0, tiled=True).astype(f32)
    total = lax.optimization_barrier(total.astype(bf))
    if n_ctx == 2:
        return total.astype(f32) + lax.ppermute(total, "ctx", swap(2, 1)).astype(f32)
    return lax.psum(total, "ctx").astype(f32)


def per_device(
    n_dp, n_ctx, n_tp,
    tokens, segment, position, gain_attn, w_query, w_key, w_value, w_out, gain_ffn, w_gate, w_up, w_down, cotangent,
):
    dp, ctx, me = lax.axis_index("dp"), lax.axis_index("ctx"), lax.axis_index("tensor")
    rows = tokens.shape[0]
    piece = rows // n_tp
    mine = functools.partial(lax.dynamic_slice_in_dim, start_index=me * piece, slice_size=piece, axis=0)

    wk, wv, wq, wo, wg, wu, wd = [
        gather_weight(w, n_dp, dp)
        for w in (
            w_key.astype(bf), w_value.astype(bf), w_query.astype(bf), w_out.astype(bf).T,
            w_gate.astype(bf), w_up.astype(bf), w_down.T.astype(bf),
        )
    ]
    gains = lax.all_gather(jnp.stack([gain_attn, gain_ffn]).astype(bf), "dp", axis=1, tiled=True).astype(f32)
    gain1, gain2 = gains[0], gains[1]

    def meta(start, size):
        seg = lax.dynamic_slice_in_dim(segment, start, size)
        pos = lax.dynamic_slice_in_dim(position, start, size)
        return (seg, pos) + rope_tables(pos)

    q_meta = meta(ctx * rows, rows)
    cos_t, sin_t = q_meta[2:]
    inputs = tokens.astype(f32)
    scale1 = lax.rsqrt(jnp.mean(inputs * inputs, axis=-1, keepdims=True) + norm_eps)
    normed1 = (inputs * scale1 * gain1).astype(bf)
    keys = project(normed1, wk, cos_t, sin_t, True)
    values = project(normed1, wv, cos_t, sin_t, False)
    query = project(normed1, wq, cos_t, sin_t, True)
    if n_ctx == 2:
        trade = lambda a: lax.ppermute(a, "ctx", swap(2, 1))
        keys_all, values_all = [keys, trade(keys)], [values, trade(values)]
        k_metas = [q_meta, meta((1 - ctx) * rows, rows)]
    else:
        spread = lambda a: [lax.all_gather(a, "ctx", axis=0, tiled=True)]
        keys_all, values_all = spread(keys), spread(values)
        k_metas = [meta(0, segment.shape[0])]

    att, lse = attention_fwd(query, keys_all, values_all, q_meta, k_metas)

    def chunk_of(array):
        return lambda i: lax.dynamic_slice_in_dim(array, i * piece, piece, 0).astype(f32)

    mixed = line_scatter(chunk_of(dot(att, wo, ((1,), (1,)))), n_tp, me, "tensor")
    hidden_in = mine(inputs) + branch_scale * mixed
    scale2 = lax.rsqrt(jnp.mean(hidden_in * hidden_in, axis=-1, keepdims=True) + norm_eps)
    normed2 = line_gather((hidden_in * scale2 * gain2).astype(bf), n_tp, me, "tensor")

    grad_out = cotangent.astype(f32)
    grad_ffn = (branch_scale * grad_out).astype(bf)
    grad_hidden = dot(grad_ffn, wd)
    gate = dot(normed2, wg)
    up_val = dot(normed2, wu)
    sigma = jax.nn.sigmoid(gate)
    active = gate * sigma
    hidden = (active * up_val).astype(bf)
    grad_gate = (grad_hidden * up_val * sigma * (1.0 + gate * (1.0 - sigma))).astype(bf)
    grad_up = (grad_hidden * active).astype(bf)
    partial2 = dot(grad_gate, wg, ((1,), (1,))) + dot(grad_up, wu, ((1,), (1,)))
    grad_norm2 = line_scatter(chunk_of(partial2), n_tp, me, "tensor")
    part_g2 = jnp.sum(grad_norm2 * hidden_in * scale2, axis=0)
    grad_h = (
        mine(grad_out)
        + scale2 * gain2 * grad_norm2
        - hidden_in * scale2**3 * jnp.mean(hidden_in * gain2 * grad_norm2, axis=-1, keepdims=True)
    )
    grad_mixed = line_gather((branch_scale * grad_h).astype(bf), n_tp, me, "tensor")

    ffn_part = line_scatter(chunk_of(dot(hidden, wd, ((1,), (1,)))), n_tp, me, "tensor")
    output = hidden_in + branch_scale * ffn_part
    output = line_gather(lax.optimization_barrier(output.astype(bf)), n_tp, me, "tensor").astype(f32)

    grad_att = dot(grad_mixed, wo).astype(bf)
    grad_q, grad_ks, grad_vs = attention_bwd(query, att, grad_att, lse, keys_all, values_all, q_meta, k_metas)
    if n_ctx == 2:
        merge = lambda pair: (pair[0].astype(f32) + trade(pair[1]).astype(f32)).astype(bf)
    else:
        merge = lambda whole: lax.psum_scatter(whole[0], "ctx", scatter_dimension=0, tiled=True)
    grad_k, grad_v = merge(grad_ks), merge(grad_vs)

    partial1 = (
        dot(grad_q, wq, ((1,), (1,))) + dot(grad_k, wk, ((1,), (1,))) + dot(grad_v, wv, ((1,), (1,)))
    )
    grad_norm1 = line_scatter(chunk_of(partial1), n_tp, me, "tensor")
    my_in, my_scale = mine(inputs), mine(scale1)
    part_g1 = jnp.sum(grad_norm1 * my_in * my_scale, axis=0)
    grad_in = (
        grad_h
        + my_scale * gain1 * grad_norm1
        - my_in * my_scale**3 * jnp.mean(my_in * gain1 * grad_norm1, axis=-1, keepdims=True)
    )
    grad_in = line_gather(lax.optimization_barrier(grad_in.astype(bf)), n_tp, me, "tensor").astype(f32)
    gain_sum = sum_all(jnp.stack([part_g1, part_g2]), (("tensor", n_tp), ("ctx", n_ctx), ("dp", n_dp)))
    shard = gain_attn.shape[0]
    gain_sum = lax.dynamic_slice_in_dim(gain_sum, dp * shard, shard, 1)

    order = (lambda a: relative_rows(a.T, n_dp, dp)) if n_dp == 4 else (lambda a: a.T)
    n1_t, n2_t = order(normed1), order(normed2)
    da_t, df_t = order(grad_mixed), order(grad_ffn)
    reduce = lambda left, right: reduce_weight(left, right, n_dp, dp, n_ctx)
    sum_wd = reduce(df_t, hidden).T
    sum_wg = reduce(n2_t, grad_gate)
    sum_wu = reduce(n2_t, grad_up)
    sum_wo = reduce(da_t, att).T
    sum_wq = reduce(n1_t, grad_q)
    sum_wk = reduce(n1_t, grad_k)
    sum_wv = reduce(n1_t, grad_v)
    return (output, grad_in, gain_sum[0], sum_wq, sum_wk, sum_wv, sum_wo, gain_sum[1], sum_wg, sum_wu, sum_wd)


def solution(mesh):
    rows, col, row = P(("dp", "ctx"), None), P("dp", "tensor"), P("tensor", "dp")
    sizes = (mesh.shape["dp"], mesh.shape["ctx"], mesh.shape["tensor"])
    return jax.shard_map(
        functools.partial(per_device, *sizes),
        mesh=mesh,
        in_specs=(rows, P("dp"), P("dp"), P("dp"), col, col, col, row, P("dp"), col, col, row, rows),
        out_specs=(rows, rows, P("dp"), col, col, col, row, P("dp"), col, col, row),
        check_vma=False,
    )
```

```python
import functools
import math

import jax
import jax.numpy as jnp
from jax import lax
from jax.experimental import pallas as pl
from jax.experimental.pallas import tpu as pltpu
from jax.sharding import PartitionSpec as P

HEAD = 64
LANES = 128
NEG = -1e30
norm_eps = 1e-05
branch_scale = 1.4 / math.sqrt(40.0)
bf = jnp.bfloat16
f32 = jnp.float32
MB = 1 << 20


def rope_tables(positions):
    freq = 10000.0 ** (-(jnp.arange(HEAD // 2, dtype=f32) * 2.0 / HEAD))
    angle = positions.astype(f32)[:, None] * freq[None, :]
    cosine, sine = jnp.cos(angle), jnp.sin(angle)
    cos_t = jnp.concatenate([cosine] * 4, axis=1)
    sin_t = jnp.concatenate([-sine, sine, -sine, sine], axis=1)
    return cos_t, sin_t


def rope_block(u, cos_t, sin_t, sign):
    lane = lax.broadcasted_iota(jnp.int32, u.shape, 1)
    low = (lane % HEAD) < HEAD // 2
    partner = jnp.where(low, pltpu.roll(u, LANES - HEAD // 2, 1), pltpu.roll(u, HEAD // 2, 1))
    return u * cos_t + sign * (partner * sin_t)


def dot(a, b, dims=((1,), (0,))):
    return lax.dot_general(a, b, (dims, ((), ())), preferred_element_type=f32)


def up_to(n, unit):
    return -(-n // unit) * unit


COST = pl.CostEstimate(flops=1024, bytes_accessed=1024, transcendentals=0)


def fetch(offs_ref, shards, scratch, sems, width):
    copies = []
    for b in range(scratch.shape[1] // width):
        row = []
        for j, ref in enumerate(shards):
            rows = min(ref.shape[0], scratch.shape[0] // min(len(shards), 4))
            first = pl.multiple_of(offs_ref[j], 16)
            copy = pltpu.make_async_copy(
                ref.at[pl.ds(0, rows), pl.ds(b * width, width)],
                scratch.at[pl.ds(first, rows), pl.ds(b * width, width)],
                sems.at[b, j],
            )
            copy.start()
            row.append(copy)
        copies.append(row)
    return copies


def wait_all(copies):
    for copy in copies:
        copy.wait()


HBM = pl.BlockSpec(memory_space=pltpu.HBM)
VM = pl.BlockSpec(memory_space=pltpu.VMEM)
SM = pl.BlockSpec(memory_space=pltpu.SMEM)


def params(mbytes):
    return pltpu.CompilerParams(vmem_limit_bytes=mbytes * MB)


def proj_kernel(ns, rotary, offs, n_ref, cos_ref, sin_ref, *rest):
    shards, (o_ref, w_ref, sems) = rest[:ns], rest[ns:]
    copies = fetch(offs, shards, w_ref, sems, w_ref.shape[1])
    wait_all(copies[0])
    y = dot(n_ref[...], w_ref[...])
    for first in range(0, o_ref.shape[1], LANES):
        u = y[:, first : first + LANES]
        if rotary:
            u = rope_block(u, cos_ref[...], sin_ref[...], 1.0)
        o_ref[:, first : first + LANES] = u.astype(bf)


def project(normed, weight, cos_t, sin_t, rotary):
    offs, shards = weight
    rows, depth = normed.shape
    feats = shards[0].shape[1]
    ns = len(shards)
    return pl.pallas_call(
        functools.partial(proj_kernel, ns, rotary),
        out_shape=jax.ShapeDtypeStruct((rows, feats), bf),
        in_specs=[SM, VM, VM, VM] + [HBM] * ns,
        out_specs=VM,
        scratch_shapes=[pltpu.VMEM((depth, feats), bf), pltpu.SemaphoreType.DMA((1, ns))],
        compiler_params=params(16),
        cost_estimate=COST,
    )(offs, normed, cos_t, sin_t, *shards)


def wide_kernel(ns, nt, width, offs, a_ref, *rest):
    shards, (o_ref, w_ref, sems) = rest[:ns], rest[ns:]
    if nt:
        for row in fetch(offs, shards, w_ref, sems, w_ref.shape[1]):
            wait_all(row)
        for first in range(0, o_ref.shape[1], width):
            part = slice(first, first + width)
            o_ref[:, part] = dot(a_ref[...], w_ref[part, :], ((1,), (1,))).astype(o_ref.dtype)
    else:
        for b, row in enumerate(fetch(offs, shards, w_ref, sems, width)):
            wait_all(row)
            part = slice(b * width, (b + 1) * width)
            o_ref[:, part] = dot(a_ref[...], w_ref[:, part]).astype(o_ref.dtype)


def wide_matmul(a, weight, nt, dtype, width=256):
    offs, shards = weight
    rows = a.shape[0]
    ns = len(shards)
    depth, feats = sum(s.shape[0] for s in shards), shards[0].shape[1]
    if feats % width and not nt:
        width = feats
    return pl.pallas_call(
        functools.partial(wide_kernel, ns, nt, width),
        out_shape=jax.ShapeDtypeStruct((rows, depth if nt else feats), dtype),
        in_specs=[SM, VM] + [HBM] * ns,
        out_specs=VM,
        scratch_shapes=[pltpu.VMEM((depth, feats), bf), pltpu.SemaphoreType.DMA((feats // width, ns))],
        compiler_params=params(20),
        cost_estimate=COST,
    )(offs, a, *shards)


def qkv_back_kernel(ns, offs, x_ref, scale_ref, *rest):
    grads, rest = rest[:3], rest[3:]
    shards, (o_ref, gain_ref, w_ref, sems) = rest[: 3 * ns], rest[3 * ns :]
    rows = [fetch(offs, shards[i * ns : (i + 1) * ns], w_ref.at[i], sems.at[i], w_ref.shape[2])[0] for i in range(3)]
    for row in rows:
        wait_all(row)
    width = 256
    for first in range(0, o_ref.shape[1], width):
        part = slice(first, first + width)
        total = None
        for i in range(3):
            y = dot(grads[i][...], w_ref[i, part, :], ((1,), (1,)))
            total = y if total is None else total + y
        o_ref[:, part] = total.astype(bf)
        gain_ref[:, part] = jnp.sum(total * (x_ref[:, part].astype(f32) * scale_ref[...]), axis=0, keepdims=True)


def qkv_back(grads, weights, tokens, scale):
    offs = weights[0][0]
    shards = [s for w in weights for s in w[1]]
    ns = len(weights[0][1])
    rows, feats = grads[0].shape
    depth = sum(s.shape[0] for s in weights[2][1])
    return pl.pallas_call(
        functools.partial(qkv_back_kernel, ns),
        out_shape=(jax.ShapeDtypeStruct((rows, depth), bf), jax.ShapeDtypeStruct((1, depth), f32)),
        in_specs=[SM] + [VM] * 5 + [HBM] * (3 * ns),
        out_specs=(VM, VM),
        scratch_shapes=[pltpu.VMEM((3, depth, feats), bf), pltpu.SemaphoreType.DMA((3, 1, ns))],
        compiler_params=params(28),
        cost_estimate=COST,
    )(offs, tokens, scale, *grads, *shards)


def ffn_kernel(ns, width, offs, n_hbm, dh_hbm, *rest):
    g_shards, u_shards, rest = rest[:ns], rest[ns : 2 * ns], rest[2 * ns :]
    outs, dn_hbm, rest = rest[:3], rest[3], rest[4:]
    n_ref, dh_ref, wg, wu, mids, dn_ref, w_sems, in_sems, out_sems = rest
    hidden, depth = dh_ref.shape[1], n_ref.shape[1]
    blocks = [slice(f, min(f + width, hidden)) for f in range(0, hidden, width)]
    span = lambda part: pl.ds(part.start, part.stop - part.start)

    def load(b):
        part = span(blocks[b])
        copies = [pltpu.make_async_copy(dh_hbm.at[:, part], dh_ref.at[:, part], in_sems.at[b + 1])]
        for i, (shards, scratch) in enumerate(((g_shards, wg), (u_shards, wu))):
            for j, ref in enumerate(shards):
                first = pl.multiple_of(offs[j], 16)
                there = scratch.at[pl.ds(first, ref.shape[0]), part]
                copies.append(pltpu.make_async_copy(ref.at[:, part], there, w_sems.at[i, b, j]))
        for copy in copies:
            copy.start()
        return copies

    first = pltpu.make_async_copy(n_hbm, n_ref, in_sems.at[0])
    first.start()
    loads = [load(0)]
    first.wait()
    stores = []
    for b, part in enumerate(blocks):
        wait_all(loads[b])
        if b + 1 < len(blocks):
            loads.append(load(b + 1))
        gate = dot(n_ref[...], wg[:, part])
        up = dot(n_ref[...], wu[:, part])
        sigma = jax.nn.sigmoid(gate)
        active = gate * sigma
        dh = dh_ref[:, part]
        mids[0, :, part] = (active * up).astype(bf)
        mids[1, :, part] = (dh * up * sigma * (1.0 + gate * (1.0 - sigma))).astype(bf)
        mids[2, :, part] = (dh * active).astype(bf)
        for i in range(3):
            copy = pltpu.make_async_copy(mids.at[i, :, span(part)], outs[i].at[:, span(part)], out_sems.at[i, b])
            copy.start()
            stores.append(copy)
    for b, f in enumerate(range(0, depth, 768)):
        part = slice(f, f + 768)
        total = dot(mids[1], wg[part, :], ((1,), (1,))) + dot(mids[2], wu[part, :], ((1,), (1,)))
        dn_ref[:, part] = total.astype(bf)
        copy = pltpu.make_async_copy(dn_ref.at[:, span(part)], dn_hbm.at[:, span(part)], out_sems.at[3, b])
        copy.start()
        stores.append(copy)
    wait_all(stores)


def ffn(normed, grad_hidden, w_gate, w_up, width=512):
    offs, g_shards = w_gate
    ns = len(g_shards)
    rows, depth = normed.shape
    hidden = g_shards[0].shape[1]
    blocks = -(-hidden // width)
    mid = jax.ShapeDtypeStruct((rows, hidden), bf)
    return pl.pallas_call(
        functools.partial(ffn_kernel, ns, width),
        out_shape=(mid, mid, mid, jax.ShapeDtypeStruct((rows, depth), bf)),
        in_specs=[SM] + [HBM] * (2 + 2 * ns),
        out_specs=(HBM,) * 4,
        scratch_shapes=[
            pltpu.VMEM((rows, depth), bf),
            pltpu.VMEM((rows, hidden), f32),
            pltpu.VMEM((depth, hidden), bf),
            pltpu.VMEM((depth, hidden), bf),
            pltpu.VMEM((3, rows, hidden), bf),
            pltpu.VMEM((rows, depth), bf),
            pltpu.SemaphoreType.DMA((2, blocks, ns)),
            pltpu.SemaphoreType.DMA((blocks + 1,)),
            pltpu.SemaphoreType.DMA((4, max(blocks, depth // 768))),
        ],
        compiler_params=params(60),
        cost_estimate=COST,
    )(offs, normed, grad_hidden, *g_shards, *w_up[1])


def mix_kernel(spans, me_ref, offs, att_ref, x_ref, gain_ref, *rest):
    ns = len(spans)
    shards, (n_ref, own_ref, wo_hbm, w_ref, h_ref, sems) = rest[:ns], rest[ns:]
    copies = []
    for j, (ref, (z0, z1)) in enumerate(zip(shards, spans)):
        rows = pl.ds(pl.multiple_of(offs[j], 16), ref.shape[1])
        copies.append(pltpu.make_async_copy(ref, w_ref.at[z0:z1, rows, :], sems.at[j]))
        copies[-1].start()
    wait_all(copies)
    keep = pltpu.make_async_copy(w_ref.at[me_ref[0]], wo_hbm, sems.at[ns])
    keep.start()
    depth = h_ref.shape[1]
    width = 768
    for f in range(0, depth, width):
        part = slice(f, f + width)
        total = None
        for z in range(att_ref.shape[0]):
            y = dot(att_ref[z], w_ref[z, part, :], ((1,), (1,)))
            total = y if total is None else total + y
        h_ref[:, part] = x_ref[:, part].astype(f32) + branch_scale * total
    step = min(128, h_ref.shape[0])
    for f in range(0, h_ref.shape[0], step):
        part = slice(f, f + step)
        h = h_ref[part, :]
        scale = lax.rsqrt(jnp.mean(h * h, axis=-1, keepdims=True) + norm_eps)
        n_ref[part, :] = (h * scale * gain_ref[...]).astype(bf)
    piece = own_ref.shape[0]
    own_ref[...] = h_ref[pl.ds(pl.multiple_of(me_ref[0] * piece, 8), piece), :]
    keep.wait()


def mix(att, tokens, gain, offs, pieces, me):
    n, rows, feats = att.shape
    depth = tokens.shape[1]
    spans, shards = [p[0] for p in pieces], [p[1] for p in pieces]
    return pl.pallas_call(
        functools.partial(mix_kernel, spans),
        out_shape=(
            jax.ShapeDtypeStruct((rows, depth), bf),
            jax.ShapeDtypeStruct((rows // n, depth), f32),
            jax.ShapeDtypeStruct((depth, feats), bf),
        ),
        in_specs=[SM, SM, VM, VM, VM] + [HBM] * len(shards),
        out_specs=(VM, VM, HBM),
        scratch_shapes=[
            pltpu.VMEM((n, depth, feats), bf),
            pltpu.VMEM((rows, depth), f32),
            pltpu.SemaphoreType.DMA((len(shards) + 1,)),
        ],
        compiler_params=params(56),
        cost_estimate=COST,
    )(me[None], offs, att, tokens, gain[None, :], *shards)


def grad_kernel(offs, a_ref, b_ref, keep_ref, send_ref, at_ref):
    at_ref[...] = a_ref[...].T
    block = keep_ref.shape[0] // 2
    for j in range(4):
        left = at_ref[pl.ds(pl.multiple_of(offs[j], 16), block), :]
        ref = send_ref if j % 2 else keep_ref
        ref[(j // 2) * block : (j // 2 + 1) * block, :] = dot(left, b_ref[...]).astype(bf)


def weight_grad(a, b, offs):
    rows, depth = a.shape
    feats = b.shape[1]
    half = jax.ShapeDtypeStruct((depth // 2, feats), bf)
    return pl.pallas_call(
        grad_kernel,
        out_shape=(half, half),
        in_specs=[SM, VM, VM],
        out_specs=(VM, VM),
        scratch_shapes=[pltpu.VMEM((depth, rows), bf)],
        compiler_params=params(20),
        cost_estimate=COST,
    )(offs, a, b)


def fill_bias(qseg_ref, qpos_ref, kseg_ref, kpos_ref, bias_ref):
    kseg = kseg_ref[...]
    allowed = ((kseg == qseg_ref[...]) | (kseg == 0)) & (kpos_ref[...] <= qpos_ref[...])
    bias_ref[...] = jnp.where(allowed, 0.0, NEG)


def attn_fwd_kernel(parts, heads, *refs):
    qseg, qpos = refs[:2]
    kseg, kpos = refs[2 : 2 + parts], refs[2 + parts : 2 + 2 * parts]
    rest = refs[2 + 2 * parts :]
    q_ref = rest[0]
    k_refs, v_refs = rest[1 : 1 + parts], rest[1 + parts : 1 + 2 * parts]
    o_ref, lse_ref = rest[1 + 2 * parts : 3 + 2 * parts]
    bias = rest[3 + 2 * parts : 3 + 3 * parts]
    ot_ref = rest[3 + 3 * parts]
    blk = pl.program_id(0)

    @pl.when(blk == 0)
    def _():
        for i in range(parts):
            fill_bias(qseg, qpos, kseg[i], kpos[i], bias[i])

    ot_ref[...] = jnp.zeros_like(ot_ref)
    lse_ref[...] = jnp.zeros_like(lse_ref)

    def one(sub):
        lane = lax.broadcasted_iota(jnp.int32, (1, LANES), 1)
        mine = (lane >= sub * HEAD) & (lane < (sub + 1) * HEAD)
        q = jnp.where(mine, q_ref[...] * 0.125, 0.0).astype(bf)
        scores = []
        best = None
        for i in range(parts):
            k = k_refs[i][...]
            s = dot(k, q, ((1,), (1,))) + bias[i][...]
            scores.append(s)
            top = jnp.max(s, axis=0, keepdims=True)
            best = top if best is None else jnp.maximum(best, top)
        total, acc = None, None
        for i in range(parts):
            p = jnp.exp(scores[i] - best)
            t = jnp.sum(p, axis=0, keepdims=True)
            v = v_refs[i][...]
            a = dot(v, p.astype(bf), ((0,), (0,)))
            total = t if total is None else total + t
            acc = a if acc is None else acc + a
        ot_ref[sub * HEAD : (sub + 1) * HEAD, :] = acc[sub * HEAD : (sub + 1) * HEAD, :] / total
        lse_ref[0, sub : sub + 1, :] = best + jnp.log(total)

    for sub in range(LANES // HEAD):
        pl.when(blk * (LANES // HEAD) + sub < heads)(functools.partial(one, sub))
    o_ref[...] = ot_ref[...].T.astype(bf)


def attn_specs(rows, key_rows, feats):
    blocks = -(-feats // LANES)
    row = pl.BlockSpec((1, rows), lambda h: (0, 0))
    cols = [pl.BlockSpec((n, 1), lambda h: (0, 0)) for n in key_rows]
    q = pl.BlockSpec((rows, LANES), lambda h: (0, h))
    ks = [pl.BlockSpec((n, LANES), lambda h: (0, h)) for n in key_rows]
    lse = pl.BlockSpec((1, 8, rows), lambda h: (h, 0, 0))
    return blocks, row, cols, q, ks, lse


def attention_fwd(q, keys, values, q_meta, k_metas, heads):
    rows, feats = q.shape
    parts = len(keys)
    key_rows = [k.shape[0] for k in keys]
    count = sum(key_rows)
    blocks, row, cols, qs, ks, lse = attn_specs(rows, key_rows, feats)
    return pl.pallas_call(
        functools.partial(attn_fwd_kernel, parts, heads),
        grid=(blocks,),
        out_shape=(
            jax.ShapeDtypeStruct((rows, feats), bf),
            jax.ShapeDtypeStruct((blocks, 8, rows), f32),
        ),
        in_specs=[row, row] + cols + cols + [qs] + ks + ks,
        out_specs=(qs, lse),
        scratch_shapes=[pltpu.VMEM((n, rows), f32) for n in key_rows] + [pltpu.VMEM((LANES, rows), f32)],
        compiler_params=pltpu.CompilerParams(vmem_limit_bytes=28 * MB),
        cost_estimate=COST,
    )(
        q_meta[0][None, :], q_meta[1][None, :],
        *[m[0][:, None] for m in k_metas], *[m[1][:, None] for m in k_metas],
        q, *keys, *values,
    )


def attn_bwd_kernel(parts, heads, *refs):
    qseg, qpos, qcos, qsin = refs[:4]
    refs = refs[4:]
    take = lambda n: (refs[:n], refs[n:])
    kseg, refs = take(parts)
    kpos, refs = take(parts)
    kcos, refs = take(parts)
    ksin, refs = take(parts)
    (q_ref, att_ref, do_ref, lse_ref), refs = take(4)
    k_refs, refs = take(parts)
    v_refs, refs = take(parts)
    (dq_ref,), refs = take(1)
    dk_refs, refs = take(parts)
    dv_refs, refs = take(parts)
    bias, refs = take(parts)
    dqt_ref, refs = refs[0], refs[1:]
    dka, refs = take(parts)
    dva, refs = take(parts)
    blk = pl.program_id(0)

    @pl.when(blk == 0)
    def _():
        for i in range(parts):
            fill_bias(qseg, qpos, kseg[i], kpos[i], bias[i])

    prod = (do_ref[...].astype(f32) * att_ref[...].astype(f32)).T
    dqt_ref[...] = jnp.zeros_like(dqt_ref)

    def one(sub):
        lane = lax.broadcasted_iota(jnp.int32, (1, LANES), 1)
        mine = (lane >= sub * HEAD) & (lane < (sub + 1) * HEAD)
        q = jnp.where(mine, q_ref[...] * 0.125, 0.0).astype(bf)
        do = jnp.where(mine, do_ref[...], 0.0).astype(bf)
        lse = lse_ref[0, sub : sub + 1, :]
        delta = jnp.sum(prod[sub * HEAD : (sub + 1) * HEAD, :], axis=0, keepdims=True)
        dqt = None
        for i in range(parts):
            k = k_refs[i][...]
            v = v_refs[i][...]
            p = jnp.exp(dot(k, q, ((1,), (1,))) + bias[i][...] - lse)
            dp = dot(v, do, ((1,), (1,)))
            ds = (p * (dp - delta)).astype(bf)
            dv = dot(p.astype(bf), do)
            dk = dot(ds, q)
            if sub == 0:
                dva[i][...] = dv
                dka[i][...] = dk
            else:
                dva[i][...] += dv
                dka[i][...] += dk
            d = dot(k, ds, ((0,), (0,)))
            dqt = d if dqt is None else dqt + d
        dqt_ref[sub * HEAD : (sub + 1) * HEAD, :] = dqt[sub * HEAD : (sub + 1) * HEAD, :] * 0.125

    for sub in range(LANES // HEAD):
        pl.when(blk * (LANES // HEAD) + sub < heads)(functools.partial(one, sub))
    dq_ref[...] = rope_block(dqt_ref[...].T, qcos[...], qsin[...], -1.0).astype(bf)
    for i in range(parts):
        dk_refs[i][...] = rope_block(dka[i][...], kcos[i][...], ksin[i][...], -1.0).astype(bf)
        dv_refs[i][...] = dva[i][...].astype(bf)


def attention_bwd(q, att, grad_att, lse, keys, values, q_meta, k_metas, heads):
    rows, feats = q.shape
    parts = len(keys)
    key_rows = [k.shape[0] for k in keys]
    count = sum(key_rows)
    blocks, row, cols, qs, ks, lses = attn_specs(rows, key_rows, feats)
    tab = pl.BlockSpec((rows, LANES), lambda h: (0, 0))
    tabs = [pl.BlockSpec((n, LANES), lambda h: (0, 0)) for n in key_rows]
    out = pl.pallas_call(
        functools.partial(attn_bwd_kernel, parts, heads),
        grid=(blocks,),
        out_shape=(jax.ShapeDtypeStruct((rows, feats), bf),)
        + tuple(jax.ShapeDtypeStruct((n, feats), bf) for n in key_rows) * 2,
        in_specs=[row, row, tab, tab] + cols + cols + tabs + tabs + [qs, qs, qs, lses] + ks + ks,
        out_specs=(qs,) + tuple(ks) + tuple(ks),
        scratch_shapes=[pltpu.VMEM((n, rows), f32) for n in key_rows]
        + [pltpu.VMEM((LANES, rows), f32)]
        + [pltpu.VMEM((n, LANES), f32) for n in key_rows] * 2,
        compiler_params=pltpu.CompilerParams(vmem_limit_bytes=40 * MB),
        cost_estimate=COST,
    )(
        q_meta[0][None, :], q_meta[1][None, :], q_meta[2], q_meta[3],
        *[m[0][:, None] for m in k_metas], *[m[1][:, None] for m in k_metas],
        *[m[2] for m in k_metas], *[m[3] for m in k_metas],
        q, att, grad_att, lse, *keys, *values,
    )
    return out[0], out[1 : 1 + parts], out[1 + parts :]


def swap(n, bit):
    return [(i, i ^ bit) for i in range(n)]


def power_of_two(n):
    return n & (n - 1) == 0


def sum_all(value, sizes):
    for axis, n in sizes:
        if power_of_two(n):
            bit = 1
            while bit < n:
                value = value + lax.ppermute(value, axis, swap(n, bit))
                bit *= 2
        else:
            value = lax.psum(value, axis)
    return value


def after(value, *others):
    return lax.optimization_barrier((value,) + others)[0]


def scatter_sum(array):
    return lax.psum_scatter(array, "tensor", scatter_dimension=0, tiled=True).astype(f32)


def gather_rows(array):
    return lax.all_gather(array, "tensor", axis=0, tiled=True)


def gather_weight(shard, n, offs, late=()):
    if n != 4:
        return offs, [lax.all_gather(shard, "dp", axis=0, tiled=True)]
    far = after(lax.ppermute(shard, "dp", swap(4, 2)), *late)
    near = lax.ppermute(shard, "dp", swap(4, 1))
    cross = lax.ppermute(far, "dp", swap(4, 1))
    return offs, [shard, near, far, cross]


def lockstep(items, waits):
    firsts, seconds, before = [], [], ()
    for step in range(len(items) + 1):
        now = []
        if step in waits:
            before += waits[step](firsts, seconds)
        if step > 0:
            seconds.append(lax.ppermute(after(firsts[-1], *before), "ctx", swap(2, 1)))
            now.append(seconds[-1])
        if step < len(items):
            firsts.append(lax.ppermute(after(items[step], *before), "dp", swap(4, 2)))
            now.append(firsts[-1])
        before = tuple(now)
    return firsts, seconds


def two_halves(shard, n, n_ctx, ctx, first, second, offs):
    half = shard.shape[1] // 2
    cross = lambda a: lax.ppermute(a, "dp", swap(4, 1))
    out = []
    for place, piece in ((ctx * half, first), ((1 - ctx) * half, second)):
        out += [(offs[2] + place, piece), (offs[3] + place, cross(piece))]
    return out


class WeightGrad:
    def __init__(self, n, n_ctx, offs):
        self.n, self.n_ctx, self.offs = n, n_ctx, offs

    def start(self, left, right):
        if self.n == 4:
            self.keep, send = weight_grad(left, right, self.offs)
            self.got = lax.ppermute(send, "dp", swap(4, 1))
            block = send.shape[0] // 2
            self.far = (self.keep[block:].astype(f32) + self.got[block:].astype(f32)).astype(bf)
        else:
            self.far = self.whole = dot(left, right, ((0,), (0,))).astype(bf)
        return self

    def along_x(self, *late):
        if self.n == 4:
            block = self.far.shape[0]
            other = after(lax.ppermute(self.far, "dp", swap(4, 2)), *late).astype(f32)
            total = self.keep[:block].astype(f32) + self.got[:block].astype(f32) + other
        else:
            total = lax.psum_scatter(self.whole, "dp", scatter_dimension=0, tiled=True).astype(f32)
        self.total = lax.optimization_barrier(total.astype(bf))
        return self.total

    def along_y(self, *late):
        if self.n_ctx == 2:
            self.other = lax.ppermute(after(self.total, *late), "ctx", swap(2, 1))
        else:
            self.other = lax.psum(self.total, "ctx")
        return self.other

    def finish(self, size, *before):
        other = after(self.other, *before).astype(f32)
        out = self.total.astype(f32) + other if self.n_ctx == 2 else other
        return out[:, :size]


def per_device(
    n_dp, n_ctx, n_tp,
    tokens, segment, position, gain_attn, w_query, w_key, w_value, w_out, gain_ffn, w_gate, w_up, w_down, cotangent,
):
    dp, ctx, me = lax.axis_index("dp"), lax.axis_index("ctx"), lax.axis_index("tensor")
    rows = tokens.shape[0]
    piece = rows // n_tp
    shard = gain_attn.shape[0]
    feats, hidden_dev = w_query.shape[1], w_gate.shape[1]
    feats_pad, hidden_pad = up_to(feats, LANES), up_to(hidden_dev, 256)
    mine = functools.partial(lax.dynamic_slice_in_dim, start_index=me * piece, slice_size=piece, axis=0)
    offs = jnp.stack([(dp ^ j) * shard for j in range(4)]) if n_dp == 4 else jnp.zeros((4,), jnp.int32)

    def padded(w, width, *before):
        return after(jnp.pad(w.astype(bf), ((0, 0), (0, width - w.shape[1]))), *before)

    wo_all = lax.all_gather(padded(w_out.T, feats_pad), "tensor", axis=0, tiled=False)
    wk_b = jnp.pad(w_key.astype(bf), ((0, 16), (0, feats_pad - feats)))
    gain_rows = jnp.pad(jnp.stack([gain_attn, gain_ffn]).astype(bf), ((0, 0), (0, feats_pad - shard)))
    wk_b = lax.dynamic_update_slice(wk_b, gain_rows, (shard, 0))
    _, wk_ext = gather_weight(wk_b, n_dp, offs)
    if n_dp == 4:
        own = jnp.stack([w[shard : shard + 2, :shard] for w in wk_ext])
        gains = jnp.zeros((2, n_dp * shard), f32)
        for j in range(4):
            gains = lax.dynamic_update_slice(gains, own[j].astype(f32), (0, offs[j]))
        wk = (offs, wk_ext)
    else:
        ext = wk_ext[0].reshape(n_dp, shard + 16, feats_pad)
        gains = ext[:, shard : shard + 2, :shard].transpose(1, 0, 2).reshape(2, n_dp * shard).astype(f32)
        wk = (offs, [ext[:, :shard].reshape(n_dp * shard, feats_pad)])
    gain1, gain2 = gains[0], gains[1]
    def meta(start, size):
        seg = lax.dynamic_slice_in_dim(segment, start, size)
        pos = lax.dynamic_slice_in_dim(position, start, size)
        return (seg, pos) + rope_tables(pos)

    q_meta = meta(ctx * rows, rows)
    cos_t, sin_t = q_meta[2:]
    inputs = tokens.astype(f32)
    scale1 = lax.rsqrt(jnp.mean(inputs * inputs, axis=-1, keepdims=True) + norm_eps)
    normed1 = (inputs * scale1 * gain1).astype(bf)
    far = lambda w: w[1][2 if n_dp == 4 else 0]
    keys = project(normed1, wk, cos_t, sin_t, True)
    wv = gather_weight(padded(w_value, feats_pad, far(wk)), n_dp, offs, (keys,))
    values = project(normed1, wv, cos_t, sin_t, False)
    if n_ctx == 2:
        trade = lambda a: lax.ppermute(a, "ctx", swap(2, 1))
        keys_all, values_all = [keys, trade(keys)], [values, trade(values)]
        k_metas = [q_meta, meta((1 - ctx) * rows, rows)]
        early = (values, keys_all[1])
    else:
        spread = lambda a: [lax.all_gather(a, "ctx", axis=0, tiled=True)]
        keys_all, values_all = spread(keys), spread(values)
        k_metas = [meta(0, segment.shape[0])]
        early = (values,)
    wq = gather_weight(padded(w_query, feats_pad, far(wv)), n_dp, offs, early)
    wide = [padded(w, hidden_pad) for w in (w_down.T, w_gate, w_up)]
    grad_ffn = (branch_scale * cotangent.astype(f32)).astype(bf)
    if n_dp == 4 and n_ctx == 2:
        half = shard // 2
        near = lambda a: lax.ppermute(a, "dp", swap(4, 1))
        cut = lambda a: lax.dynamic_slice_in_dim(a, ctx * half, half, a.ndim - 2)
        mid = n_tp // 2
        items = [cut(wide[0]), cut(wo_all[:mid]), cut(wo_all[mid:]), cut(wide[1]), cut(wide[2])]
        items[0] = after(items[0], far(wq))
        query = project(normed1, wq, cos_t, sin_t, True)
        early = []

        def shards_of(own, first, second):
            got = two_halves(own[None], n_dp, n_ctx, ctx, first, second, offs)
            places, pieces = zip((offs[0], own), (offs[1], near(own)), *got)
            return jnp.stack(places), list(pieces)

        def attend(firsts, seconds):
            early.append(attention_fwd(after(query, *wide), keys_all, values_all, q_meta, k_metas, feats // HEAD))
            return (early[0][0],)

        def work_ahead(firsts, seconds):
            wd = shards_of(wide[0], firsts[0], seconds[0])
            early.extend((wd, wide_matmul(after(grad_ffn, firsts[2]), wd, False, f32)))
            return (early[2],)

        waits = {1: lambda f, s: (query, values_all[1]), 2: attend, 4: work_ahead}
        firsts, seconds = lockstep(items, waits)
        att, lse = early.pop(0)
        wd, grad_hidden = early
        wg = shards_of(wide[1], firsts[3], seconds[3])
        places, wo_pieces = [offs[0], offs[1]], [((0, n_tp), wo_all), ((0, n_tp), near(wo_all))]
        for k, span in ((1, (0, mid)), (2, (mid, n_tp))):
            for place, piece in two_halves(wo_all, n_dp, n_ctx, ctx, firsts[k], seconds[k], offs):
                places.append(place)
                wo_pieces.append((span, piece))
        places = jnp.stack(places)
        late = (firsts[4], seconds[3])
    else:
        wd, wg, wu = [gather_weight(w, n_dp, offs) for w in wide]
        places, wo_pieces = offs[:1] * 0, [((0, n_tp), lax.all_gather(wo_all, "dp", axis=1, tiled=True))]
        late = ()
        query = project(normed1, wq, cos_t, sin_t, True)
        att, lse = attention_fwd(query, keys_all, values_all, q_meta, k_metas, feats // HEAD)
        grad_hidden = wide_matmul(grad_ffn, wd, False, f32)
    att_all = after(lax.all_gather(att, "tensor", axis=0, tiled=False), *late)
    my_in, my_scale = mine(tokens).astype(f32), mine(scale1)
    normed2, hidden_in, wo_dev = mix(att_all, tokens, gain2, places, wo_pieces, me)
    wo = (jnp.zeros((1,), jnp.int32), [wo_dev])
    if n_dp == 4 and n_ctx == 2:
        wu = shards_of(wide[2], firsts[4], after(seconds[4], normed2))
    scale2 = lax.rsqrt(jnp.mean(hidden_in * hidden_in, axis=-1, keepdims=True) + norm_eps)

    hidden, grad_gate, grad_up, partial2 = ffn(normed2, grad_hidden, wg, wu)
    make = lambda: WeightGrad(n_dp, n_ctx, offs)
    grad_d = make().start(grad_ffn, hidden)
    ffn_part = wide_matmul(hidden, wd, True, bf)
    grad_g = make().start(after(normed2, grad_d.far), grad_gate)
    grad_norm2 = after(scatter_sum(partial2), grad_d.along_x(), ffn_part, grad_g.far)
    part_g2 = jnp.sum(grad_norm2 * hidden_in * scale2, axis=0)
    grad_h = (
        mine(cotangent).astype(f32)
        + scale2 * gain2 * grad_norm2
        - hidden_in * scale2**3 * jnp.mean(hidden_in * gain2 * grad_norm2, axis=-1, keepdims=True)
    )
    local_mixed = (branch_scale * grad_h).astype(bf)
    grad_mixed = gather_rows(local_mixed)

    grad_u = make().start(after(normed2, local_mixed), grad_up)
    grad_mixed = after(grad_mixed, grad_d.along_y(), grad_g.along_x(), grad_u.far)
    ffn_part = scatter_sum(after(ffn_part, grad_mixed))

    grad_att = wide_matmul(grad_mixed, wo, False, bf)
    back = lambda k, v, m: attention_bwd(query, att, grad_att, lse, k, v, q_meta, m, feats // HEAD)
    if n_ctx == 2:
        grad_q1, grad_k1, grad_v1 = back(keys_all[1:], values_all[1:], k_metas[1:])
        grad_att = after(grad_att, grad_q1, grad_g.along_y(), grad_u.along_x())
        grad_q0, grad_k0, grad_v0 = back(keys_all[:1], values_all[:1], k_metas[:1])
        grad_q = (grad_q0.astype(f32) + grad_q1.astype(f32)).astype(bf)
        grad_ks, grad_vs = grad_k0 + grad_k1, grad_v0 + grad_v1
    else:
        grad_g.along_y(), grad_u.along_x()
        grad_q, grad_ks, grad_vs = back(keys_all, values_all, k_metas)
    if n_ctx == 2:
        merge = lambda pair: (pair[0].astype(f32) + trade(pair[1]).astype(f32)).astype(bf)
    else:
        merge = lambda whole: lax.psum_scatter(whole[0], "ctx", scatter_dimension=0, tiled=True)
    grad_k, grad_v = merge(grad_ks), merge(grad_vs)

    grad_o = make().start(grad_mixed, att)
    grad_q = after(grad_q, grad_o.far)
    partial1, part_g1 = qkv_back((grad_q, grad_k, grad_v), (wq, wk, wv), tokens, scale1)
    output = hidden_in + branch_scale * after(ffn_part, grad_q)
    output = gather_rows(lax.optimization_barrier(output.astype(bf)))
    grads_a = [make().start(normed1, g) for g in (grad_q, grad_k, grad_v)]
    grad_norm1 = after(scatter_sum(after(partial1, output)), grad_o.along_x(), *[g.along_x() for g in grads_a[:2]])
    gain_sum = jnp.concatenate([part_g1, part_g2[None, :]])
    gain_sum = sum_all(gain_sum, (("dp", n_dp), ("ctx", n_ctx), ("tensor", n_tp)))
    grad_norm1 = after(grad_norm1, gain_sum)
    grad_in = (
        grad_h
        + my_scale * gain1 * grad_norm1
        - my_in * my_scale**3 * jnp.mean(my_in * gain1 * grad_norm1, axis=-1, keepdims=True)
    )
    local_in = lax.optimization_barrier(grad_in.astype(bf))
    grad_in = gather_rows(local_in).astype(f32)
    gain_sum = lax.dynamic_slice_in_dim(gain_sum, dp * shard, shard, 1)

    grad_u.along_y(grad_k, grad_v)
    grad_o.along_y(grad_k, grad_v)
    grads_a[2].along_x(local_in)
    for g in grads_a:
        g.along_y()
    sum_wd = grad_d.finish(hidden_dev, local_in).T
    sum_wg, sum_wu = grad_g.finish(hidden_dev, local_in), grad_u.finish(hidden_dev, local_in)
    sum_wo = grad_o.finish(feats, local_in).T
    sum_wq, sum_wk, sum_wv = [g.finish(feats, local_in) for g in grads_a]
    return (output.astype(f32), grad_in, gain_sum[0], sum_wq, sum_wk, sum_wv, sum_wo, gain_sum[1], sum_wg, sum_wu, sum_wd)


def solution(mesh):
    rows, col, row = P(("dp", "ctx"), None), P("dp", "tensor"), P("tensor", "dp")
    sizes = (mesh.shape["dp"], mesh.shape["ctx"], mesh.shape["tensor"])
    return jax.shard_map(
        functools.partial(per_device, *sizes),
        mesh=mesh,
        in_specs=(rows, P("dp"), P("dp"), P("dp"), col, col, col, row, P("dp"), col, col, row, rows),
        out_specs=(rows, rows, P("dp"), col, col, col, row, P("dp"), col, col, row),
        check_vma=False,
    )
```

```python
import functools
import math

import jax
import jax.numpy as jnp
from jax import lax
from jax.experimental import pallas as pl
from jax.experimental.pallas import tpu as pltpu
from jax.sharding import PartitionSpec as P

HEAD = 64
LANES = 128
NEG = -1e30
norm_eps = 1e-05
branch_scale = 1.4 / math.sqrt(40.0)
bf = jnp.bfloat16
f32 = jnp.float32
MB = 1 << 20


def rope_tables(positions):
    freq = 10000.0 ** (-(jnp.arange(HEAD // 2, dtype=f32) * 2.0 / HEAD))
    angle = positions.astype(f32)[:, None] * freq[None, :]
    cosine, sine = jnp.cos(angle), jnp.sin(angle)
    cos_t = jnp.concatenate([cosine] * 4, axis=1)
    sin_t = jnp.concatenate([-sine, sine, -sine, sine], axis=1)
    return cos_t, sin_t


def rope_block(u, cos_t, sin_t, sign):
    lane = lax.broadcasted_iota(jnp.int32, u.shape, 1)
    low = (lane % HEAD) < HEAD // 2
    partner = jnp.where(low, pltpu.roll(u, LANES - HEAD // 2, 1), pltpu.roll(u, HEAD // 2, 1))
    return u * cos_t + sign * (partner * sin_t)


def dot(a, b, dims=((1,), (0,))):
    return lax.dot_general(a, b, (dims, ((), ())), preferred_element_type=f32)


def up_to(n, unit):
    return -(-n // unit) * unit


COST = pl.CostEstimate(flops=1024, bytes_accessed=1024, transcendentals=0)


def fetch(offs_ref, shards, scratch, sems, width):
    copies = []
    for b in range(scratch.shape[1] // width):
        row = []
        for j, ref in enumerate(shards):
            rows = min(ref.shape[0], scratch.shape[0] // min(len(shards), 4))
            first = pl.multiple_of(offs_ref[j], 16)
            copy = pltpu.make_async_copy(
                ref.at[pl.ds(0, rows), pl.ds(b * width, width)],
                scratch.at[pl.ds(first, rows), pl.ds(b * width, width)],
                sems.at[b, j],
            )
            copy.start()
            row.append(copy)
        copies.append(row)
    return copies


def wait_all(copies):
    for copy in copies:
        copy.wait()


HBM = pl.BlockSpec(memory_space=pltpu.HBM)
VM = pl.BlockSpec(memory_space=pltpu.VMEM)
SM = pl.BlockSpec(memory_space=pltpu.SMEM)


def params(mbytes):
    return pltpu.CompilerParams(vmem_limit_bytes=mbytes * MB)


def proj_kernel(ns, rotary, offs, n_ref, cos_ref, sin_ref, *rest):
    shards, (o_ref, w_ref, sems) = rest[:ns], rest[ns:]
    copies = fetch(offs, shards, w_ref, sems, w_ref.shape[1])
    wait_all(copies[0])
    y = dot(n_ref[...], w_ref[...])
    for first in range(0, o_ref.shape[1], LANES):
        u = y[:, first : first + LANES]
        if rotary:
            u = rope_block(u, cos_ref[...], sin_ref[...], 1.0)
        o_ref[:, first : first + LANES] = u.astype(bf)


def project(normed, weight, cos_t, sin_t, rotary):
    offs, shards = weight
    rows, depth = normed.shape
    feats = shards[0].shape[1]
    ns = len(shards)
    return pl.pallas_call(
        functools.partial(proj_kernel, ns, rotary),
        out_shape=jax.ShapeDtypeStruct((rows, feats), bf),
        in_specs=[SM, VM, VM, VM] + [HBM] * ns,
        out_specs=VM,
        scratch_shapes=[pltpu.VMEM((depth, feats), bf), pltpu.SemaphoreType.DMA((1, ns))],
        compiler_params=params(16),
        cost_estimate=COST,
    )(offs, normed, cos_t, sin_t, *shards)


def wide_kernel(ns, nt, width, offs, a_ref, *rest):
    shards, (o_ref, w_ref, sems) = rest[:ns], rest[ns:]
    if nt:
        for row in fetch(offs, shards, w_ref, sems, w_ref.shape[1]):
            wait_all(row)
        for first in range(0, o_ref.shape[1], width):
            part = slice(first, first + width)
            o_ref[:, part] = dot(a_ref[...], w_ref[part, :], ((1,), (1,))).astype(o_ref.dtype)
    else:
        for b, row in enumerate(fetch(offs, shards, w_ref, sems, width)):
            wait_all(row)
            part = slice(b * width, (b + 1) * width)
            o_ref[:, part] = dot(a_ref[...], w_ref[:, part]).astype(o_ref.dtype)


def wide_matmul(a, weight, nt, dtype, width=256):
    offs, shards = weight
    rows = a.shape[0]
    ns = len(shards)
    depth, feats = sum(s.shape[0] for s in shards), shards[0].shape[1]
    if feats % width and not nt:
        width = feats
    return pl.pallas_call(
        functools.partial(wide_kernel, ns, nt, width),
        out_shape=jax.ShapeDtypeStruct((rows, depth if nt else feats), dtype),
        in_specs=[SM, VM] + [HBM] * ns,
        out_specs=VM,
        scratch_shapes=[pltpu.VMEM((depth, feats), bf), pltpu.SemaphoreType.DMA((feats // width, ns))],
        compiler_params=params(20),
        cost_estimate=COST,
    )(offs, a, *shards)


def qkv_back_kernel(ns, offs, x_ref, scale_ref, *rest):
    grads, rest = rest[:3], rest[3:]
    shards, (o_ref, gain_ref, w_ref, sems) = rest[: 3 * ns], rest[3 * ns :]
    rows = [fetch(offs, shards[i * ns : (i + 1) * ns], w_ref.at[i], sems.at[i], w_ref.shape[2])[0] for i in range(3)]
    for row in rows:
        wait_all(row)
    width = 256
    for first in range(0, o_ref.shape[1], width):
        part = slice(first, first + width)
        total = None
        for i in range(3):
            y = dot(grads[i][...], w_ref[i, part, :], ((1,), (1,)))
            total = y if total is None else total + y
        o_ref[:, part] = total.astype(bf)
        gain_ref[:, part] = jnp.sum(total * (x_ref[:, part].astype(f32) * scale_ref[...]), axis=0, keepdims=True)


def qkv_back(grads, weights, tokens, scale):
    offs = weights[0][0]
    shards = [s for w in weights for s in w[1]]
    ns = len(weights[0][1])
    rows, feats = grads[0].shape
    depth = sum(s.shape[0] for s in weights[2][1])
    return pl.pallas_call(
        functools.partial(qkv_back_kernel, ns),
        out_shape=(jax.ShapeDtypeStruct((rows, depth), bf), jax.ShapeDtypeStruct((1, depth), f32)),
        in_specs=[SM] + [VM] * 5 + [HBM] * (3 * ns),
        out_specs=(VM, VM),
        scratch_shapes=[pltpu.VMEM((3, depth, feats), bf), pltpu.SemaphoreType.DMA((3, 1, ns))],
        compiler_params=params(28),
        cost_estimate=COST,
    )(offs, tokens, scale, *grads, *shards)


def ffn_kernel(ns, width, offs, n_hbm, dh_hbm, *rest):
    g_shards, u_shards, rest = rest[:ns], rest[ns : 2 * ns], rest[2 * ns :]
    outs, dn_hbm, rest = rest[:3], rest[3], rest[4:]
    n_ref, dh_ref, wg, wu, mids, dn_ref, w_sems, in_sems, out_sems = rest
    hidden, depth = dh_ref.shape[1], n_ref.shape[1]
    blocks = [slice(f, min(f + width, hidden)) for f in range(0, hidden, width)]
    span = lambda part: pl.ds(part.start, part.stop - part.start)

    def load(b):
        part = span(blocks[b])
        copies = [pltpu.make_async_copy(dh_hbm.at[:, part], dh_ref.at[:, part], in_sems.at[b + 1])]
        for i, (shards, scratch) in enumerate(((g_shards, wg), (u_shards, wu))):
            for j, ref in enumerate(shards):
                first = pl.multiple_of(offs[j], 16)
                there = scratch.at[pl.ds(first, ref.shape[0]), part]
                copies.append(pltpu.make_async_copy(ref.at[:, part], there, w_sems.at[i, b, j]))
        for copy in copies:
            copy.start()
        return copies

    first = pltpu.make_async_copy(n_hbm, n_ref, in_sems.at[0])
    first.start()
    loads = [load(0)]
    first.wait()
    stores = []
    for b, part in enumerate(blocks):
        wait_all(loads[b])
        if b + 1 < len(blocks):
            loads.append(load(b + 1))
        gate = dot(n_ref[...], wg[:, part])
        up = dot(n_ref[...], wu[:, part])
        sigma = jax.nn.sigmoid(gate)
        active = gate * sigma
        dh = dh_ref[:, part]
        mids[0, :, part] = (active * up).astype(bf)
        mids[1, :, part] = (dh * up * sigma * (1.0 + gate * (1.0 - sigma))).astype(bf)
        mids[2, :, part] = (dh * active).astype(bf)
        for i in range(3):
            copy = pltpu.make_async_copy(mids.at[i, :, span(part)], outs[i].at[:, span(part)], out_sems.at[i, b])
            copy.start()
            stores.append(copy)
    for b, f in enumerate(range(0, depth, 768)):
        part = slice(f, f + 768)
        total = dot(mids[1], wg[part, :], ((1,), (1,))) + dot(mids[2], wu[part, :], ((1,), (1,)))
        dn_ref[:, part] = total.astype(bf)
        copy = pltpu.make_async_copy(dn_ref.at[:, span(part)], dn_hbm.at[:, span(part)], out_sems.at[3, b])
        copy.start()
        stores.append(copy)
    wait_all(stores)


def ffn(normed, grad_hidden, w_gate, w_up, width=512):
    offs, g_shards = w_gate
    ns = len(g_shards)
    rows, depth = normed.shape
    hidden = g_shards[0].shape[1]
    blocks = -(-hidden // width)
    mid = jax.ShapeDtypeStruct((rows, hidden), bf)
    return pl.pallas_call(
        functools.partial(ffn_kernel, ns, width),
        out_shape=(mid, mid, mid, jax.ShapeDtypeStruct((rows, depth), bf)),
        in_specs=[SM] + [HBM] * (2 + 2 * ns),
        out_specs=(HBM,) * 4,
        scratch_shapes=[
            pltpu.VMEM((rows, depth), bf),
            pltpu.VMEM((rows, hidden), f32),
            pltpu.VMEM((depth, hidden), bf),
            pltpu.VMEM((depth, hidden), bf),
            pltpu.VMEM((3, rows, hidden), bf),
            pltpu.VMEM((rows, depth), bf),
            pltpu.SemaphoreType.DMA((2, blocks, ns)),
            pltpu.SemaphoreType.DMA((blocks + 1,)),
            pltpu.SemaphoreType.DMA((4, max(blocks, depth // 768))),
        ],
        compiler_params=params(60),
        cost_estimate=COST,
    )(offs, normed, grad_hidden, *g_shards, *w_up[1])


def mix_kernel(spans, me_ref, offs, att_ref, x_ref, gain_ref, *rest):
    ns = len(spans)
    shards, (n_ref, own_ref, wo_hbm, w_ref, h_ref, sems) = rest[:ns], rest[ns:]
    copies = []
    for j, (ref, (z0, z1)) in enumerate(zip(shards, spans)):
        rows = pl.ds(pl.multiple_of(offs[j], 16), ref.shape[1])
        copies.append(pltpu.make_async_copy(ref, w_ref.at[z0:z1, rows, :], sems.at[j]))
        copies[-1].start()
    wait_all(copies)
    keep = pltpu.make_async_copy(w_ref.at[me_ref[0]], wo_hbm, sems.at[ns])
    keep.start()
    depth = h_ref.shape[1]
    width = 768
    for f in range(0, depth, width):
        part = slice(f, f + width)
        total = None
        for z in range(att_ref.shape[0]):
            y = dot(att_ref[z], w_ref[z, part, :], ((1,), (1,)))
            total = y if total is None else total + y
        h_ref[:, part] = x_ref[:, part].astype(f32) + branch_scale * total
    step = min(128, h_ref.shape[0])
    for f in range(0, h_ref.shape[0], step):
        part = slice(f, f + step)
        h = h_ref[part, :]
        scale = lax.rsqrt(jnp.mean(h * h, axis=-1, keepdims=True) + norm_eps)
        n_ref[part, :] = (h * scale * gain_ref[...]).astype(bf)
    piece = own_ref.shape[0]
    own_ref[...] = h_ref[pl.ds(pl.multiple_of(me_ref[0] * piece, 8), piece), :]
    keep.wait()


def mix(att, tokens, gain, offs, pieces, me):
    n, rows, feats = att.shape
    depth = tokens.shape[1]
    spans, shards = [p[0] for p in pieces], [p[1] for p in pieces]
    return pl.pallas_call(
        functools.partial(mix_kernel, spans),
        out_shape=(
            jax.ShapeDtypeStruct((rows, depth), bf),
            jax.ShapeDtypeStruct((rows // n, depth), f32),
            jax.ShapeDtypeStruct((depth, feats), bf),
        ),
        in_specs=[SM, SM, VM, VM, VM] + [HBM] * len(shards),
        out_specs=(VM, VM, HBM),
        scratch_shapes=[
            pltpu.VMEM((n, depth, feats), bf),
            pltpu.VMEM((rows, depth), f32),
            pltpu.SemaphoreType.DMA((len(shards) + 1,)),
        ],
        compiler_params=params(56),
        cost_estimate=COST,
    )(me[None], offs, att, tokens, gain[None, :], *shards)


def grad_kernel(offs, a_ref, b_ref, keep_ref, send_ref, at_ref):
    at_ref[...] = a_ref[...].T
    block = keep_ref.shape[0] // 2
    for j in range(4):
        left = at_ref[pl.ds(pl.multiple_of(offs[j], 16), block), :]
        ref = send_ref if j % 2 else keep_ref
        ref[(j // 2) * block : (j // 2 + 1) * block, :] = dot(left, b_ref[...]).astype(bf)


def weight_grad(a, b, offs):
    rows, depth = a.shape
    feats = b.shape[1]
    half = jax.ShapeDtypeStruct((depth // 2, feats), bf)
    return pl.pallas_call(
        grad_kernel,
        out_shape=(half, half),
        in_specs=[SM, VM, VM],
        out_specs=(VM, VM),
        scratch_shapes=[pltpu.VMEM((depth, rows), bf)],
        compiler_params=params(20),
        cost_estimate=COST,
    )(offs, a, b)


def add_kernel(*refs):
    total = refs[0][...].astype(f32)
    for ref in refs[1:-1]:
        total = total + ref[...].astype(f32)
    refs[-1][...] = total.astype(bf)


def add_halves(pairs, others, half):
    rows, cols = pairs[0].shape[0] // 2, pairs[0].shape[1]
    steps = 4 if rows % 64 == 0 else 1
    block = (rows // steps, cols)
    picked = pl.BlockSpec(block, lambda i: (i + half * steps, 0))
    plain = pl.BlockSpec(block, lambda i: (i, 0))
    return pl.pallas_call(
        add_kernel,
        grid=(steps,),
        out_shape=jax.ShapeDtypeStruct((rows, cols), bf),
        in_specs=[picked] * len(pairs) + [plain] * len(others),
        out_specs=plain,
        compiler_params=params(16),
        cost_estimate=COST,
    )(*pairs, *others)


def fill_bias(qseg_ref, qpos_ref, kseg_ref, kpos_ref, bias_ref):
    kseg = kseg_ref[...]
    allowed = ((kseg == qseg_ref[...]) | (kseg == 0)) & (kpos_ref[...] <= qpos_ref[...])
    bias_ref[...] = jnp.where(allowed, 0.0, NEG)


def attn_fwd_kernel(parts, heads, *refs):
    qseg, qpos = refs[:2]
    kseg, kpos = refs[2 : 2 + parts], refs[2 + parts : 2 + 2 * parts]
    rest = refs[2 + 2 * parts :]
    q_ref = rest[0]
    k_refs, v_refs = rest[1 : 1 + parts], rest[1 + parts : 1 + 2 * parts]
    o_ref, lse_ref = rest[1 + 2 * parts : 3 + 2 * parts]
    bias = rest[3 + 2 * parts : 3 + 3 * parts]
    ot_ref = rest[3 + 3 * parts]
    blk = pl.program_id(0)

    @pl.when(blk == 0)
    def _():
        for i in range(parts):
            fill_bias(qseg, qpos, kseg[i], kpos[i], bias[i])

    ot_ref[...] = jnp.zeros_like(ot_ref)
    lse_ref[...] = jnp.zeros_like(lse_ref)

    def one(sub):
        lane = lax.broadcasted_iota(jnp.int32, (1, LANES), 1)
        mine = (lane >= sub * HEAD) & (lane < (sub + 1) * HEAD)
        q = jnp.where(mine, q_ref[...] * 0.125, 0.0).astype(bf)
        scores = []
        best = None
        for i in range(parts):
            k = k_refs[i][...]
            s = dot(k, q, ((1,), (1,))) + bias[i][...]
            scores.append(s)
            top = jnp.max(s, axis=0, keepdims=True)
            best = top if best is None else jnp.maximum(best, top)
        total, acc = None, None
        for i in range(parts):
            p = jnp.exp(scores[i] - best)
            t = jnp.sum(p, axis=0, keepdims=True)
            v = v_refs[i][...]
            a = dot(v, p.astype(bf), ((0,), (0,)))
            total = t if total is None else total + t
            acc = a if acc is None else acc + a
        ot_ref[sub * HEAD : (sub + 1) * HEAD, :] = acc[sub * HEAD : (sub + 1) * HEAD, :] / total
        lse_ref[0, sub : sub + 1, :] = best + jnp.log(total)

    for sub in range(LANES // HEAD):
        pl.when(blk * (LANES // HEAD) + sub < heads)(functools.partial(one, sub))
    o_ref[...] = ot_ref[...].T.astype(bf)


def attn_specs(rows, key_rows, feats):
    blocks = -(-feats // LANES)
    row = pl.BlockSpec((1, rows), lambda h: (0, 0))
    cols = [pl.BlockSpec((n, 1), lambda h: (0, 0)) for n in key_rows]
    q = pl.BlockSpec((rows, LANES), lambda h: (0, h))
    ks = [pl.BlockSpec((n, LANES), lambda h: (0, h)) for n in key_rows]
    lse = pl.BlockSpec((1, 8, rows), lambda h: (h, 0, 0))
    return blocks, row, cols, q, ks, lse


def attention_fwd(q, keys, values, q_meta, k_metas, heads):
    rows, feats = q.shape
    parts = len(keys)
    key_rows = [k.shape[0] for k in keys]
    count = sum(key_rows)
    blocks, row, cols, qs, ks, lse = attn_specs(rows, key_rows, feats)
    return pl.pallas_call(
        functools.partial(attn_fwd_kernel, parts, heads),
        grid=(blocks,),
        out_shape=(
            jax.ShapeDtypeStruct((rows, feats), bf),
            jax.ShapeDtypeStruct((blocks, 8, rows), f32),
        ),
        in_specs=[row, row] + cols + cols + [qs] + ks + ks,
        out_specs=(qs, lse),
        scratch_shapes=[pltpu.VMEM((n, rows), f32) for n in key_rows] + [pltpu.VMEM((LANES, rows), f32)],
        compiler_params=pltpu.CompilerParams(vmem_limit_bytes=28 * MB),
        cost_estimate=COST,
    )(
        q_meta[0][None, :], q_meta[1][None, :],
        *[m[0][:, None] for m in k_metas], *[m[1][:, None] for m in k_metas],
        q, *keys, *values,
    )


def attn_bwd_kernel(parts, heads, *refs):
    qseg, qpos, qcos, qsin = refs[:4]
    refs = refs[4:]
    take = lambda n: (refs[:n], refs[n:])
    kseg, refs = take(parts)
    kpos, refs = take(parts)
    kcos, refs = take(parts)
    ksin, refs = take(parts)
    (q_ref, att_ref, do_ref, lse_ref), refs = take(4)
    k_refs, refs = take(parts)
    v_refs, refs = take(parts)
    (dq_ref,), refs = take(1)
    dk_refs, refs = take(parts)
    dv_refs, refs = take(parts)
    bias, refs = take(parts)
    dqt_ref, refs = refs[0], refs[1:]
    dka, refs = take(parts)
    dva, refs = take(parts)
    blk = pl.program_id(0)

    @pl.when(blk == 0)
    def _():
        for i in range(parts):
            fill_bias(qseg, qpos, kseg[i], kpos[i], bias[i])

    prod = (do_ref[...].astype(f32) * att_ref[...].astype(f32)).T
    dqt_ref[...] = jnp.zeros_like(dqt_ref)

    def one(sub):
        lane = lax.broadcasted_iota(jnp.int32, (1, LANES), 1)
        mine = (lane >= sub * HEAD) & (lane < (sub + 1) * HEAD)
        q = jnp.where(mine, q_ref[...] * 0.125, 0.0).astype(bf)
        do = jnp.where(mine, do_ref[...], 0.0).astype(bf)
        lse = lse_ref[0, sub : sub + 1, :]
        delta = jnp.sum(prod[sub * HEAD : (sub + 1) * HEAD, :], axis=0, keepdims=True)
        dqt = None
        for i in range(parts):
            k = k_refs[i][...]
            v = v_refs[i][...]
            p = jnp.exp(dot(k, q, ((1,), (1,))) + bias[i][...] - lse)
            dp = dot(v, do, ((1,), (1,)))
            ds = (p * (dp - delta)).astype(bf)
            dv = dot(p.astype(bf), do)
            dk = dot(ds, q)
            if sub == 0:
                dva[i][...] = dv
                dka[i][...] = dk
            else:
                dva[i][...] += dv
                dka[i][...] += dk
            d = dot(k, ds, ((0,), (0,)))
            dqt = d if dqt is None else dqt + d
        dqt_ref[sub * HEAD : (sub + 1) * HEAD, :] = dqt[sub * HEAD : (sub + 1) * HEAD, :] * 0.125

    for sub in range(LANES // HEAD):
        pl.when(blk * (LANES // HEAD) + sub < heads)(functools.partial(one, sub))
    dq_ref[...] = rope_block(dqt_ref[...].T, qcos[...], qsin[...], -1.0).astype(bf)
    for i in range(parts):
        dk_refs[i][...] = rope_block(dka[i][...], kcos[i][...], ksin[i][...], -1.0).astype(bf)
        dv_refs[i][...] = dva[i][...].astype(bf)


def attention_bwd(q, att, grad_att, lse, keys, values, q_meta, k_metas, heads):
    rows, feats = q.shape
    parts = len(keys)
    key_rows = [k.shape[0] for k in keys]
    count = sum(key_rows)
    blocks, row, cols, qs, ks, lses = attn_specs(rows, key_rows, feats)
    tab = pl.BlockSpec((rows, LANES), lambda h: (0, 0))
    tabs = [pl.BlockSpec((n, LANES), lambda h: (0, 0)) for n in key_rows]
    out = pl.pallas_call(
        functools.partial(attn_bwd_kernel, parts, heads),
        grid=(blocks,),
        out_shape=(jax.ShapeDtypeStruct((rows, feats), bf),)
        + tuple(jax.ShapeDtypeStruct((n, feats), bf) for n in key_rows) * 2,
        in_specs=[row, row, tab, tab] + cols + cols + tabs + tabs + [qs, qs, qs, lses] + ks + ks,
        out_specs=(qs,) + tuple(ks) + tuple(ks),
        scratch_shapes=[pltpu.VMEM((n, rows), f32) for n in key_rows]
        + [pltpu.VMEM((LANES, rows), f32)]
        + [pltpu.VMEM((n, LANES), f32) for n in key_rows] * 2,
        compiler_params=pltpu.CompilerParams(vmem_limit_bytes=40 * MB),
        cost_estimate=COST,
    )(
        q_meta[0][None, :], q_meta[1][None, :], q_meta[2], q_meta[3],
        *[m[0][:, None] for m in k_metas], *[m[1][:, None] for m in k_metas],
        *[m[2] for m in k_metas], *[m[3] for m in k_metas],
        q, att, grad_att, lse, *keys, *values,
    )
    return out[0], out[1 : 1 + parts], out[1 + parts :]


def swap(n, bit):
    return [(i, i ^ bit) for i in range(n)]


def power_of_two(n):
    return n & (n - 1) == 0


def sum_all(value, sizes):
    for axis, n in sizes:
        if power_of_two(n):
            bit = 1
            while bit < n:
                value = value + lax.ppermute(value, axis, swap(n, bit))
                bit *= 2
        else:
            value = lax.psum(value, axis)
    return value


def after(value, *others):
    return lax.optimization_barrier((value,) + others)[0]


def scatter_sum(array):
    return lax.psum_scatter(array, "tensor", scatter_dimension=0, tiled=True).astype(f32)


def gather_rows(array):
    return lax.all_gather(array, "tensor", axis=0, tiled=True)


def gather_weight(shard, n, offs, late=()):
    if n != 4:
        whole = lax.all_gather(shard, "dp", axis=0, tiled=True)
        return offs, [whole], whole
    raw = lax.ppermute(shard, "dp", swap(4, 2))
    far = after(raw, *late)
    near = lax.ppermute(shard, "dp", swap(4, 1))
    cross = lax.ppermute(far, "dp", swap(4, 1))
    return offs, [shard, near, far, cross], raw


def lockstep(items, waits):
    firsts, seconds, before = [], [], ()
    for step in range(len(items) + 1):
        now = []
        if step in waits:
            before += waits[step](firsts, seconds)
        if step > 0:
            seconds.append(lax.ppermute(after(firsts[-1], *before), "ctx", swap(2, 1)))
            now.append(seconds[-1])
        if step < len(items):
            firsts.append(lax.ppermute(after(items[step], *before), "dp", swap(4, 2)))
            now.append(firsts[-1])
        before = tuple(now)
    return firsts, seconds


def two_halves(shard, n, n_ctx, ctx, first, second, offs):
    half = shard.shape[1] // 2
    cross = lambda a: lax.ppermute(a, "dp", swap(4, 1))
    out = []
    for place, piece in ((ctx * half, first), ((1 - ctx) * half, second)):
        out += [(offs[2] + place, piece), (offs[3] + place, cross(piece))]
    return out


class WeightGrad:
    def __init__(self, n, n_ctx, offs):
        self.n, self.n_ctx, self.offs = n, n_ctx, offs

    def start(self, left, right):
        if self.n == 4:
            self.keep, send = weight_grad(left, right, self.offs)
            self.first = send
            self.got = lax.ppermute(send, "dp", swap(4, 1))
            self.far = add_halves((self.keep, self.got), (), 1)
        else:
            self.first = self.far = self.whole = dot(left, right, ((0,), (0,))).astype(bf)
        return self

    def start_x(self):
        if self.n == 4:
            self.raw = lax.ppermute(self.far, "dp", swap(4, 2))
        else:
            self.raw = lax.psum_scatter(self.whole, "dp", scatter_dimension=0, tiled=True)
        return self.raw

    def finish_x(self, *late):
        other = after(self.raw, *late)
        if self.n == 4:
            other = add_halves((self.keep, self.got), (other,), 0)
        self.total = lax.optimization_barrier(other)
        return self.total

    def along_x(self, *late):
        self.start_x()
        return self.finish_x(*late)

    def along_y(self, *late):
        if self.n_ctx == 2:
            self.other = lax.ppermute(after(self.total, *late), "ctx", swap(2, 1))
        else:
            self.other = lax.psum(self.total, "ctx")
        return self.other

    def finish(self, size, *before):
        other = after(self.other, *before).astype(f32)
        out = self.total.astype(f32) + other if self.n_ctx == 2 else other
        return out[:, :size]


def per_device(
    n_dp, n_ctx, n_tp,
    tokens, segment, position, gain_attn, w_query, w_key, w_value, w_out, gain_ffn, w_gate, w_up, w_down, cotangent,
):
    dp, ctx, me = lax.axis_index("dp"), lax.axis_index("ctx"), lax.axis_index("tensor")
    rows = tokens.shape[0]
    piece = rows // n_tp
    shard = gain_attn.shape[0]
    feats, hidden_dev = w_query.shape[1], w_gate.shape[1]
    feats_pad, hidden_pad = up_to(feats, LANES), up_to(hidden_dev, 256)
    mine = functools.partial(lax.dynamic_slice_in_dim, start_index=me * piece, slice_size=piece, axis=0)
    offs = jnp.stack([(dp ^ j) * shard for j in range(4)]) if n_dp == 4 else jnp.zeros((4,), jnp.int32)

    def padded(w, width):
        return jnp.pad(w.astype(bf), ((0, 0), (0, width - w.shape[1])))

    wo_all = lax.all_gather(padded(w_out.T, feats_pad), "tensor", axis=0, tiled=False)
    wk_b = jnp.pad(w_key.astype(bf), ((0, 16), (0, feats_pad - feats)))
    gain_rows = jnp.pad(jnp.stack([gain_attn, gain_ffn]).astype(bf), ((0, 0), (0, feats_pad - shard)))
    wk_b = lax.dynamic_update_slice(wk_b, gain_rows, (shard, 0))
    v_cast, q_cast = padded(w_value, feats_pad), padded(w_query, feats_pad)
    _, wk_ext, raw_k = gather_weight(wk_b, n_dp, offs, (v_cast, q_cast))
    if n_dp == 4:
        own = jnp.stack([w[shard : shard + 2, :shard] for w in wk_ext])
        gains = jnp.zeros((2, n_dp * shard), f32)
        for j in range(4):
            gains = lax.dynamic_update_slice(gains, own[j].astype(f32), (0, offs[j]))
        wk = (offs, wk_ext)
    else:
        ext = wk_ext[0].reshape(n_dp, shard + 16, feats_pad)
        gains = ext[:, shard : shard + 2, :shard].transpose(1, 0, 2).reshape(2, n_dp * shard).astype(f32)
        wk = (offs, [ext[:, :shard].reshape(n_dp * shard, feats_pad)])
    gain1, gain2 = gains[0], gains[1]
    def meta(start, size):
        seg = lax.dynamic_slice_in_dim(segment, start, size)
        pos = lax.dynamic_slice_in_dim(position, start, size)
        return (seg, pos) + rope_tables(pos)

    q_meta = meta(ctx * rows, rows)
    cos_t, sin_t = q_meta[2:]
    inputs = tokens.astype(f32)
    scale1 = lax.rsqrt(jnp.mean(inputs * inputs, axis=-1, keepdims=True) + norm_eps)
    normed1 = (inputs * scale1 * gain1).astype(bf)
    keys = project(normed1, wk, cos_t, sin_t, True)
    *wv, raw_v = gather_weight(after(v_cast, raw_k), n_dp, offs, (keys,))
    values = project(normed1, wv, cos_t, sin_t, False)
    if n_ctx == 2:
        trade = lambda a: lax.ppermute(a, "ctx", swap(2, 1))
        keys_all = [keys, trade(keys)]
        values_all = [values, trade(after(values, keys_all[1]))]
        k_metas = [q_meta, meta((1 - ctx) * rows, rows)]
        early = (values_all[1],)
    else:
        spread = lambda a: [lax.all_gather(a, "ctx", axis=0, tiled=True)]
        keys_all, values_all = spread(keys), spread(values)
        k_metas = [meta(0, segment.shape[0])]
        early = (values,)
    wide = [padded(w, hidden_pad) for w in (w_down.T, w_gate, w_up)]
    half, mid = shard // 2, n_tp // 2
    items = []
    if n_dp == 4 and n_ctx == 2:
        cut = lambda a: lax.dynamic_slice_in_dim(a, ctx * half, half, a.ndim - 2)
        items = [cut(wide[0]), cut(wo_all[:mid]), cut(wo_all[mid:]), cut(wide[1]), cut(wide[2])]
    *wq, raw_q = gather_weight(after(q_cast, wv[1][-2] if n_dp == 4 else raw_v), n_dp, offs, early + tuple(wide))
    grad_ffn = (branch_scale * cotangent.astype(f32)).astype(bf)
    if n_dp == 4 and n_ctx == 2:
        near = lambda a: lax.ppermute(a, "dp", swap(4, 1))
        items[0] = after(items[0], raw_q)
        query = project(normed1, wq, cos_t, sin_t, True)
        early = []

        def shards_of(own, first, second):
            got = two_halves(own[None], n_dp, n_ctx, ctx, first, second, offs)
            places, pieces = zip((offs[0], own), (offs[1], near(own)), *got)
            return jnp.stack(places), list(pieces)

        def attend(firsts, seconds):
            early.append(attention_fwd(query, keys_all, values_all, q_meta, k_metas, feats // HEAD))
            return (early[0][0],)

        def work_ahead(firsts, seconds):
            wd = shards_of(wide[0], firsts[0], seconds[0])
            early.extend((wd, wide_matmul(after(grad_ffn, firsts[2]), wd, False, f32)))
            return (early[2],)

        waits = {1: lambda f, s: (query, values_all[1]), 2: attend, 4: work_ahead}
        firsts, seconds = lockstep(items, waits)
        att, lse = early.pop(0)
        wd, grad_hidden = early
        wg = shards_of(wide[1], firsts[3], seconds[3])
        places, wo_pieces = [offs[0], offs[1]], [((0, n_tp), wo_all), ((0, n_tp), near(wo_all))]
        for k, span in ((1, (0, mid)), (2, (mid, n_tp))):
            for place, got in two_halves(wo_all, n_dp, n_ctx, ctx, firsts[k], seconds[k], offs):
                places.append(place)
                wo_pieces.append((span, got))
        places = jnp.stack(places)
        late = (firsts[4], seconds[3])
    else:
        wd, wg, wu = [gather_weight(w, n_dp, offs)[:2] for w in wide]
        places, wo_pieces = offs[:1] * 0, [((0, n_tp), lax.all_gather(wo_all, "dp", axis=1, tiled=True))]
        late = ()
        query = project(normed1, wq, cos_t, sin_t, True)
        att, lse = attention_fwd(query, keys_all, values_all, q_meta, k_metas, feats // HEAD)
        grad_hidden = wide_matmul(grad_ffn, wd, False, f32)
    att_all = after(lax.all_gather(att, "tensor", axis=0, tiled=False), *late)
    my_in, my_scale = mine(tokens).astype(f32), mine(scale1)
    att_all = after(att_all, *[t for m in k_metas for t in m[2:]])
    normed2, hidden_in, wo_dev = mix(att_all, tokens, gain2, places, wo_pieces, me)
    wo = (jnp.zeros((1,), jnp.int32), [wo_dev])
    if n_dp == 4 and n_ctx == 2:
        wu = shards_of(wide[2], firsts[4], after(seconds[4], normed2))
    scale2 = lax.rsqrt(jnp.mean(hidden_in * hidden_in, axis=-1, keepdims=True) + norm_eps)

    hidden, grad_gate, grad_up, partial2 = ffn(normed2, grad_hidden, wg, wu)
    make = lambda: WeightGrad(n_dp, n_ctx, offs)
    grad_d = make().start(grad_ffn, hidden)
    ffn_part = wide_matmul(hidden, wd, True, bf)
    grad_g = make().start(after(normed2, grad_d.far, ffn_part), grad_gate)
    grad_norm2 = scatter_sum(partial2)
    grad_d.along_x(grad_norm2)
    grad_norm2 = after(grad_norm2, grad_d.raw, ffn_part, grad_g.first)
    part_g2 = jnp.sum(grad_norm2 * hidden_in * scale2, axis=0)
    grad_h = (
        mine(cotangent).astype(f32)
        + scale2 * gain2 * grad_norm2
        - hidden_in * scale2**3 * jnp.mean(hidden_in * gain2 * grad_norm2, axis=-1, keepdims=True)
    )
    local_mixed = (branch_scale * grad_h).astype(bf)
    grad_mixed = gather_rows(local_mixed)

    grad_u = make().start(after(normed2, local_mixed), grad_up)
    grad_mixed = after(grad_mixed, grad_d.along_y(), grad_g.along_x(), grad_u.far)
    ffn_part = scatter_sum(after(ffn_part, grad_mixed))

    grad_att = wide_matmul(grad_mixed, wo, False, bf)
    back = lambda k, v, m: attention_bwd(query, att, grad_att, lse, k, v, q_meta, m, feats // HEAD)
    if n_ctx == 2:
        grad_q1, grad_k1, grad_v1 = back(keys_all[1:], values_all[1:], k_metas[1:])
        grad_att = after(grad_att, grad_q1, grad_g.along_y(), grad_u.along_x(grad_q1))
        grad_q0, grad_k0, grad_v0 = back(keys_all[:1], values_all[:1], k_metas[:1])
        grad_q = (grad_q0.astype(f32) + grad_q1.astype(f32)).astype(bf)
        grad_ks, grad_vs = grad_k0 + grad_k1, grad_v0 + grad_v1
    else:
        grad_g.along_y(), grad_u.along_x()
        grad_q, grad_ks, grad_vs = back(keys_all, values_all, k_metas)
    if n_ctx == 2:
        merge = lambda pair: (pair[0].astype(f32) + trade(pair[1]).astype(f32)).astype(bf)
    else:
        merge = lambda whole: lax.psum_scatter(whole[0], "ctx", scatter_dimension=0, tiled=True)
    grad_k, grad_v = merge(grad_ks), merge(grad_vs)

    grad_o = make().start(grad_mixed, att)
    worked = (grad_q, grad_k)
    grad_q = after(grad_q, grad_o.along_x())
    grad_u.along_y(grad_k, grad_v)
    partial1, part_g1 = qkv_back((grad_q, grad_k, grad_v), (wq, wk, wv), tokens, scale1)
    output = hidden_in + branch_scale * after(ffn_part, *worked)
    output = gather_rows(lax.optimization_barrier(output.astype(bf)))
    grads_a = [make().start(normed1, g) for g in (grad_q, grad_k, grad_v)]
    gain_sum = sum_all(jnp.concatenate([part_g1, part_g2[None, :]]), (("ctx", n_ctx), ("dp", n_dp)))
    totals = [g.along_x() for g in grads_a[:2]]
    grad_u.other = after(grad_u.other, *totals)
    grad_norm1 = after(scatter_sum(after(partial1, output, gain_sum)), *totals, grads_a[2].start_x(), grad_u.other)
    grad_o.along_y()
    grad_in = (
        grad_h
        + my_scale * gain1 * grad_norm1
        - my_in * my_scale**3 * jnp.mean(my_in * gain1 * grad_norm1, axis=-1, keepdims=True)
    )
    local_in = lax.optimization_barrier(grad_in.astype(bf))
    grads_a[2].finish_x(local_in)
    grad_in = gather_rows(local_in).astype(f32)
    gain_sum = sum_all(after(gain_sum, local_in), (("tensor", n_tp),))
    gain_sum = lax.dynamic_slice_in_dim(gain_sum, dp * shard, shard, 1)

    for g in grads_a:
        g.along_y()
    sum_wd = grad_d.finish(hidden_dev, local_in).T
    sum_wg, sum_wu = grad_g.finish(hidden_dev, local_in), grad_u.finish(hidden_dev, local_in)
    sum_wo = grad_o.finish(feats, local_in).T
    sum_wq, sum_wk, sum_wv = [g.finish(feats, local_in) for g in grads_a]
    return (output.astype(f32), grad_in, gain_sum[0], sum_wq, sum_wk, sum_wv, sum_wo, gain_sum[1], sum_wg, sum_wu, sum_wd)


def solution(mesh):
    rows, col, row = P(("dp", "ctx"), None), P("dp", "tensor"), P("tensor", "dp")
    sizes = (mesh.shape["dp"], mesh.shape["ctx"], mesh.shape["tensor"])
    return jax.shard_map(
        functools.partial(per_device, *sizes),
        mesh=mesh,
        in_specs=(rows, P("dp"), P("dp"), P("dp"), col, col, col, row, P("dp"), col, col, row, rows),
        out_specs=(rows, rows, P("dp"), col, col, col, row, P("dp"), col, col, row),
        check_vma=False,
    )
```

```python
import functools
import math

import jax
import jax.numpy as jnp
from jax import lax
from jax.experimental import pallas as pl
from jax.experimental.pallas import tpu as pltpu
from jax.sharding import PartitionSpec as P

HEAD = 64
LANES = 128
NEG = -1e30
norm_eps = 1e-05
branch_scale = 1.4 / math.sqrt(40.0)
bf = jnp.bfloat16
f32 = jnp.float32
MB = 1 << 20


def rope_tables(positions):
    freq = 10000.0 ** (-(jnp.arange(HEAD // 2, dtype=f32) * 2.0 / HEAD))
    angle = positions.astype(f32)[:, None] * freq[None, :]
    cosine, sine = jnp.cos(angle), jnp.sin(angle)
    cos_t = jnp.concatenate([cosine] * 4, axis=1)
    sin_t = jnp.concatenate([-sine, sine, -sine, sine], axis=1)
    return cos_t, sin_t


def rope_block(u, cos_t, sin_t, sign):
    lane = lax.broadcasted_iota(jnp.int32, u.shape, 1)
    low = (lane % HEAD) < HEAD // 2
    partner = jnp.where(low, pltpu.roll(u, LANES - HEAD // 2, 1), pltpu.roll(u, HEAD // 2, 1))
    return u * cos_t + sign * (partner * sin_t)


def dot(a, b, dims=((1,), (0,))):
    return lax.dot_general(a, b, (dims, ((), ())), preferred_element_type=f32)


def up_to(n, unit):
    return -(-n // unit) * unit


COST = pl.CostEstimate(flops=1024, bytes_accessed=1024, transcendentals=0)


def fetch(offs_ref, shards, scratch, sems, width):
    copies = []
    for b in range(scratch.shape[1] // width):
        row = []
        for j, ref in enumerate(shards):
            rows = min(ref.shape[0], scratch.shape[0] // min(len(shards), 4))
            first = pl.multiple_of(offs_ref[j], 16)
            copy = pltpu.make_async_copy(
                ref.at[pl.ds(0, rows), pl.ds(b * width, width)],
                scratch.at[pl.ds(first, rows), pl.ds(b * width, width)],
                sems.at[b, j],
            )
            copy.start()
            row.append(copy)
        copies.append(row)
    return copies


def wait_all(copies):
    for copy in copies:
        copy.wait()


HBM = pl.BlockSpec(memory_space=pltpu.HBM)
VM = pl.BlockSpec(memory_space=pltpu.VMEM)
SM = pl.BlockSpec(memory_space=pltpu.SMEM)


def params(mbytes):
    return pltpu.CompilerParams(vmem_limit_bytes=mbytes * MB)


def proj_kernel(ns, rotary, offs, n_ref, cos_ref, sin_ref, *rest):
    shards, (o_ref, w_ref, sems) = rest[:ns], rest[ns:]
    copies = fetch(offs, shards, w_ref, sems, w_ref.shape[1])
    wait_all(copies[0])
    y = dot(n_ref[...], w_ref[...])
    for first in range(0, o_ref.shape[1], LANES):
        u = y[:, first : first + LANES]
        if rotary:
            u = rope_block(u, cos_ref[...], sin_ref[...], 1.0)
        o_ref[:, first : first + LANES] = u.astype(bf)


def project(normed, weight, cos_t, sin_t, rotary):
    offs, shards = weight
    rows, depth = normed.shape
    feats = shards[0].shape[1]
    ns = len(shards)
    return pl.pallas_call(
        functools.partial(proj_kernel, ns, rotary),
        out_shape=jax.ShapeDtypeStruct((rows, feats), bf),
        in_specs=[SM, VM, VM, VM] + [HBM] * ns,
        out_specs=VM,
        scratch_shapes=[pltpu.VMEM((depth, feats), bf), pltpu.SemaphoreType.DMA((1, ns))],
        compiler_params=params(16),
        cost_estimate=COST,
    )(offs, normed, cos_t, sin_t, *shards)


def wide_kernel(ns, nt, width, offs, a_ref, *rest):
    shards, (o_ref, w_ref, sems) = rest[:ns], rest[ns:]
    if nt:
        for row in fetch(offs, shards, w_ref, sems, w_ref.shape[1]):
            wait_all(row)
        for first in range(0, o_ref.shape[1], width):
            part = slice(first, first + width)
            o_ref[:, part] = dot(a_ref[...], w_ref[part, :], ((1,), (1,))).astype(o_ref.dtype)
    else:
        for b, row in enumerate(fetch(offs, shards, w_ref, sems, width)):
            wait_all(row)
            part = slice(b * width, (b + 1) * width)
            o_ref[:, part] = dot(a_ref[...], w_ref[:, part]).astype(o_ref.dtype)


def wide_matmul(a, weight, nt, dtype, width=256):
    offs, shards = weight
    rows = a.shape[0]
    ns = len(shards)
    depth, feats = sum(s.shape[0] for s in shards), shards[0].shape[1]
    if feats % width and not nt:
        width = feats
    return pl.pallas_call(
        functools.partial(wide_kernel, ns, nt, width),
        out_shape=jax.ShapeDtypeStruct((rows, depth if nt else feats), dtype),
        in_specs=[SM, VM] + [HBM] * ns,
        out_specs=VM,
        scratch_shapes=[pltpu.VMEM((depth, feats), bf), pltpu.SemaphoreType.DMA((feats // width, ns))],
        compiler_params=params(20),
        cost_estimate=COST,
    )(offs, a, *shards)


def row_kernel(a_ref, w_ref, o_ref):
    o_ref[...] = dot(a_ref[...], w_ref[...]).astype(bf)


def row_matmul(a, weight):
    rows, depth = a.shape
    feats = weight.shape[1]
    step = 128 if rows % 128 == 0 else rows
    return pl.pallas_call(
        row_kernel,
        grid=(rows // step,),
        out_shape=jax.ShapeDtypeStruct((rows, feats), bf),
        in_specs=[pl.BlockSpec((step, depth), lambda i: (i, 0)), pl.BlockSpec((depth, feats), lambda i: (0, 0))],
        out_specs=pl.BlockSpec((step, feats), lambda i: (i, 0)),
        compiler_params=params(56),
        cost_estimate=COST,
    )(a, weight)


def qkv_back_kernel(ns, offs, x_ref, scale_ref, *rest):
    grads, rest = rest[:3], rest[3:]
    shards, (o_ref, gain_ref, w_ref, sems) = rest[: 3 * ns], rest[3 * ns :]
    rows = [fetch(offs, shards[i * ns : (i + 1) * ns], w_ref.at[i], sems.at[i], w_ref.shape[2])[0] for i in range(3)]
    for row in rows:
        wait_all(row)
    width = 256
    for first in range(0, o_ref.shape[1], width):
        part = slice(first, first + width)
        total = None
        for i in range(3):
            y = dot(grads[i][...], w_ref[i, part, :], ((1,), (1,)))
            total = y if total is None else total + y
        o_ref[:, part] = total.astype(bf)
        gain_ref[:, part] = jnp.sum(total * (x_ref[:, part].astype(f32) * scale_ref[...]), axis=0, keepdims=True)


def qkv_back(grads, weights, tokens, scale):
    offs = weights[0][0]
    shards = [s for w in weights for s in w[1]]
    ns = len(weights[0][1])
    rows, feats = grads[0].shape
    depth = sum(s.shape[0] for s in weights[2][1])
    return pl.pallas_call(
        functools.partial(qkv_back_kernel, ns),
        out_shape=(jax.ShapeDtypeStruct((rows, depth), bf), jax.ShapeDtypeStruct((1, depth), f32)),
        in_specs=[SM] + [VM] * 5 + [HBM] * (3 * ns),
        out_specs=(VM, VM),
        scratch_shapes=[pltpu.VMEM((3, depth, feats), bf), pltpu.SemaphoreType.DMA((3, 1, ns))],
        compiler_params=params(28),
        cost_estimate=COST,
    )(offs, tokens, scale, *grads, *shards)


def ffn_kernel(ns, width, offs, n_hbm, dh_hbm, *rest):
    g_shards, u_shards, rest = rest[:ns], rest[ns : 2 * ns], rest[2 * ns :]
    outs, dn_hbm, rest = rest[:3], rest[3], rest[4:]
    n_ref, dh_ref, wg, wu, mids, dn_ref, w_sems, in_sems, out_sems = rest
    hidden, depth = dh_ref.shape[1], n_ref.shape[1]
    blocks = [slice(f, min(f + width, hidden)) for f in range(0, hidden, width)]
    span = lambda part: pl.ds(part.start, part.stop - part.start)

    def load(b):
        part = span(blocks[b])
        copies = [pltpu.make_async_copy(dh_hbm.at[:, part], dh_ref.at[:, part], in_sems.at[b + 1])]
        for i, (shards, scratch) in enumerate(((g_shards, wg), (u_shards, wu))):
            for j, ref in enumerate(shards):
                first = pl.multiple_of(offs[j], 16)
                there = scratch.at[pl.ds(first, ref.shape[0]), part]
                copies.append(pltpu.make_async_copy(ref.at[:, part], there, w_sems.at[i, b, j]))
        for copy in copies:
            copy.start()
        return copies

    first = pltpu.make_async_copy(n_hbm, n_ref, in_sems.at[0])
    first.start()
    loads = [load(0)]
    first.wait()
    stores = []
    for b, part in enumerate(blocks):
        wait_all(loads[b])
        if b + 1 < len(blocks):
            loads.append(load(b + 1))
        gate = dot(n_ref[...], wg[:, part])
        up = dot(n_ref[...], wu[:, part])
        sigma = jax.nn.sigmoid(gate)
        active = gate * sigma
        dh = dh_ref[:, part]
        mids[0, :, part] = (active * up).astype(bf)
        mids[1, :, part] = (dh * up * sigma * (1.0 + gate * (1.0 - sigma))).astype(bf)
        mids[2, :, part] = (dh * active).astype(bf)
        for i in range(3):
            copy = pltpu.make_async_copy(mids.at[i, :, span(part)], outs[i].at[:, span(part)], out_sems.at[i, b])
            copy.start()
            stores.append(copy)
    for b, f in enumerate(range(0, depth, 768)):
        part = slice(f, f + 768)
        total = dot(mids[1], wg[part, :], ((1,), (1,))) + dot(mids[2], wu[part, :], ((1,), (1,)))
        dn_ref[:, part] = total.astype(bf)
        copy = pltpu.make_async_copy(dn_ref.at[:, span(part)], dn_hbm.at[:, span(part)], out_sems.at[3, b])
        copy.start()
        stores.append(copy)
    wait_all(stores)


def ffn(normed, grad_hidden, w_gate, w_up, width=512):
    offs, g_shards = w_gate
    ns = len(g_shards)
    rows, depth = normed.shape
    hidden = g_shards[0].shape[1]
    blocks = -(-hidden // width)
    mid = jax.ShapeDtypeStruct((rows, hidden), bf)
    return pl.pallas_call(
        functools.partial(ffn_kernel, ns, width),
        out_shape=(mid, mid, mid, jax.ShapeDtypeStruct((rows, depth), bf)),
        in_specs=[SM] + [HBM] * (2 + 2 * ns),
        out_specs=(HBM,) * 4,
        scratch_shapes=[
            pltpu.VMEM((rows, depth), bf),
            pltpu.VMEM((rows, hidden), f32),
            pltpu.VMEM((depth, hidden), bf),
            pltpu.VMEM((depth, hidden), bf),
            pltpu.VMEM((3, rows, hidden), bf),
            pltpu.VMEM((rows, depth), bf),
            pltpu.SemaphoreType.DMA((2, blocks, ns)),
            pltpu.SemaphoreType.DMA((blocks + 1,)),
            pltpu.SemaphoreType.DMA((4, max(blocks, depth // 768))),
        ],
        compiler_params=params(60),
        cost_estimate=COST,
    )(offs, normed, grad_hidden, *g_shards, *w_up[1])


def mix_kernel(spans, me_ref, offs, att_ref, x_ref, gain_ref, *rest):
    ns = len(spans)
    shards, (n_ref, own_ref, wo_hbm, w_ref, h_ref, sems) = rest[:ns], rest[ns:]
    copies = []
    for j, (ref, (z0, z1)) in enumerate(zip(shards, spans)):
        rows = pl.ds(pl.multiple_of(offs[j], 16), ref.shape[1])
        copies.append(pltpu.make_async_copy(ref, w_ref.at[z0:z1, rows, :], sems.at[j]))
        copies[-1].start()
    wait_all(copies)
    keep = pltpu.make_async_copy(w_ref.at[me_ref[0]], wo_hbm, sems.at[ns])
    keep.start()
    depth = h_ref.shape[1]
    width = 768
    for f in range(0, depth, width):
        part = slice(f, f + width)
        total = None
        for z in range(att_ref.shape[0]):
            y = dot(att_ref[z], w_ref[z, part, :], ((1,), (1,)))
            total = y if total is None else total + y
        h_ref[:, part] = x_ref[:, part].astype(f32) + branch_scale * total
    step = min(128, h_ref.shape[0])
    for f in range(0, h_ref.shape[0], step):
        part = slice(f, f + step)
        h = h_ref[part, :]
        scale = lax.rsqrt(jnp.mean(h * h, axis=-1, keepdims=True) + norm_eps)
        n_ref[part, :] = (h * scale * gain_ref[...]).astype(bf)
    piece = own_ref.shape[0]
    own_ref[...] = h_ref[pl.ds(pl.multiple_of(me_ref[0] * piece, 8), piece), :]
    keep.wait()


def mix(att, tokens, gain, offs, pieces, me):
    n, rows, feats = att.shape
    depth = tokens.shape[1]
    spans, shards = [p[0] for p in pieces], [p[1] for p in pieces]
    return pl.pallas_call(
        functools.partial(mix_kernel, spans),
        out_shape=(
            jax.ShapeDtypeStruct((rows, depth), bf),
            jax.ShapeDtypeStruct((rows // n, depth), f32),
            jax.ShapeDtypeStruct((depth, feats), bf),
        ),
        in_specs=[SM, SM, VM, VM, VM] + [HBM] * len(shards),
        out_specs=(VM, VM, HBM),
        scratch_shapes=[
            pltpu.VMEM((n, depth, feats), bf),
            pltpu.VMEM((rows, depth), f32),
            pltpu.SemaphoreType.DMA((len(shards) + 1,)),
        ],
        compiler_params=params(56),
        cost_estimate=COST,
    )(me[None], offs, att, tokens, gain[None, :], *shards)


def grad_kernel(offs, a_ref, b_ref, keep_ref, send_ref, at_ref):
    at_ref[...] = a_ref[...].T
    block = keep_ref.shape[0] // 2
    for j in range(4):
        left = at_ref[pl.ds(pl.multiple_of(offs[j], 16), block), :]
        ref = send_ref if j % 2 else keep_ref
        ref[(j // 2) * block : (j // 2 + 1) * block, :] = dot(left, b_ref[...]).astype(bf)


def weight_grad(a, b, offs):
    rows, depth = a.shape
    feats = b.shape[1]
    half = jax.ShapeDtypeStruct((depth // 2, feats), bf)
    return pl.pallas_call(
        grad_kernel,
        out_shape=(half, half),
        in_specs=[SM, VM, VM],
        out_specs=(VM, VM),
        scratch_shapes=[pltpu.VMEM((depth, rows), bf)],
        compiler_params=params(20),
        cost_estimate=COST,
    )(offs, a, b)


def add_kernel(*refs):
    total = refs[0][...].astype(f32)
    for ref in refs[1:-1]:
        total = total + ref[...].astype(f32)
    refs[-1][...] = total.astype(bf)


def add_halves(pairs, others, half):
    rows, cols = pairs[0].shape[0] // 2, pairs[0].shape[1]
    steps = 4 if rows % 64 == 0 else 1
    block = (rows // steps, cols)
    picked = pl.BlockSpec(block, lambda i: (i + half * steps, 0))
    plain = pl.BlockSpec(block, lambda i: (i, 0))
    return pl.pallas_call(
        add_kernel,
        grid=(steps,),
        out_shape=jax.ShapeDtypeStruct((rows, cols), bf),
        in_specs=[picked] * len(pairs) + [plain] * len(others),
        out_specs=plain,
        compiler_params=params(16),
        cost_estimate=COST,
    )(*pairs, *others)


def assemble_kernel(me_ref, *refs):
    out, parts = refs[-1], refs[:-1]
    n, rows = len(parts), parts[0].shape[0]
    for k, part in enumerate(parts):
        first = pl.multiple_of((me_ref[0] + n - k) % n * rows, 8)
        out[pl.ds(first, rows), :] = part[...].astype(f32)


def assemble(parts, me):
    rows, cols = parts[0].shape
    return pl.pallas_call(
        assemble_kernel,
        out_shape=jax.ShapeDtypeStruct((rows * len(parts), cols), f32),
        in_specs=[SM] + [VM] * len(parts),
        out_specs=VM,
        compiler_params=params(24),
        cost_estimate=COST,
    )(me[None], *parts)


def fill_bias(qseg_ref, qpos_ref, kseg_ref, kpos_ref, bias_ref):
    kseg = kseg_ref[...]
    allowed = ((kseg == qseg_ref[...]) | (kseg == 0)) & (kpos_ref[...] <= qpos_ref[...])
    bias_ref[...] = jnp.where(allowed, 0.0, NEG)


def attn_fwd_kernel(parts, heads, *refs):
    qseg, qpos = refs[:2]
    kseg, kpos = refs[2 : 2 + parts], refs[2 + parts : 2 + 2 * parts]
    rest = refs[2 + 2 * parts :]
    q_ref = rest[0]
    k_refs, v_refs = rest[1 : 1 + parts], rest[1 + parts : 1 + 2 * parts]
    o_ref, lse_ref = rest[1 + 2 * parts : 3 + 2 * parts]
    bias = rest[3 + 2 * parts : 3 + 3 * parts]
    ot_ref = rest[3 + 3 * parts]
    blk = pl.program_id(0)

    @pl.when(blk == 0)
    def _():
        for i in range(parts):
            fill_bias(qseg, qpos, kseg[i], kpos[i], bias[i])

    ot_ref[...] = jnp.zeros_like(ot_ref)
    lse_ref[...] = jnp.zeros_like(lse_ref)

    def one(sub):
        lane = lax.broadcasted_iota(jnp.int32, (1, LANES), 1)
        mine = (lane >= sub * HEAD) & (lane < (sub + 1) * HEAD)
        q = jnp.where(mine, q_ref[...] * 0.125, 0.0).astype(bf)
        scores = []
        best = None
        for i in range(parts):
            k = k_refs[i][...]
            s = dot(k, q, ((1,), (1,))) + bias[i][...]
            scores.append(s)
            top = jnp.max(s, axis=0, keepdims=True)
            best = top if best is None else jnp.maximum(best, top)
        total, acc = None, None
        for i in range(parts):
            p = jnp.exp(scores[i] - best)
            t = jnp.sum(p, axis=0, keepdims=True)
            v = v_refs[i][...]
            a = dot(v, p.astype(bf), ((0,), (0,)))
            total = t if total is None else total + t
            acc = a if acc is None else acc + a
        ot_ref[sub * HEAD : (sub + 1) * HEAD, :] = acc[sub * HEAD : (sub + 1) * HEAD, :] / total
        lse_ref[0, sub : sub + 1, :] = best + jnp.log(total)

    for sub in range(LANES // HEAD):
        pl.when(blk * (LANES // HEAD) + sub < heads)(functools.partial(one, sub))
    o_ref[...] = ot_ref[...].T.astype(bf)


def attn_specs(rows, key_rows, feats):
    blocks = -(-feats // LANES)
    row = pl.BlockSpec((1, rows), lambda h: (0, 0))
    cols = [pl.BlockSpec((n, 1), lambda h: (0, 0)) for n in key_rows]
    q = pl.BlockSpec((rows, LANES), lambda h: (0, h))
    ks = [pl.BlockSpec((n, LANES), lambda h: (0, h)) for n in key_rows]
    lse = pl.BlockSpec((1, 8, rows), lambda h: (h, 0, 0))
    return blocks, row, cols, q, ks, lse


def attention_fwd(q, keys, values, q_meta, k_metas, heads):
    rows, feats = q.shape
    parts = len(keys)
    key_rows = [k.shape[0] for k in keys]
    count = sum(key_rows)
    blocks, row, cols, qs, ks, lse = attn_specs(rows, key_rows, feats)
    return pl.pallas_call(
        functools.partial(attn_fwd_kernel, parts, heads),
        grid=(blocks,),
        out_shape=(
            jax.ShapeDtypeStruct((rows, feats), bf),
            jax.ShapeDtypeStruct((blocks, 8, rows), f32),
        ),
        in_specs=[row, row] + cols + cols + [qs] + ks + ks,
        out_specs=(qs, lse),
        scratch_shapes=[pltpu.VMEM((n, rows), f32) for n in key_rows] + [pltpu.VMEM((LANES, rows), f32)],
        compiler_params=pltpu.CompilerParams(vmem_limit_bytes=28 * MB),
        cost_estimate=COST,
    )(
        q_meta[0][None, :], q_meta[1][None, :],
        *[m[0][:, None] for m in k_metas], *[m[1][:, None] for m in k_metas],
        q, *keys, *values,
    )


def attn_bwd_kernel(parts, heads, *refs):
    qseg, qpos, qcos, qsin = refs[:4]
    refs = refs[4:]
    take = lambda n: (refs[:n], refs[n:])
    kseg, refs = take(parts)
    kpos, refs = take(parts)
    kcos, refs = take(parts)
    ksin, refs = take(parts)
    (q_ref, att_ref, do_ref, lse_ref), refs = take(4)
    k_refs, refs = take(parts)
    v_refs, refs = take(parts)
    (dq_ref,), refs = take(1)
    dk_refs, refs = take(parts)
    dv_refs, refs = take(parts)
    bias, refs = take(parts)
    dqt_ref, refs = refs[0], refs[1:]
    dka, refs = take(parts)
    dva, refs = take(parts)
    blk = pl.program_id(0)

    @pl.when(blk == 0)
    def _():
        for i in range(parts):
            fill_bias(qseg, qpos, kseg[i], kpos[i], bias[i])

    prod = (do_ref[...].astype(f32) * att_ref[...].astype(f32)).T
    dqt_ref[...] = jnp.zeros_like(dqt_ref)

    def one(sub):
        lane = lax.broadcasted_iota(jnp.int32, (1, LANES), 1)
        mine = (lane >= sub * HEAD) & (lane < (sub + 1) * HEAD)
        q = jnp.where(mine, q_ref[...] * 0.125, 0.0).astype(bf)
        do = jnp.where(mine, do_ref[...], 0.0).astype(bf)
        lse = lse_ref[0, sub : sub + 1, :]
        delta = jnp.sum(prod[sub * HEAD : (sub + 1) * HEAD, :], axis=0, keepdims=True)
        dqt = None
        for i in range(parts):
            k = k_refs[i][...]
            v = v_refs[i][...]
            p = jnp.exp(dot(k, q, ((1,), (1,))) + bias[i][...] - lse)
            dp = dot(v, do, ((1,), (1,)))
            ds = (p * (dp - delta)).astype(bf)
            dv = dot(p.astype(bf), do)
            dk = dot(ds, q)
            if sub == 0:
                dva[i][...] = dv
                dka[i][...] = dk
            else:
                dva[i][...] += dv
                dka[i][...] += dk
            d = dot(k, ds, ((0,), (0,)))
            dqt = d if dqt is None else dqt + d
        dqt_ref[sub * HEAD : (sub + 1) * HEAD, :] = dqt[sub * HEAD : (sub + 1) * HEAD, :] * 0.125

    for sub in range(LANES // HEAD):
        pl.when(blk * (LANES // HEAD) + sub < heads)(functools.partial(one, sub))
    dq_ref[...] = rope_block(dqt_ref[...].T, qcos[...], qsin[...], -1.0).astype(bf)
    for i in range(parts):
        dk_refs[i][...] = rope_block(dka[i][...], kcos[i][...], ksin[i][...], -1.0).astype(bf)
        dv_refs[i][...] = dva[i][...].astype(bf)


def attention_bwd(q, att, grad_att, lse, keys, values, q_meta, k_metas, heads):
    rows, feats = q.shape
    parts = len(keys)
    key_rows = [k.shape[0] for k in keys]
    count = sum(key_rows)
    blocks, row, cols, qs, ks, lses = attn_specs(rows, key_rows, feats)
    tab = pl.BlockSpec((rows, LANES), lambda h: (0, 0))
    tabs = [pl.BlockSpec((n, LANES), lambda h: (0, 0)) for n in key_rows]
    out = pl.pallas_call(
        functools.partial(attn_bwd_kernel, parts, heads),
        grid=(blocks,),
        out_shape=(jax.ShapeDtypeStruct((rows, feats), bf),)
        + tuple(jax.ShapeDtypeStruct((n, feats), bf) for n in key_rows) * 2,
        in_specs=[row, row, tab, tab] + cols + cols + tabs + tabs + [qs, qs, qs, lses] + ks + ks,
        out_specs=(qs,) + tuple(ks) + tuple(ks),
        scratch_shapes=[pltpu.VMEM((n, rows), f32) for n in key_rows]
        + [pltpu.VMEM((LANES, rows), f32)]
        + [pltpu.VMEM((n, LANES), f32) for n in key_rows] * 2,
        compiler_params=pltpu.CompilerParams(vmem_limit_bytes=40 * MB),
        cost_estimate=COST,
    )(
        q_meta[0][None, :], q_meta[1][None, :], q_meta[2], q_meta[3],
        *[m[0][:, None] for m in k_metas], *[m[1][:, None] for m in k_metas],
        *[m[2] for m in k_metas], *[m[3] for m in k_metas],
        q, att, grad_att, lse, *keys, *values,
    )
    return out[0], out[1 : 1 + parts], out[1 + parts :]


def swap(n, bit):
    return [(i, i ^ bit) for i in range(n)]


def power_of_two(n):
    return n & (n - 1) == 0


def sum_all(value, sizes):
    for axis, n in sizes:
        if power_of_two(n):
            bit = 1
            while bit < n:
                value = value + lax.ppermute(value, axis, swap(n, bit))
                bit *= 2
        else:
            value = lax.psum(value, axis)
    return value


def after(value, *others):
    return lax.optimization_barrier((value,) + others)[0]


def scatter_sum(array):
    return lax.psum_scatter(array, "tensor", scatter_dimension=0, tiled=True).astype(f32)


def gather_rows(array):
    return lax.all_gather(array, "tensor", axis=0, tiled=True)


def gather_weight(shard, n, offs, late=()):
    if n != 4:
        whole = lax.all_gather(shard, "dp", axis=0, tiled=True)
        return offs, [whole], whole
    raw = lax.ppermute(shard, "dp", swap(4, 2))
    far = after(raw, *late)
    near = lax.ppermute(shard, "dp", swap(4, 1))
    cross = lax.ppermute(far, "dp", swap(4, 1))
    return offs, [shard, near, far, cross], raw


def lockstep(items, waits):
    firsts, seconds, before = [], [], ()
    for step in range(len(items) + 1):
        now = []
        if step in waits:
            before += waits[step](firsts, seconds)
        if step > 0:
            seconds.append(lax.ppermute(after(firsts[-1], *before), "ctx", swap(2, 1)))
            now.append(seconds[-1])
        if step < len(items):
            firsts.append(lax.ppermute(after(items[step], *before), "dp", swap(4, 2)))
            now.append(firsts[-1])
        before = tuple(now)
    return firsts, seconds


def two_halves(shard, n, n_ctx, ctx, first, second, offs):
    half = shard.shape[1] // 2
    cross = lambda a: lax.ppermute(a, "dp", swap(4, 1))
    out = []
    for place, piece in ((ctx * half, first), ((1 - ctx) * half, second)):
        out += [(offs[2] + place, piece), (offs[3] + place, cross(piece))]
    return out


class WeightGrad:
    def __init__(self, n, n_ctx, offs):
        self.n, self.n_ctx, self.offs = n, n_ctx, offs

    def make(self, left, right):
        if self.n == 4:
            self.keep, self.first = weight_grad(left, right, self.offs)
        else:
            self.first = self.far = self.whole = dot(left, right, ((0,), (0,))).astype(bf)
        return self

    def trade(self, *late):
        if self.n == 4:
            self.got = lax.ppermute(after(self.first, *late), "dp", swap(4, 1))
            self.far = add_halves((self.keep, self.got), (), 1)
        return self

    def start(self, left, right):
        return self.make(left, right).trade()

    def start_x(self):
        if self.n == 4:
            self.raw = lax.ppermute(self.far, "dp", swap(4, 2))
        else:
            self.raw = lax.psum_scatter(self.whole, "dp", scatter_dimension=0, tiled=True)
        return self.raw

    def finish_x(self, *late):
        other = after(self.raw, *late)
        if self.n == 4:
            other = add_halves((self.keep, self.got), (other,), 0)
        self.total = lax.optimization_barrier(other)
        return self.total

    def along_x(self, *late):
        self.start_x()
        return self.finish_x(*late)

    def along_y(self, *late):
        if self.n_ctx == 2:
            self.other = lax.ppermute(after(self.total, *late), "ctx", swap(2, 1))
        else:
            self.other = lax.psum(self.total, "ctx")
        return self.other

    def along_y_halves(self, first, *late):
        if self.n_ctx != 2:
            return self.along_y()
        half = self.total.shape[0] // 2
        parts = [after(self.total[:half], *first), after(self.total[half:], *late)]
        parts = [lax.ppermute(p, "ctx", swap(2, 1)) for p in parts]
        self.other = jnp.concatenate(parts)
        return parts[0]

    def finish(self, size, *before):
        other = after(self.other, *before).astype(f32)
        out = self.total.astype(f32) + other if self.n_ctx == 2 else other
        return out[:, :size]


def per_device(
    n_dp, n_ctx, n_tp,
    tokens, segment, position, gain_attn, w_query, w_key, w_value, w_out, gain_ffn, w_gate, w_up, w_down, cotangent,
):
    dp, ctx, me = lax.axis_index("dp"), lax.axis_index("ctx"), lax.axis_index("tensor")
    rows = tokens.shape[0]
    piece = rows // n_tp
    shard = gain_attn.shape[0]
    feats, hidden_dev = w_query.shape[1], w_gate.shape[1]
    feats_pad, hidden_pad = up_to(feats, LANES), up_to(hidden_dev, 256)
    mine = functools.partial(lax.dynamic_slice_in_dim, start_index=me * piece, slice_size=piece, axis=0)
    offs = jnp.stack([(dp ^ j) * shard for j in range(4)]) if n_dp == 4 else jnp.zeros((4,), jnp.int32)

    def padded(w, width):
        return jnp.pad(w.astype(bf), ((0, 0), (0, width - w.shape[1])))

    wo_all = lax.all_gather(padded(w_out.T, feats_pad), "tensor", axis=0, tiled=False)
    wk_b = jnp.pad(w_key.astype(bf), ((0, 16), (0, feats_pad - feats)))
    gain_rows = jnp.pad(jnp.stack([gain_attn, gain_ffn]).astype(bf), ((0, 0), (0, feats_pad - shard)))
    wk_b = lax.dynamic_update_slice(wk_b, gain_rows, (shard, 0))
    v_cast, q_cast = padded(w_value, feats_pad), padded(w_query, feats_pad)
    _, wk_ext, raw_k = gather_weight(wk_b, n_dp, offs, (v_cast, q_cast))
    if n_dp == 4:
        own = jnp.stack([w[shard : shard + 2, :shard] for w in wk_ext])
        gains = jnp.zeros((2, n_dp * shard), f32)
        for j in range(4):
            gains = lax.dynamic_update_slice(gains, own[j].astype(f32), (0, offs[j]))
        wk = (offs, wk_ext)
    else:
        ext = wk_ext[0].reshape(n_dp, shard + 16, feats_pad)
        gains = ext[:, shard : shard + 2, :shard].transpose(1, 0, 2).reshape(2, n_dp * shard).astype(f32)
        wk = (offs, [ext[:, :shard].reshape(n_dp * shard, feats_pad)])
    gain1, gain2 = gains[0], gains[1]
    def meta(start, size):
        seg = lax.dynamic_slice_in_dim(segment, start, size)
        pos = lax.dynamic_slice_in_dim(position, start, size)
        return (seg, pos) + rope_tables(pos)

    q_meta = meta(ctx * rows, rows)
    cos_t, sin_t = q_meta[2:]
    inputs = tokens.astype(f32)
    scale1 = lax.rsqrt(jnp.mean(inputs * inputs, axis=-1, keepdims=True) + norm_eps)
    normed1 = (inputs * scale1 * gain1).astype(bf)
    keys = project(normed1, wk, cos_t, sin_t, True)
    *wv, raw_v = gather_weight(after(v_cast, raw_k), n_dp, offs, (keys,))
    values = project(normed1, wv, cos_t, sin_t, False)
    if n_ctx == 2:
        trade = lambda a: lax.ppermute(a, "ctx", swap(2, 1))
        keys_all = [keys, trade(keys)]
        values_all = [values, trade(after(values, keys_all[1]))]
        k_metas = [q_meta, meta((1 - ctx) * rows, rows)]
        early = (values_all[1],)
    else:
        spread = lambda a: [lax.all_gather(a, "ctx", axis=0, tiled=True)]
        keys_all, values_all = spread(keys), spread(values)
        k_metas = [meta(0, segment.shape[0])]
        early = (values,)
    wide = [padded(w, hidden_pad) for w in (w_down.T, w_gate, w_up)]
    half, mid = shard // 2, n_tp // 2
    items = []
    if n_dp == 4 and n_ctx == 2:
        cut = lambda a: lax.dynamic_slice_in_dim(a, ctx * half, half, a.ndim - 2)
        items = [cut(wide[0]), cut(wo_all[:mid]), cut(wo_all[mid:]), cut(wide[1]), cut(wide[2])]
    *wq, raw_q = gather_weight(after(q_cast, wv[1][-2] if n_dp == 4 else raw_v), n_dp, offs, early + tuple(wide) + tuple(t for m in k_metas for t in m[2:]))
    grad_ffn = (branch_scale * cotangent.astype(f32)).astype(bf)
    if n_dp == 4 and n_ctx == 2:
        near = lambda a: lax.ppermute(a, "dp", swap(4, 1))
        items[0] = after(items[0], raw_q)
        query = project(normed1, wq, cos_t, sin_t, True)
        early = []

        def shards_of(own, first, second):
            got = two_halves(own[None], n_dp, n_ctx, ctx, first, second, offs)
            places, pieces = zip((offs[0], own), (offs[1], near(own)), *got)
            return jnp.stack(places), list(pieces)

        def attend(firsts, seconds):
            early.append(attention_fwd(query, keys_all, values_all, q_meta, k_metas, feats // HEAD))
            return (early[0][0],)

        def work_ahead(firsts, seconds):
            wd = shards_of(wide[0], firsts[0], seconds[0])
            early.extend((wd, wide_matmul(after(grad_ffn, firsts[2]), wd, False, f32)))
            return (early[2],)

        waits = {1: lambda f, s: (query, values_all[1]), 2: attend, 4: work_ahead}
        firsts, seconds = lockstep(items, waits)
        att, lse = early.pop(0)
        wd, grad_hidden = early
        wg = shards_of(wide[1], firsts[3], seconds[3])
        places, wo_pieces = [offs[0], offs[1]], [((0, n_tp), wo_all), ((0, n_tp), near(wo_all))]
        for k, span in ((1, (0, mid)), (2, (mid, n_tp))):
            for place, got in two_halves(wo_all, n_dp, n_ctx, ctx, firsts[k], seconds[k], offs):
                places.append(place)
                wo_pieces.append((span, got))
        places = jnp.stack(places)
        late = (firsts[4], seconds[3])
    else:
        wd, wg, wu = [gather_weight(w, n_dp, offs)[:2] for w in wide]
        places, wo_pieces = offs[:1] * 0, [((0, n_tp), lax.all_gather(wo_all, "dp", axis=1, tiled=True))]
        late = ()
        query = project(normed1, wq, cos_t, sin_t, True)
        att, lse = attention_fwd(query, keys_all, values_all, q_meta, k_metas, feats // HEAD)
        grad_hidden = wide_matmul(grad_ffn, wd, False, f32)
    att_all = after(lax.all_gather(att, "tensor", axis=0, tiled=False), *late)
    my_in, my_scale = mine(tokens).astype(f32), mine(scale1)
    normed2, hidden_in, wo_dev = mix(att_all, tokens, gain2, places, wo_pieces, me)
    if n_dp == 4 and n_ctx == 2:
        wu = shards_of(wide[2], firsts[4], after(seconds[4], normed2))
    scale2 = lax.rsqrt(jnp.mean(hidden_in * hidden_in, axis=-1, keepdims=True) + norm_eps)

    hidden, grad_gate, grad_up, partial2 = ffn(normed2, grad_hidden, wg, wu)
    make = lambda: WeightGrad(n_dp, n_ctx, offs)
    grad_d = make().start(grad_ffn, hidden)
    ffn_part = wide_matmul(hidden, wd, True, bf)
    grad_g = make().start(after(normed2, grad_d.far, ffn_part), grad_gate)
    grad_norm2 = scatter_sum(partial2)
    grad_d.along_x(grad_norm2)
    grad_norm2 = after(grad_norm2, grad_d.raw, ffn_part, grad_g.first)
    part_g2 = jnp.sum(grad_norm2 * hidden_in * scale2, axis=0)
    grad_h = (
        mine(cotangent).astype(f32)
        + scale2 * gain2 * grad_norm2
        - hidden_in * scale2**3 * jnp.mean(hidden_in * gain2 * grad_norm2, axis=-1, keepdims=True)
    )
    local_mixed = (branch_scale * grad_h).astype(bf)
    grad_mixed = gather_rows(local_mixed)

    grad_u = make().start(after(normed2, local_mixed), grad_up)
    grad_mixed = after(grad_mixed, grad_d.along_y(), grad_g.along_x(), grad_u.far)
    ffn_part = scatter_sum(after(ffn_part, grad_mixed))

    grad_att = row_matmul(grad_mixed, wo_dev)
    back = lambda k, v, m: attention_bwd(query, att, grad_att, lse, k, v, q_meta, m, feats // HEAD)
    if n_ctx == 2:
        grad_q1, grad_k1, grad_v1 = back(keys_all[1:], values_all[1:], k_metas[1:])
        grad_o = make().start(after(grad_mixed, grad_q1), att)
        grad_att = after(grad_att, grad_o.got, grad_u.start_x())
        grad_q0, grad_k0, grad_v0 = back(keys_all[:1], values_all[:1], k_metas[:1])
        grad_q = (grad_q0.astype(f32) + grad_q1.astype(f32)).astype(bf)
        grad_ks, grad_vs = grad_k0 + grad_k1, grad_v0 + grad_v1
    else:
        grad_u.start_x()
        grad_q, grad_ks, grad_vs = back(keys_all, values_all, k_metas)
        grad_o = make().start(grad_mixed, att)
    if n_ctx == 2:
        merge = lambda pair: (pair[0].astype(f32) + trade(pair[1]).astype(f32)).astype(bf)
    else:
        merge = lambda whole: lax.psum_scatter(whole[0], "ctx", scatter_dimension=0, tiled=True)
    grad_k, grad_v = merge(grad_ks), merge(grad_vs)

    output = (hidden_in + branch_scale * after(ffn_part, grad_q)).astype(bf)
    rounds = [lax.optimization_barrier(output)]
    total_u, total_o = grad_u.finish_x(grad_q), grad_o.along_x()
    partial1, part_g1 = qkv_back((grad_q, grad_k, grad_v), (wq, wk, wv), tokens, scale1)
    ring = [(i, (i + 1) % n_tp) for i in range(n_tp)]
    step = lambda *before: rounds.append(lax.ppermute(after(rounds[-1], *before), "tensor", ring)) or rounds[-1]
    rest = n_tp - 1
    grad_norm1 = scatter_sum(after(partial1, *([step()] if rest > 0 else [])))
    grads_a = [make().start(normed1, g) for g in (grad_q, grad_k, grad_v)]
    totals = [g.along_x() for g in grads_a[:2]]
    grad_g.along_y(grad_k, grad_v)
    part_u = grad_u.along_y_halves((grad_g.other, grads_a[0].raw))
    beside = [step()] if rest > 1 else []
    grad_norm1 = after(grad_norm1, *totals, grad_g.other, part_u, *beside)
    grad_o.along_y()
    grad_in = (
        grad_h
        + my_scale * gain1 * grad_norm1
        - my_in * my_scale**3 * jnp.mean(my_in * gain1 * grad_norm1, axis=-1, keepdims=True)
    )
    local_in = lax.optimization_barrier(grad_in.astype(bf))
    grads_a[2].along_x(local_in)
    grad_in = gather_rows(local_in).astype(f32)
    while len(rounds) < n_tp:
        step(local_in)
    output = assemble(rounds, me)
    gain_sum = after(jnp.concatenate([part_g1, part_g2[None, :]]), local_in)
    gain_sum = sum_all(gain_sum, (("tensor", n_tp), ("dp", n_dp), ("ctx", n_ctx)))
    gain_sum = lax.dynamic_slice_in_dim(gain_sum, dp * shard, shard, 1)

    for g in grads_a:
        g.along_y()
    sum_wd = grad_d.finish(hidden_dev, local_in).T
    sum_wg, sum_wu = grad_g.finish(hidden_dev, local_in), grad_u.finish(hidden_dev, local_in)
    sum_wo = grad_o.finish(feats, local_in, rounds[-1]).T
    sum_wq, sum_wk, sum_wv = [g.finish(feats, local_in) for g in grads_a]
    return (output, grad_in, gain_sum[0], sum_wq, sum_wk, sum_wv, sum_wo, gain_sum[1], sum_wg, sum_wu, sum_wd)


def solution(mesh):
    rows, col, row = P(("dp", "ctx"), None), P("dp", "tensor"), P("tensor", "dp")
    sizes = (mesh.shape["dp"], mesh.shape["ctx"], mesh.shape["tensor"])
    return jax.shard_map(
        functools.partial(per_device, *sizes),
        mesh=mesh,
        in_specs=(rows, P("dp"), P("dp"), P("dp"), col, col, col, row, P("dp"), col, col, row, rows),
        out_specs=(rows, rows, P("dp"), col, col, col, row, P("dp"), col, col, row),
        check_vma=False,
    )
```

```python
import functools
import math

import jax
import jax.numpy as jnp
from jax import lax
from jax.experimental import pallas as pl
from jax.experimental.pallas import tpu as pltpu
from jax.sharding import PartitionSpec as P

HEAD = 64
LANES = 128
NEG = -1e30
norm_eps = 1e-05
branch_scale = 1.4 / math.sqrt(40.0)
bf = jnp.bfloat16
f32 = jnp.float32
MB = 1 << 20


def rope_tables(positions):
    freq = 10000.0 ** (-(jnp.arange(HEAD // 2, dtype=f32) * 2.0 / HEAD))
    angle = positions.astype(f32)[:, None] * freq[None, :]
    cosine, sine = jnp.cos(angle), jnp.sin(angle)
    cos_t = jnp.concatenate([cosine] * 4, axis=1)
    sin_t = jnp.concatenate([-sine, sine, -sine, sine], axis=1)
    return cos_t, sin_t


def rope_block(u, cos_t, sin_t, sign):
    lane = lax.broadcasted_iota(jnp.int32, u.shape, 1)
    low = (lane % HEAD) < HEAD // 2
    partner = jnp.where(low, pltpu.roll(u, LANES - HEAD // 2, 1), pltpu.roll(u, HEAD // 2, 1))
    return u * cos_t + sign * (partner * sin_t)


def dot(a, b, dims=((1,), (0,))):
    return lax.dot_general(a, b, (dims, ((), ())), preferred_element_type=f32)


def up_to(n, unit):
    return -(-n // unit) * unit


COST = pl.CostEstimate(flops=1024, bytes_accessed=1024, transcendentals=0)


def fetch(offs_ref, shards, scratch, sems, width):
    copies = []
    for b in range(scratch.shape[1] // width):
        row = []
        for j, ref in enumerate(shards):
            rows = min(ref.shape[0], scratch.shape[0] // min(len(shards), 4))
            first = pl.multiple_of(offs_ref[j], 16)
            copy = pltpu.make_async_copy(
                ref.at[pl.ds(0, rows), pl.ds(b * width, width)],
                scratch.at[pl.ds(first, rows), pl.ds(b * width, width)],
                sems.at[b, j],
            )
            copy.start()
            row.append(copy)
        copies.append(row)
    return copies


def wait_all(copies):
    for copy in copies:
        copy.wait()


HBM = pl.BlockSpec(memory_space=pltpu.HBM)
VM = pl.BlockSpec(memory_space=pltpu.VMEM)
SM = pl.BlockSpec(memory_space=pltpu.SMEM)


def params(mbytes):
    return pltpu.CompilerParams(vmem_limit_bytes=mbytes * MB)


def proj_kernel(ns, rotary, offs, n_ref, cos_ref, sin_ref, *rest):
    shards, (o_ref, w_ref, sems) = rest[:ns], rest[ns:]
    copies = fetch(offs, shards, w_ref, sems, w_ref.shape[1])
    wait_all(copies[0])
    y = dot(n_ref[...], w_ref[...])
    for first in range(0, o_ref.shape[1], LANES):
        u = y[:, first : first + LANES]
        if rotary:
            u = rope_block(u, cos_ref[...], sin_ref[...], 1.0)
        o_ref[:, first : first + LANES] = u.astype(bf)


def project(normed, weight, cos_t, sin_t, rotary):
    offs, shards = weight
    rows, depth = normed.shape
    feats = shards[0].shape[1]
    ns = len(shards)
    return pl.pallas_call(
        functools.partial(proj_kernel, ns, rotary),
        out_shape=jax.ShapeDtypeStruct((rows, feats), bf),
        in_specs=[SM, VM, VM, VM] + [HBM] * ns,
        out_specs=VM,
        scratch_shapes=[pltpu.VMEM((depth, feats), bf), pltpu.SemaphoreType.DMA((1, ns))],
        compiler_params=params(16),
        cost_estimate=COST,
    )(offs, normed, cos_t, sin_t, *shards)


def wide_kernel(ns, nt, width, offs, a_ref, *rest):
    shards, (o_ref, w_ref, sems) = rest[:ns], rest[ns:]
    if nt:
        for row in fetch(offs, shards, w_ref, sems, w_ref.shape[1]):
            wait_all(row)
        for first in range(0, o_ref.shape[1], width):
            part = slice(first, first + width)
            o_ref[:, part] = dot(a_ref[...], w_ref[part, :], ((1,), (1,))).astype(o_ref.dtype)
    else:
        for b, row in enumerate(fetch(offs, shards, w_ref, sems, width)):
            wait_all(row)
            part = slice(b * width, (b + 1) * width)
            o_ref[:, part] = dot(a_ref[...], w_ref[:, part]).astype(o_ref.dtype)


def wide_matmul(a, weight, nt, dtype, width=256):
    offs, shards = weight
    rows = a.shape[0]
    ns = len(shards)
    depth, feats = sum(s.shape[0] for s in shards), shards[0].shape[1]
    if feats % width and not nt:
        width = feats
    return pl.pallas_call(
        functools.partial(wide_kernel, ns, nt, width),
        out_shape=jax.ShapeDtypeStruct((rows, depth if nt else feats), dtype),
        in_specs=[SM, VM] + [HBM] * ns,
        out_specs=VM,
        scratch_shapes=[pltpu.VMEM((depth, feats), bf), pltpu.SemaphoreType.DMA((feats // width, ns))],
        compiler_params=params(20),
        cost_estimate=COST,
    )(offs, a, *shards)


def row_kernel(a_ref, w_ref, o_ref):
    o_ref[...] = dot(a_ref[...], w_ref[...]).astype(bf)


def row_matmul(a, weight):
    rows, depth = a.shape
    feats = weight.shape[1]
    step = 320 if rows % 320 == 0 else rows
    return pl.pallas_call(
        row_kernel,
        grid=(rows // step,),
        out_shape=jax.ShapeDtypeStruct((rows, feats), bf),
        in_specs=[pl.BlockSpec((step, depth), lambda i: (i, 0)), pl.BlockSpec((depth, feats), lambda i: (0, 0))],
        out_specs=pl.BlockSpec((step, feats), lambda i: (i, 0)),
        compiler_params=params(56),
        cost_estimate=COST,
    )(a, weight)


def qkv_back_kernel(ns, offs, x_ref, scale_ref, *rest):
    grads, rest = rest[:3], rest[3:]
    shards, (o_ref, gain_ref, w_ref, g_ref, sems) = rest[: 3 * ns], rest[3 * ns :]
    feats = grads[0].shape[1]
    copies = []
    for i in range(3):
        cols = pl.ds(i * feats, feats)
        for j, ref in enumerate(shards[i * ns : (i + 1) * ns]):
            rows = pl.ds(pl.multiple_of(offs[j], 16), w_ref.shape[0] // min(ns, 4))
            copies.append(pltpu.make_async_copy(ref.at[pl.ds(0, rows.size), :], w_ref.at[rows, cols], sems.at[i, j]))
            copies[-1].start()
        g_ref[:, i * feats : (i + 1) * feats] = grads[i][...]
    wait_all(copies)
    width = 256
    for first in range(0, o_ref.shape[1], width):
        part = slice(first, first + width)
        total = dot(g_ref[...], w_ref[part, :], ((1,), (1,)))
        o_ref[:, part] = total.astype(bf)
        gain_ref[:, part] = jnp.sum(total * (x_ref[:, part].astype(f32) * scale_ref[...]), axis=0, keepdims=True)


def qkv_back(grads, weights, tokens, scale):
    offs = weights[0][0]
    shards = [s for w in weights for s in w[1]]
    ns = len(weights[0][1])
    rows, feats = grads[0].shape
    depth = sum(s.shape[0] for s in weights[2][1])
    return pl.pallas_call(
        functools.partial(qkv_back_kernel, ns),
        out_shape=(jax.ShapeDtypeStruct((rows, depth), bf), jax.ShapeDtypeStruct((1, depth), f32)),
        in_specs=[SM] + [VM] * 5 + [HBM] * (3 * ns),
        out_specs=(VM, VM),
        scratch_shapes=[
            pltpu.VMEM((depth, 3 * feats), bf),
            pltpu.VMEM((rows, 3 * feats), bf),
            pltpu.SemaphoreType.DMA((3, ns)),
        ],
        compiler_params=params(32),
        cost_estimate=COST,
    )(offs, tokens, scale, *grads, *shards)


def ffn_kernel(ns, width, offs, n_hbm, dh_hbm, *rest):
    g_shards, u_shards, rest = rest[:ns], rest[ns : 2 * ns], rest[2 * ns :]
    outs, dn_hbm, rest = rest[:3], rest[3], rest[4:]
    n_ref, dh_ref, wg, wu, mids, dn_ref, w_sems, in_sems, out_sems = rest
    hidden, depth = dh_ref.shape[1], n_ref.shape[1]
    edges = [0] + list(range(width // 2, hidden, width)) + [hidden]
    blocks = [slice(a, b) for a, b in zip(edges[:-1], edges[1:])]
    span = lambda part: pl.ds(part.start, part.stop - part.start)

    def load(b):
        part = span(blocks[b])
        copies = [pltpu.make_async_copy(dh_hbm.at[:, part], dh_ref.at[:, part], in_sems.at[b + 1])]
        for i, (shards, scratch) in enumerate(((g_shards, wg), (u_shards, wu))):
            for j, ref in enumerate(shards):
                first = pl.multiple_of(offs[j], 16)
                there = scratch.at[pl.ds(first, ref.shape[0]), part]
                copies.append(pltpu.make_async_copy(ref.at[:, part], there, w_sems.at[i, b, j]))
        for copy in copies:
            copy.start()
        return copies

    first = pltpu.make_async_copy(n_hbm, n_ref, in_sems.at[0])
    first.start()
    loads = [load(0)]
    first.wait()
    stores = []
    for b, part in enumerate(blocks):
        wait_all(loads[b])
        if b + 1 < len(blocks):
            loads.append(load(b + 1))
        gate = dot(n_ref[...], wg[:, part])
        up = dot(n_ref[...], wu[:, part])
        sigma = jax.nn.sigmoid(gate)
        active = gate * sigma
        dh = dh_ref[:, part]
        mids[0, :, part] = (active * up).astype(bf)
        mids[1, :, part] = (dh * up * sigma * (1.0 + gate * (1.0 - sigma))).astype(bf)
        mids[2, :, part] = (dh * active).astype(bf)
        for i in range(3):
            copy = pltpu.make_async_copy(mids.at[i, :, span(part)], outs[i].at[:, span(part)], out_sems.at[i, b])
            copy.start()
            stores.append(copy)
    for b, f in enumerate(range(0, depth, 768)):
        part = slice(f, f + 768)
        total = dot(mids[1], wg[part, :], ((1,), (1,))) + dot(mids[2], wu[part, :], ((1,), (1,)))
        dn_ref[:, part] = total.astype(bf)
        copy = pltpu.make_async_copy(dn_ref.at[:, span(part)], dn_hbm.at[:, span(part)], out_sems.at[3, b])
        copy.start()
        stores.append(copy)
    wait_all(stores)


def ffn(normed, grad_hidden, w_gate, w_up, width=512):
    offs, g_shards = w_gate
    ns = len(g_shards)
    rows, depth = normed.shape
    hidden = g_shards[0].shape[1]
    blocks = -(-hidden // width) + 1
    mid = jax.ShapeDtypeStruct((rows, hidden), bf)
    return pl.pallas_call(
        functools.partial(ffn_kernel, ns, width),
        out_shape=(mid, mid, mid, jax.ShapeDtypeStruct((rows, depth), bf)),
        in_specs=[SM] + [HBM] * (2 + 2 * ns),
        out_specs=(HBM,) * 4,
        scratch_shapes=[
            pltpu.VMEM((rows, depth), bf),
            pltpu.VMEM((rows, hidden), f32),
            pltpu.VMEM((depth, hidden), bf),
            pltpu.VMEM((depth, hidden), bf),
            pltpu.VMEM((3, rows, hidden), bf),
            pltpu.VMEM((rows, depth), bf),
            pltpu.SemaphoreType.DMA((2, blocks, ns)),
            pltpu.SemaphoreType.DMA((blocks + 1,)),
            pltpu.SemaphoreType.DMA((4, max(blocks, depth // 768))),
        ],
        compiler_params=params(60),
        cost_estimate=COST,
    )(offs, normed, grad_hidden, *g_shards, *w_up[1])


def mix_kernel(spans, me_ref, offs, gain_ref, att_hbm, x_hbm, *rest):
    ns = len(spans)
    shards, rest = rest[:ns], rest[ns:]
    n_hbm, own_ref, wo_hbm, att_ref, x_ref, w_ref, h_ref, n_ref, w_sems, in_sems, out_sems = rest
    heads, _, feats = att_hbm.shape
    loads = []
    for z in range(heads):
        cols = pl.ds(z * feats, feats)
        row = [pltpu.make_async_copy(att_hbm.at[z], att_ref.at[:, cols], in_sems.at[z])]
        for j, (ref, (z0, z1)) in enumerate(zip(shards, spans)):
            if z0 <= z < z1:
                rows = pl.ds(pl.multiple_of(offs[j], 16), ref.shape[1])
                row.append(pltpu.make_async_copy(ref.at[z - z0], w_ref.at[rows, cols], w_sems.at[z, j]))
        if z == 0:
            row.append(pltpu.make_async_copy(x_hbm, x_ref, in_sems.at[heads]))
        for copy in row:
            copy.start()
        loads.append(row)
    depth, width = h_ref.shape[1], 768
    half = heads // 2
    for z in range(0, heads, half):
        for row in loads[z : z + half]:
            wait_all(row)
        cols = slice(z * feats, (z + half) * feats)
        for f in range(0, depth, width):
            part = slice(f, f + width)
            y = branch_scale * dot(att_ref[:, cols], w_ref[part, cols], ((1,), (1,)))
            h_ref[:, part] = (x_ref[:, part].astype(f32) if z == 0 else h_ref[:, part]) + y
    mine = pl.ds(pl.multiple_of(me_ref[0] * feats, LANES), feats)
    stores = [pltpu.make_async_copy(w_ref.at[:, mine], wo_hbm, out_sems.at[0])]
    stores[0].start()
    rows = h_ref.shape[0]
    step = 128 if rows % 128 == 0 else rows
    for k, f in enumerate(range(0, rows, step)):
        part = slice(f, f + step)
        h = h_ref[part, :]
        scale = lax.rsqrt(jnp.mean(h * h, axis=-1, keepdims=True) + norm_eps)
        n_ref[part, :] = (h * scale * gain_ref[...]).astype(bf)
        stores.append(pltpu.make_async_copy(n_ref.at[pl.ds(f, step), :], n_hbm.at[pl.ds(f, step), :], out_sems.at[k + 1]))
        stores[-1].start()
    piece = own_ref.shape[0]
    own_ref[...] = h_ref[pl.ds(pl.multiple_of(me_ref[0] * piece, 8), piece), :]
    wait_all(stores)


def mix(att, tokens, gain, offs, pieces, me):
    n, rows, feats = att.shape
    depth = tokens.shape[1]
    spans, shards = [p[0] for p in pieces], [p[1] for p in pieces]
    return pl.pallas_call(
        functools.partial(mix_kernel, spans),
        out_shape=(
            jax.ShapeDtypeStruct((rows, depth), bf),
            jax.ShapeDtypeStruct((rows // n, depth), f32),
            jax.ShapeDtypeStruct((depth, feats), bf),
        ),
        in_specs=[SM, SM, VM] + [HBM] * (2 + len(shards)),
        out_specs=(HBM, VM, HBM),
        scratch_shapes=[
            pltpu.VMEM((rows, n * feats), bf),
            pltpu.VMEM((rows, depth), bf),
            pltpu.VMEM((depth, n * feats), bf),
            pltpu.VMEM((rows, depth), f32),
            pltpu.VMEM((rows, depth), bf),
            pltpu.SemaphoreType.DMA((n, len(shards))),
            pltpu.SemaphoreType.DMA((n + 1,)),
            pltpu.SemaphoreType.DMA((1 + -(-rows // 128),)),
        ],
        compiler_params=params(56),
        cost_estimate=COST,
    )(me[None], offs, gain[None, :], att, tokens, *shards)


def grad_kernel(offs, a_ref, b_ref, keep_ref, send_ref, at_ref):
    at_ref[...] = a_ref[...].T
    block = keep_ref.shape[0] // 2
    for j in range(4):
        left = at_ref[pl.ds(pl.multiple_of(offs[j], 16), block), :]
        ref = send_ref if j % 2 else keep_ref
        ref[(j // 2) * block : (j // 2 + 1) * block, :] = dot(left, b_ref[...]).astype(bf)


def weight_grad(a, b, offs):
    rows, depth = a.shape
    feats = b.shape[1]
    half = jax.ShapeDtypeStruct((depth // 2, feats), bf)
    return pl.pallas_call(
        grad_kernel,
        out_shape=(half, half),
        in_specs=[SM, VM, VM],
        out_specs=(VM, VM),
        scratch_shapes=[pltpu.VMEM((depth, rows), bf)],
        compiler_params=params(20),
        cost_estimate=COST,
    )(offs, a, b)


def add_kernel(*refs):
    total = refs[0][...].astype(f32)
    for ref in refs[1:-1]:
        total = total + ref[...].astype(f32)
    refs[-1][...] = total.astype(bf)


def add_halves(pairs, others, half):
    rows, cols = pairs[0].shape[0] // 2, pairs[0].shape[1]
    steps = 4 if rows % 64 == 0 else 1
    block = (rows // steps, cols)
    picked = pl.BlockSpec(block, lambda i: (i + half * steps, 0))
    plain = pl.BlockSpec(block, lambda i: (i, 0))
    return pl.pallas_call(
        add_kernel,
        grid=(steps,),
        out_shape=jax.ShapeDtypeStruct((rows, cols), bf),
        in_specs=[picked] * len(pairs) + [plain] * len(others),
        out_specs=plain,
        compiler_params=params(16),
        cost_estimate=COST,
    )(*pairs, *others)


def assemble_kernel(me_ref, *refs):
    out, parts = refs[-1], refs[:-1]
    n, rows = len(parts), parts[0].shape[0]
    for k, part in enumerate(parts):
        first = pl.multiple_of((me_ref[0] + n - k) % n * rows, 8)
        out[pl.ds(first, rows), :] = part[...].astype(f32)


def assemble(parts, me):
    rows, cols = parts[0].shape
    return pl.pallas_call(
        assemble_kernel,
        out_shape=jax.ShapeDtypeStruct((rows * len(parts), cols), f32),
        in_specs=[SM] + [VM] * len(parts),
        out_specs=VM,
        compiler_params=params(24),
        cost_estimate=COST,
    )(me[None], *parts)


def fill_bias(qseg_ref, qpos_ref, kseg_ref, kpos_ref, bias_ref):
    kseg = kseg_ref[...]
    allowed = ((kseg == qseg_ref[...]) | (kseg == 0)) & (kpos_ref[...] <= qpos_ref[...])
    bias_ref[...] = jnp.where(allowed, 0.0, NEG)


def attn_fwd_kernel(parts, heads, *refs):
    qseg, qpos = refs[:2]
    kseg, kpos = refs[2 : 2 + parts], refs[2 + parts : 2 + 2 * parts]
    rest = refs[2 + 2 * parts :]
    q_ref = rest[0]
    k_refs, v_refs = rest[1 : 1 + parts], rest[1 + parts : 1 + 2 * parts]
    o_ref, lse_ref = rest[1 + 2 * parts : 3 + 2 * parts]
    bias = rest[3 + 2 * parts : 3 + 3 * parts]
    ot_ref = rest[3 + 3 * parts]
    blk = pl.program_id(0)

    @pl.when(blk == 0)
    def _():
        for i in range(parts):
            fill_bias(qseg, qpos, kseg[i], kpos[i], bias[i])

    ot_ref[...] = jnp.zeros_like(ot_ref)
    lse_ref[...] = jnp.zeros_like(lse_ref)

    def one(sub):
        lane = lax.broadcasted_iota(jnp.int32, (1, LANES), 1)
        mine = (lane >= sub * HEAD) & (lane < (sub + 1) * HEAD)
        q = jnp.where(mine, q_ref[...] * 0.125, 0.0).astype(bf)
        scores = []
        best = None
        for i in range(parts):
            k = k_refs[i][...]
            s = dot(k, q, ((1,), (1,))) + bias[i][...]
            scores.append(s)
            top = jnp.max(s, axis=0, keepdims=True)
            best = top if best is None else jnp.maximum(best, top)
        total, acc = None, None
        for i in range(parts):
            p = jnp.exp(scores[i] - best)
            t = jnp.sum(p, axis=0, keepdims=True)
            v = v_refs[i][...]
            a = dot(v, p.astype(bf), ((0,), (0,)))
            total = t if total is None else total + t
            acc = a if acc is None else acc + a
        ot_ref[sub * HEAD : (sub + 1) * HEAD, :] = acc[sub * HEAD : (sub + 1) * HEAD, :] / total
        lse_ref[0, sub : sub + 1, :] = best + jnp.log(total)

    for sub in range(LANES // HEAD):
        pl.when(blk * (LANES // HEAD) + sub < heads)(functools.partial(one, sub))
    o_ref[...] = ot_ref[...].T.astype(bf)


def attn_specs(rows, key_rows, feats):
    blocks = -(-feats // LANES)
    row = pl.BlockSpec((1, rows), lambda h: (0, 0))
    cols = [pl.BlockSpec((n, 1), lambda h: (0, 0)) for n in key_rows]
    q = pl.BlockSpec((rows, LANES), lambda h: (0, h))
    ks = [pl.BlockSpec((n, LANES), lambda h: (0, h)) for n in key_rows]
    lse = pl.BlockSpec((1, 8, rows), lambda h: (h, 0, 0))
    return blocks, row, cols, q, ks, lse


def attention_fwd(q, keys, values, q_meta, k_metas, heads):
    rows, feats = q.shape
    parts = len(keys)
    key_rows = [k.shape[0] for k in keys]
    count = sum(key_rows)
    blocks, row, cols, qs, ks, lse = attn_specs(rows, key_rows, feats)
    return pl.pallas_call(
        functools.partial(attn_fwd_kernel, parts, heads),
        grid=(blocks,),
        out_shape=(
            jax.ShapeDtypeStruct((rows, feats), bf),
            jax.ShapeDtypeStruct((blocks, 8, rows), f32),
        ),
        in_specs=[row, row] + cols + cols + [qs] + ks + ks,
        out_specs=(qs, lse),
        scratch_shapes=[pltpu.VMEM((n, rows), f32) for n in key_rows] + [pltpu.VMEM((LANES, rows), f32)],
        compiler_params=pltpu.CompilerParams(vmem_limit_bytes=28 * MB),
        cost_estimate=COST,
    )(
        q_meta[0][None, :], q_meta[1][None, :],
        *[m[0][:, None] for m in k_metas], *[m[1][:, None] for m in k_metas],
        q, *keys, *values,
    )


def attn_bwd_kernel(parts, heads, *refs):
    qseg, qpos, qcos, qsin = refs[:4]
    refs = refs[4:]
    take = lambda n: (refs[:n], refs[n:])
    kseg, refs = take(parts)
    kpos, refs = take(parts)
    kcos, refs = take(parts)
    ksin, refs = take(parts)
    (q_ref, att_ref, do_ref, lse_ref), refs = take(4)
    k_refs, refs = take(parts)
    v_refs, refs = take(parts)
    (dq_ref,), refs = take(1)
    dk_refs, refs = take(parts)
    dv_refs, refs = take(parts)
    bias, refs = take(parts)
    dqt_ref, refs = refs[0], refs[1:]
    dka, refs = take(parts)
    dva, refs = take(parts)
    blk = pl.program_id(0)

    @pl.when(blk == 0)
    def _():
        for i in range(parts):
            fill_bias(qseg, qpos, kseg[i], kpos[i], bias[i])

    prod = (do_ref[...].astype(f32) * att_ref[...].astype(f32)).T
    dqt_ref[...] = jnp.zeros_like(dqt_ref)

    def one(sub):
        lane = lax.broadcasted_iota(jnp.int32, (1, LANES), 1)
        mine = (lane >= sub * HEAD) & (lane < (sub + 1) * HEAD)
        q = jnp.where(mine, q_ref[...] * 0.125, 0.0).astype(bf)
        do = jnp.where(mine, do_ref[...], 0.0).astype(bf)
        lse = lse_ref[0, sub : sub + 1, :]
        delta = jnp.sum(prod[sub * HEAD : (sub + 1) * HEAD, :], axis=0, keepdims=True)
        dqt = None
        for i in range(parts):
            k = k_refs[i][...]
            v = v_refs[i][...]
            p = jnp.exp(dot(k, q, ((1,), (1,))) + bias[i][...] - lse)
            dp = dot(v, do, ((1,), (1,)))
            ds = (p * (dp - delta)).astype(bf)
            dv = dot(p.astype(bf), do)
            dk = dot(ds, q)
            if sub == 0:
                dva[i][...] = dv
                dka[i][...] = dk
            else:
                dva[i][...] += dv
                dka[i][...] += dk
            d = dot(k, ds, ((0,), (0,)))
            dqt = d if dqt is None else dqt + d
        dqt_ref[sub * HEAD : (sub + 1) * HEAD, :] = dqt[sub * HEAD : (sub + 1) * HEAD, :] * 0.125

    for sub in range(LANES // HEAD):
        pl.when(blk * (LANES // HEAD) + sub < heads)(functools.partial(one, sub))
    dq_ref[...] = rope_block(dqt_ref[...].T, qcos[...], qsin[...], -1.0).astype(bf)
    for i in range(parts):
        dk_refs[i][...] = rope_block(dka[i][...], kcos[i][...], ksin[i][...], -1.0).astype(bf)
        dv_refs[i][...] = dva[i][...].astype(bf)


def attention_bwd(q, att, grad_att, lse, keys, values, q_meta, k_metas, heads):
    rows, feats = q.shape
    parts = len(keys)
    key_rows = [k.shape[0] for k in keys]
    count = sum(key_rows)
    blocks, row, cols, qs, ks, lses = attn_specs(rows, key_rows, feats)
    tab = pl.BlockSpec((rows, LANES), lambda h: (0, 0))
    tabs = [pl.BlockSpec((n, LANES), lambda h: (0, 0)) for n in key_rows]
    out = pl.pallas_call(
        functools.partial(attn_bwd_kernel, parts, heads),
        grid=(blocks,),
        out_shape=(jax.ShapeDtypeStruct((rows, feats), bf),)
        + tuple(jax.ShapeDtypeStruct((n, feats), bf) for n in key_rows) * 2,
        in_specs=[row, row, tab, tab] + cols + cols + tabs + tabs + [qs, qs, qs, lses] + ks + ks,
        out_specs=(qs,) + tuple(ks) + tuple(ks),
        scratch_shapes=[pltpu.VMEM((n, rows), f32) for n in key_rows]
        + [pltpu.VMEM((LANES, rows), f32)]
        + [pltpu.VMEM((n, LANES), f32) for n in key_rows] * 2,
        compiler_params=pltpu.CompilerParams(vmem_limit_bytes=40 * MB),
        cost_estimate=COST,
    )(
        q_meta[0][None, :], q_meta[1][None, :], q_meta[2], q_meta[3],
        *[m[0][:, None] for m in k_metas], *[m[1][:, None] for m in k_metas],
        *[m[2] for m in k_metas], *[m[3] for m in k_metas],
        q, att, grad_att, lse, *keys, *values,
    )
    return out[0], out[1 : 1 + parts], out[1 + parts :]


def swap(n, bit):
    return [(i, i ^ bit) for i in range(n)]


def power_of_two(n):
    return n & (n - 1) == 0


def sum_all(value, sizes):
    for axis, n in sizes:
        if power_of_two(n):
            bit = 1
            while bit < n:
                value = value + lax.ppermute(value, axis, swap(n, bit))
                bit *= 2
        else:
            value = lax.psum(value, axis)
    return value


def after(value, *others):
    return lax.optimization_barrier((value,) + others)[0]


def scatter_sum(array):
    return lax.psum_scatter(array, "tensor", scatter_dimension=0, tiled=True).astype(f32)


def gather_rows(array):
    return lax.all_gather(array, "tensor", axis=0, tiled=True)


def gather_weight(shard, n, offs, late=()):
    if n != 4:
        whole = lax.all_gather(shard, "dp", axis=0, tiled=True)
        return offs, [whole], whole
    raw = lax.ppermute(shard, "dp", swap(4, 2))
    far = after(raw, *late)
    near = lax.ppermute(shard, "dp", swap(4, 1))
    cross = lax.ppermute(far, "dp", swap(4, 1))
    return offs, [shard, near, far, cross], raw


def lockstep(items, waits):
    firsts, seconds, before = [], [], ()
    for step in range(len(items) + 1):
        now = []
        if step in waits:
            before += waits[step](firsts, seconds)
        if step > 0:
            seconds.append(lax.ppermute(after(firsts[-1], *before), "ctx", swap(2, 1)))
            now.append(seconds[-1])
        if step < len(items):
            firsts.append(lax.ppermute(after(items[step], *before), "dp", swap(4, 2)))
            now.append(firsts[-1])
        before = tuple(now)
    return firsts, seconds


def two_halves(shard, n, n_ctx, ctx, first, second, offs):
    half = shard.shape[1] // 2
    cross = lambda a: lax.ppermute(a, "dp", swap(4, 1))
    out = []
    for place, piece in ((ctx * half, first), ((1 - ctx) * half, second)):
        out += [(offs[2] + place, piece), (offs[3] + place, cross(piece))]
    return out


class WeightGrad:
    def __init__(self, n, n_ctx, offs):
        self.n, self.n_ctx, self.offs = n, n_ctx, offs

    def make(self, left, right):
        if self.n == 4:
            self.keep, self.first = weight_grad(left, right, self.offs)
        else:
            self.first = self.far = self.whole = dot(left, right, ((0,), (0,))).astype(bf)
        return self

    def trade(self, *late):
        if self.n == 4:
            self.got = lax.ppermute(after(self.first, *late), "dp", swap(4, 1))
            self.far = add_halves((self.keep, self.got), (), 1)
        return self

    def start(self, left, right):
        return self.make(left, right).trade()

    def start_x(self):
        if self.n == 4:
            self.raw = lax.ppermute(self.far, "dp", swap(4, 2))
        else:
            self.raw = lax.psum_scatter(self.whole, "dp", scatter_dimension=0, tiled=True)
        return self.raw

    def finish_x(self, *late):
        other = after(self.raw, *late)
        if self.n == 4:
            other = add_halves((self.keep, self.got), (other,), 0)
        self.total = lax.optimization_barrier(other)
        return self.total

    def along_x(self, *late):
        self.start_x()
        return self.finish_x(*late)

    def along_y(self, *late):
        if self.n_ctx == 2:
            self.other = lax.ppermute(after(self.total, *late), "ctx", swap(2, 1))
        else:
            self.other = lax.psum(self.total, "ctx")
        return self.other

    def along_y_halves(self, first, *late):
        if self.n_ctx != 2:
            return self.along_y()
        half = self.total.shape[0] // 2
        parts = [after(self.total[:half], *first), after(self.total[half:], *late)]
        parts = [lax.ppermute(p, "ctx", swap(2, 1)) for p in parts]
        self.other = jnp.concatenate(parts)
        return parts[0]

    def finish(self, size, *before):
        other = after(self.other, *before).astype(f32)
        out = self.total.astype(f32) + other if self.n_ctx == 2 else other
        return out[:, :size]


def per_device(
    n_dp, n_ctx, n_tp,
    tokens, segment, position, gain_attn, w_query, w_key, w_value, w_out, gain_ffn, w_gate, w_up, w_down, cotangent,
):
    dp, ctx, me = lax.axis_index("dp"), lax.axis_index("ctx"), lax.axis_index("tensor")
    rows = tokens.shape[0]
    piece = rows // n_tp
    shard = gain_attn.shape[0]
    feats, hidden_dev = w_query.shape[1], w_gate.shape[1]
    feats_pad, hidden_pad = up_to(feats, LANES), up_to(hidden_dev, 256)
    mine = functools.partial(lax.dynamic_slice_in_dim, start_index=me * piece, slice_size=piece, axis=0)
    offs = jnp.stack([(dp ^ j) * shard for j in range(4)]) if n_dp == 4 else jnp.zeros((4,), jnp.int32)

    def padded(w, width):
        return jnp.pad(w.astype(bf), ((0, 0), (0, width - w.shape[1])))

    wo_all = lax.all_gather(padded(w_out.T, feats_pad), "tensor", axis=0, tiled=False)
    wk_b = jnp.pad(w_key.astype(bf), ((0, 16), (0, feats_pad - feats)))
    gain_rows = jnp.pad(jnp.stack([gain_attn, gain_ffn]).astype(bf), ((0, 0), (0, feats_pad - shard)))
    wk_b = lax.dynamic_update_slice(wk_b, gain_rows, (shard, 0))
    v_cast, q_cast = padded(w_value, feats_pad), padded(w_query, feats_pad)
    _, wk_ext, raw_k = gather_weight(wk_b, n_dp, offs, (v_cast, q_cast))
    if n_dp == 4:
        own = jnp.stack([w[shard : shard + 2, :shard] for w in wk_ext])
        gains = jnp.zeros((2, n_dp * shard), f32)
        for j in range(4):
            gains = lax.dynamic_update_slice(gains, own[j].astype(f32), (0, offs[j]))
        wk = (offs, wk_ext)
    else:
        ext = wk_ext[0].reshape(n_dp, shard + 16, feats_pad)
        gains = ext[:, shard : shard + 2, :shard].transpose(1, 0, 2).reshape(2, n_dp * shard).astype(f32)
        wk = (offs, [ext[:, :shard].reshape(n_dp * shard, feats_pad)])
    gain1, gain2 = gains[0], gains[1]
    def meta(start, size):
        seg = lax.dynamic_slice_in_dim(segment, start, size)
        pos = lax.dynamic_slice_in_dim(position, start, size)
        return (seg, pos) + rope_tables(pos)

    q_meta = meta(ctx * rows, rows)
    cos_t, sin_t = q_meta[2:]
    inputs = tokens.astype(f32)
    scale1 = lax.rsqrt(jnp.mean(inputs * inputs, axis=-1, keepdims=True) + norm_eps)
    normed1 = (inputs * scale1 * gain1).astype(bf)
    keys = project(normed1, wk, cos_t, sin_t, True)
    *wv, raw_v = gather_weight(after(v_cast, raw_k), n_dp, offs, (keys,))
    values = project(normed1, wv, cos_t, sin_t, False)
    if n_ctx == 2:
        trade = lambda a: lax.ppermute(a, "ctx", swap(2, 1))
        keys_all = [keys, trade(keys)]
        values_all = [values, trade(after(values, keys_all[1]))]
        k_metas = [q_meta, meta((1 - ctx) * rows, rows)]
        early = (values_all[1],)
    else:
        spread = lambda a: [lax.all_gather(a, "ctx", axis=0, tiled=True)]
        keys_all, values_all = spread(keys), spread(values)
        k_metas = [meta(0, segment.shape[0])]
        early = (values,)
    wide = [padded(w, hidden_pad) for w in (w_down.T, w_gate, w_up)]
    half, mid = shard // 2, n_tp // 2
    items = []
    if n_dp == 4 and n_ctx == 2:
        cut = lambda a: lax.dynamic_slice_in_dim(a, ctx * half, half, a.ndim - 2)
        items = [cut(wide[0]), cut(wo_all[:mid]), cut(wo_all[mid:]), cut(wide[1]), cut(wide[2])]
    *wq, raw_q = gather_weight(after(q_cast, wv[1][-2] if n_dp == 4 else raw_v), n_dp, offs, early + tuple(wide) + tuple(t for m in k_metas for t in m[2:]))
    grad_ffn = (branch_scale * cotangent.astype(f32)).astype(bf)
    if n_dp == 4 and n_ctx == 2:
        near = lambda a: lax.ppermute(a, "dp", swap(4, 1))
        items[0] = after(items[0], raw_q)
        query = project(normed1, wq, cos_t, sin_t, True)
        early = []

        def shards_of(own, first, second):
            got = two_halves(own[None], n_dp, n_ctx, ctx, first, second, offs)
            places, pieces = zip((offs[0], own), (offs[1], near(own)), *got)
            return jnp.stack(places), list(pieces)

        def attend(firsts, seconds):
            early.append(attention_fwd(query, keys_all, values_all, q_meta, k_metas, feats // HEAD))
            return (early[0][0],)

        def work_ahead(firsts, seconds):
            wd = shards_of(wide[0], firsts[0], seconds[0])
            early.extend((wd, wide_matmul(after(grad_ffn, firsts[2]), wd, False, f32)))
            return (early[2],)

        waits = {1: lambda f, s: (query, values_all[1]), 2: attend, 4: work_ahead}
        firsts, seconds = lockstep(items, waits)
        att, lse = early.pop(0)
        wd, grad_hidden = early
        wg = shards_of(wide[1], firsts[3], seconds[3])
        places, wo_pieces = [offs[0], offs[1]], [((0, n_tp), wo_all), ((0, n_tp), near(wo_all))]
        for k, span in ((1, (0, mid)), (2, (mid, n_tp))):
            for place, got in two_halves(wo_all, n_dp, n_ctx, ctx, firsts[k], seconds[k], offs):
                places.append(place)
                wo_pieces.append((span, got))
        places = jnp.stack(places)
        late = (firsts[4], seconds[3])
    else:
        wd, wg, wu = [gather_weight(w, n_dp, offs)[:2] for w in wide]
        places, wo_pieces = offs[:1] * 0, [((0, n_tp), lax.all_gather(wo_all, "dp", axis=1, tiled=True))]
        late = ()
        query = project(normed1, wq, cos_t, sin_t, True)
        att, lse = attention_fwd(query, keys_all, values_all, q_meta, k_metas, feats // HEAD)
        grad_hidden = wide_matmul(grad_ffn, wd, False, f32)
    att_all = after(lax.all_gather(att, "tensor", axis=0, tiled=False), *late)
    my_in, my_scale = mine(tokens).astype(f32), mine(scale1)
    normed2, hidden_in, wo_dev = mix(att_all, tokens, gain2, places, wo_pieces, me)
    if n_dp == 4 and n_ctx == 2:
        wu = shards_of(wide[2], firsts[4], after(seconds[4], normed2))
    scale2 = lax.rsqrt(jnp.mean(hidden_in * hidden_in, axis=-1, keepdims=True) + norm_eps)

    hidden, grad_gate, grad_up, partial2 = ffn(normed2, grad_hidden, wg, wu)
    make = lambda: WeightGrad(n_dp, n_ctx, offs)
    grad_d = make().start(grad_ffn, hidden)
    ffn_part = wide_matmul(hidden, wd, True, bf)
    grad_g = make().start(after(normed2, grad_d.far, ffn_part), grad_gate)
    grad_norm2 = scatter_sum(partial2)
    grad_d.along_x(grad_norm2)
    grad_norm2 = after(grad_norm2, grad_d.raw, ffn_part, grad_g.first)
    part_g2 = jnp.sum(grad_norm2 * hidden_in * scale2, axis=0)
    grad_h = (
        mine(cotangent).astype(f32)
        + scale2 * gain2 * grad_norm2
        - hidden_in * scale2**3 * jnp.mean(hidden_in * gain2 * grad_norm2, axis=-1, keepdims=True)
    )
    local_mixed = (branch_scale * grad_h).astype(bf)
    grad_mixed = gather_rows(local_mixed)

    grad_u = make().start(after(normed2, local_mixed), grad_up)
    grad_mixed = after(grad_mixed, grad_d.along_y(), grad_g.along_x(), grad_u.far)
    ffn_part = scatter_sum(after(ffn_part, grad_mixed))

    grad_att = row_matmul(grad_mixed, wo_dev)
    back = lambda k, v, m: attention_bwd(query, att, grad_att, lse, k, v, q_meta, m, feats // HEAD)
    if n_ctx == 2:
        grad_q1, grad_k1, grad_v1 = back(keys_all[1:], values_all[1:], k_metas[1:])
        grad_o = make().start(after(grad_mixed, grad_q1), att)
        grad_att = after(grad_att, grad_o.got, grad_u.start_x())
        grad_q0, grad_k0, grad_v0 = back(keys_all[:1], values_all[:1], k_metas[:1])
        grad_q = (grad_q0.astype(f32) + grad_q1.astype(f32)).astype(bf)
        grad_ks, grad_vs = grad_k0 + grad_k1, grad_v0 + grad_v1
    else:
        grad_u.start_x()
        grad_q, grad_ks, grad_vs = back(keys_all, values_all, k_metas)
        grad_o = make().start(grad_mixed, att)
    if n_ctx == 2:
        merge = lambda pair: (pair[0].astype(f32) + trade(pair[1]).astype(f32)).astype(bf)
    else:
        merge = lambda whole: lax.psum_scatter(whole[0], "ctx", scatter_dimension=0, tiled=True)
    grad_k, grad_v = merge(grad_ks), merge(grad_vs)

    output = (hidden_in + branch_scale * after(ffn_part, grad_q)).astype(bf)
    rounds = [lax.optimization_barrier(output)]
    total_u, total_o = grad_u.finish_x(grad_q), grad_o.along_x()
    partial1, part_g1 = qkv_back((grad_q, grad_k, grad_v), (wq, wk, wv), tokens, scale1)
    ring = [(i, (i + 1) % n_tp) for i in range(n_tp)]
    step = lambda *before: rounds.append(lax.ppermute(after(rounds[-1], *before), "tensor", ring)) or rounds[-1]
    rest = n_tp - 1
    grad_norm1 = scatter_sum(after(partial1, *([step()] if rest > 0 else [])))
    grads_a = [make().start(normed1, g) for g in (grad_q, grad_k, grad_v)]
    totals = [g.along_x() for g in grads_a[:2]]
    grad_g.along_y(grad_k, grad_v)
    part_u = grad_u.along_y_halves((grad_g.other, grads_a[0].raw))
    beside = [step()] if rest > 1 else []
    grad_norm1 = after(grad_norm1, *totals, grad_g.other, part_u, *beside)
    grad_o.along_y()
    grad_in = (
        grad_h
        + my_scale * gain1 * grad_norm1
        - my_in * my_scale**3 * jnp.mean(my_in * gain1 * grad_norm1, axis=-1, keepdims=True)
    )
    local_in = lax.optimization_barrier(grad_in.astype(bf))
    grads_a[2].along_x(local_in)
    grad_in = gather_rows(local_in).astype(f32)
    while len(rounds) < n_tp:
        step(local_in)
    output = assemble(rounds, me)
    gain_sum = after(jnp.concatenate([part_g1, part_g2[None, :]]), local_in)
    gain_sum = sum_all(gain_sum, (("tensor", n_tp), ("dp", n_dp)))
    gain_sum = sum_all(after(gain_sum, output), (("ctx", n_ctx),))
    gain_sum = lax.dynamic_slice_in_dim(gain_sum, dp * shard, shard, 1)

    for g in grads_a:
        g.along_y()
    sum_wd = grad_d.finish(hidden_dev, local_in).T
    sum_wg, sum_wu = grad_g.finish(hidden_dev, local_in), grad_u.finish(hidden_dev, local_in)
    sum_wo = grad_o.finish(feats, local_in, rounds[-1]).T
    sum_wq, sum_wk, sum_wv = [g.finish(feats, local_in) for g in grads_a]
    return (output, grad_in, gain_sum[0], sum_wq, sum_wk, sum_wv, sum_wo, gain_sum[1], sum_wg, sum_wu, sum_wd)


def solution(mesh):
    rows, col, row = P(("dp", "ctx"), None), P("dp", "tensor"), P("tensor", "dp")
    sizes = (mesh.shape["dp"], mesh.shape["ctx"], mesh.shape["tensor"])
    return jax.shard_map(
        functools.partial(per_device, *sizes),
        mesh=mesh,
        in_specs=(rows, P("dp"), P("dp"), P("dp"), col, col, col, row, P("dp"), col, col, row, rows),
        out_specs=(rows, rows, P("dp"), col, col, col, row, P("dp"), col, col, row),
        check_vma=False,
    )
```

```python
import functools
import math

import jax
import jax.numpy as jnp
from jax import lax
from jax.experimental import pallas as pl
from jax.experimental.pallas import tpu as pltpu
from jax.sharding import PartitionSpec as P

HEAD = 64
LANES = 128
NEG = -1e30
norm_eps = 1e-05
branch_scale = 1.4 / math.sqrt(40.0)
bf = jnp.bfloat16
f32 = jnp.float32
MB = 1 << 20


def rope_tables(positions):
    freq = 10000.0 ** (-(jnp.arange(HEAD // 2, dtype=f32) * 2.0 / HEAD))
    angle = positions.astype(f32)[:, None] * freq[None, :]
    cosine, sine = jnp.cos(angle), jnp.sin(angle)
    cos_t = jnp.concatenate([cosine] * 4, axis=1)
    sin_t = jnp.concatenate([-sine, sine, -sine, sine], axis=1)
    return cos_t, sin_t


def rope_block(u, cos_t, sin_t, sign):
    lane = lax.broadcasted_iota(jnp.int32, u.shape, 1)
    low = (lane % HEAD) < HEAD // 2
    partner = jnp.where(low, pltpu.roll(u, LANES - HEAD // 2, 1), pltpu.roll(u, HEAD // 2, 1))
    return u * cos_t + sign * (partner * sin_t)


def dot(a, b, dims=((1,), (0,))):
    return lax.dot_general(a, b, (dims, ((), ())), preferred_element_type=f32)


def up_to(n, unit):
    return -(-n // unit) * unit


COST = pl.CostEstimate(flops=1024, bytes_accessed=1024, transcendentals=0)


def fetch(offs_ref, shards, scratch, sems, width):
    copies = []
    for b in range(scratch.shape[1] // width):
        row = []
        for j, ref in enumerate(shards):
            rows = min(ref.shape[0], scratch.shape[0] // min(len(shards), 4))
            first = pl.multiple_of(offs_ref[j], 16)
            copy = pltpu.make_async_copy(
                ref.at[pl.ds(0, rows), pl.ds(b * width, width)],
                scratch.at[pl.ds(first, rows), pl.ds(b * width, width)],
                sems.at[b, j],
            )
            copy.start()
            row.append(copy)
        copies.append(row)
    return copies


def wait_all(copies):
    for copy in copies:
        copy.wait()


HBM = pl.BlockSpec(memory_space=pltpu.HBM)
VM = pl.BlockSpec(memory_space=pltpu.VMEM)
SM = pl.BlockSpec(memory_space=pltpu.SMEM)


def params(mbytes):
    return pltpu.CompilerParams(vmem_limit_bytes=mbytes * MB)


def proj_kernel(ns, rotary, offs, n_ref, cos_ref, sin_ref, *rest):
    shards, (o_ref, w_ref, sems) = rest[:ns], rest[ns:]
    copies = fetch(offs, shards, w_ref, sems, w_ref.shape[1])
    wait_all(copies[0])
    y = dot(n_ref[...], w_ref[...])
    for first in range(0, o_ref.shape[1], LANES):
        u = y[:, first : first + LANES]
        if rotary:
            u = rope_block(u, cos_ref[...], sin_ref[...], 1.0)
        o_ref[:, first : first + LANES] = u.astype(bf)


def project(normed, weight, cos_t, sin_t, rotary):
    offs, shards = weight
    rows, depth = normed.shape
    feats = shards[0].shape[1]
    ns = len(shards)
    return pl.pallas_call(
        functools.partial(proj_kernel, ns, rotary),
        out_shape=jax.ShapeDtypeStruct((rows, feats), bf),
        in_specs=[SM, VM, VM, VM] + [HBM] * ns,
        out_specs=VM,
        scratch_shapes=[pltpu.VMEM((depth, feats), bf), pltpu.SemaphoreType.DMA((1, ns))],
        compiler_params=params(16),
        cost_estimate=COST,
    )(offs, normed, cos_t, sin_t, *shards)


def wide_kernel(ns, nt, width, offs, a_ref, *rest):
    shards, (o_ref, w_ref, sems) = rest[:ns], rest[ns:]
    if nt:
        for row in fetch(offs, shards, w_ref, sems, w_ref.shape[1]):
            wait_all(row)
        for first in range(0, o_ref.shape[1], width):
            part = slice(first, first + width)
            o_ref[:, part] = dot(a_ref[...], w_ref[part, :], ((1,), (1,))).astype(o_ref.dtype)
    else:
        for b, row in enumerate(fetch(offs, shards, w_ref, sems, width)):
            wait_all(row)
            part = slice(b * width, (b + 1) * width)
            o_ref[:, part] = dot(a_ref[...], w_ref[:, part]).astype(o_ref.dtype)


def wide_matmul(a, weight, nt, dtype, width=256):
    offs, shards = weight
    rows = a.shape[0]
    ns = len(shards)
    depth, feats = sum(s.shape[0] for s in shards), shards[0].shape[1]
    if feats % width and not nt:
        width = feats
    return pl.pallas_call(
        functools.partial(wide_kernel, ns, nt, width),
        out_shape=jax.ShapeDtypeStruct((rows, depth if nt else feats), dtype),
        in_specs=[SM, VM] + [HBM] * ns,
        out_specs=VM,
        scratch_shapes=[pltpu.VMEM((depth, feats), bf), pltpu.SemaphoreType.DMA((feats // width, ns))],
        compiler_params=params(20),
        cost_estimate=COST,
    )(offs, a, *shards)


def row_kernel(a_ref, w_ref, o_ref):
    o_ref[...] = dot(a_ref[...], w_ref[...]).astype(bf)


def row_matmul(a, weight):
    rows, depth = a.shape
    feats = weight.shape[1]
    step = 320 if rows % 320 == 0 else rows
    return pl.pallas_call(
        row_kernel,
        grid=(rows // step,),
        out_shape=jax.ShapeDtypeStruct((rows, feats), bf),
        in_specs=[pl.BlockSpec((step, depth), lambda i: (i, 0)), pl.BlockSpec((depth, feats), lambda i: (0, 0))],
        out_specs=pl.BlockSpec((step, feats), lambda i: (i, 0)),
        compiler_params=params(56),
        cost_estimate=COST,
    )(a, weight)


def qkv_back_kernel(ns, offs, x_ref, scale_ref, *rest):
    grads, rest = rest[:3], rest[3:]
    shards, (o_ref, gain_ref, w_ref, g_ref, sems) = rest[: 3 * ns], rest[3 * ns :]
    feats = grads[0].shape[1]
    copies = []
    for i in range(3):
        cols = pl.ds(i * feats, feats)
        for j, ref in enumerate(shards[i * ns : (i + 1) * ns]):
            rows = pl.ds(pl.multiple_of(offs[j], 16), w_ref.shape[0] // min(ns, 4))
            copies.append(pltpu.make_async_copy(ref.at[pl.ds(0, rows.size), :], w_ref.at[rows, cols], sems.at[i, j]))
            copies[-1].start()
        g_ref[:, i * feats : (i + 1) * feats] = grads[i][...]
    wait_all(copies)
    width = 256
    for first in range(0, o_ref.shape[1], width):
        part = slice(first, first + width)
        total = dot(g_ref[...], w_ref[part, :], ((1,), (1,)))
        o_ref[:, part] = total.astype(bf)
        gain_ref[:, part] = jnp.sum(total * (x_ref[:, part].astype(f32) * scale_ref[...]), axis=0, keepdims=True)


def qkv_back(grads, weights, tokens, scale):
    offs = weights[0][0]
    shards = [s for w in weights for s in w[1]]
    ns = len(weights[0][1])
    rows, feats = grads[0].shape
    depth = sum(s.shape[0] for s in weights[2][1])
    return pl.pallas_call(
        functools.partial(qkv_back_kernel, ns),
        out_shape=(jax.ShapeDtypeStruct((rows, depth), bf), jax.ShapeDtypeStruct((1, depth), f32)),
        in_specs=[SM] + [VM] * 5 + [HBM] * (3 * ns),
        out_specs=(VM, VM),
        scratch_shapes=[
            pltpu.VMEM((depth, 3 * feats), bf),
            pltpu.VMEM((rows, 3 * feats), bf),
            pltpu.SemaphoreType.DMA((3, ns)),
        ],
        compiler_params=params(32),
        cost_estimate=COST,
    )(offs, tokens, scale, *grads, *shards)


def ffn_kernel(ns, width, offs, n_hbm, dh_hbm, *rest):
    g_shards, u_shards, rest = rest[:ns], rest[ns : 2 * ns], rest[2 * ns :]
    outs, dn_hbm, rest = rest[:3], rest[3], rest[4:]
    n_ref, dh_ref, wg, wu, mids, dn_ref, w_sems, in_sems, out_sems = rest
    hidden, depth = dh_ref.shape[1], n_ref.shape[1]
    edges = [0] + list(range(width // 2, hidden, width)) + [hidden]
    blocks = [slice(a, b) for a, b in zip(edges[:-1], edges[1:])]
    span = lambda part: pl.ds(part.start, part.stop - part.start)

    def load(b):
        part = span(blocks[b])
        copies = [pltpu.make_async_copy(dh_hbm.at[:, part], dh_ref.at[:, part], in_sems.at[b + 1])]
        for i, (shards, scratch) in enumerate(((g_shards, wg), (u_shards, wu))):
            for j, ref in enumerate(shards):
                first = pl.multiple_of(offs[j], 16)
                there = scratch.at[pl.ds(first, ref.shape[0]), part]
                copies.append(pltpu.make_async_copy(ref.at[:, part], there, w_sems.at[i, b, j]))
        for copy in copies:
            copy.start()
        return copies

    first = pltpu.make_async_copy(n_hbm, n_ref, in_sems.at[0])
    first.start()
    loads = [load(0)]
    first.wait()
    stores = []
    for b, part in enumerate(blocks):
        wait_all(loads[b])
        if b + 1 < len(blocks):
            loads.append(load(b + 1))
        gate = dot(n_ref[...], wg[:, part])
        up = dot(n_ref[...], wu[:, part])
        sigma = jax.nn.sigmoid(gate)
        active = gate * sigma
        dh = dh_ref[:, part]
        mids[0, :, part] = (active * up).astype(bf)
        mids[1, :, part] = (dh * up * sigma * (1.0 + gate * (1.0 - sigma))).astype(bf)
        mids[2, :, part] = (dh * active).astype(bf)
        for i in range(3):
            copy = pltpu.make_async_copy(mids.at[i, :, span(part)], outs[i].at[:, span(part)], out_sems.at[i, b])
            copy.start()
            stores.append(copy)
    for b, f in enumerate(range(0, depth, 768)):
        part = slice(f, f + 768)
        total = dot(mids[1], wg[part, :], ((1,), (1,))) + dot(mids[2], wu[part, :], ((1,), (1,)))
        dn_ref[:, part] = total.astype(bf)
        copy = pltpu.make_async_copy(dn_ref.at[:, span(part)], dn_hbm.at[:, span(part)], out_sems.at[3, b])
        copy.start()
        stores.append(copy)
    wait_all(stores)


def ffn(normed, grad_hidden, w_gate, w_up, width=512):
    offs, g_shards = w_gate
    ns = len(g_shards)
    rows, depth = normed.shape
    hidden = g_shards[0].shape[1]
    blocks = -(-hidden // width) + 1
    mid = jax.ShapeDtypeStruct((rows, hidden), bf)
    return pl.pallas_call(
        functools.partial(ffn_kernel, ns, width),
        out_shape=(mid, mid, mid, jax.ShapeDtypeStruct((rows, depth), bf)),
        in_specs=[SM] + [HBM] * (2 + 2 * ns),
        out_specs=(HBM,) * 4,
        scratch_shapes=[
            pltpu.VMEM((rows, depth), bf),
            pltpu.VMEM((rows, hidden), f32),
            pltpu.VMEM((depth, hidden), bf),
            pltpu.VMEM((depth, hidden), bf),
            pltpu.VMEM((3, rows, hidden), bf),
            pltpu.VMEM((rows, depth), bf),
            pltpu.SemaphoreType.DMA((2, blocks, ns)),
            pltpu.SemaphoreType.DMA((blocks + 1,)),
            pltpu.SemaphoreType.DMA((4, max(blocks, depth // 768))),
        ],
        compiler_params=params(60),
        cost_estimate=COST,
    )(offs, normed, grad_hidden, *g_shards, *w_up[1])


def mix_kernel(spans, me_ref, offs, gain_ref, att_hbm, x_hbm, *rest):
    ns = len(spans)
    shards, rest = rest[:ns], rest[ns:]
    n_hbm, own_ref, wo_hbm, att_ref, x_ref, w_ref, h_ref, n_ref, w_sems, in_sems, out_sems = rest
    heads, _, feats = att_hbm.shape
    loads = []
    for z in range(heads):
        cols = pl.ds(z * feats, feats)
        row = [pltpu.make_async_copy(att_hbm.at[z], att_ref.at[:, cols], in_sems.at[z])]
        for j, (ref, (z0, z1)) in enumerate(zip(shards, spans)):
            if z0 <= z < z1:
                rows = pl.ds(pl.multiple_of(offs[j], 16), ref.shape[1])
                row.append(pltpu.make_async_copy(ref.at[z - z0], w_ref.at[rows, cols], w_sems.at[z, j]))
        if z == 0:
            row.append(pltpu.make_async_copy(x_hbm, x_ref, in_sems.at[heads]))
        for copy in row:
            copy.start()
        loads.append(row)
    depth, width = h_ref.shape[1], 768
    half = heads // 2
    for z in range(0, heads, half):
        for row in loads[z : z + half]:
            wait_all(row)
        cols = slice(z * feats, (z + half) * feats)
        for f in range(0, depth, width):
            part = slice(f, f + width)
            y = branch_scale * dot(att_ref[:, cols], w_ref[part, cols], ((1,), (1,)))
            h_ref[:, part] = (x_ref[:, part].astype(f32) if z == 0 else h_ref[:, part]) + y
    mine = pl.ds(pl.multiple_of(me_ref[0] * feats, LANES), feats)
    stores = [pltpu.make_async_copy(w_ref.at[:, mine], wo_hbm, out_sems.at[0])]
    stores[0].start()
    rows = h_ref.shape[0]
    step = 128 if rows % 128 == 0 else rows
    for k, f in enumerate(range(0, rows, step)):
        part = slice(f, f + step)
        h = h_ref[part, :]
        scale = lax.rsqrt(jnp.mean(h * h, axis=-1, keepdims=True) + norm_eps)
        n_ref[part, :] = (h * scale * gain_ref[...]).astype(bf)
        stores.append(pltpu.make_async_copy(n_ref.at[pl.ds(f, step), :], n_hbm.at[pl.ds(f, step), :], out_sems.at[k + 1]))
        stores[-1].start()
    piece = own_ref.shape[0]
    own_ref[...] = h_ref[pl.ds(pl.multiple_of(me_ref[0] * piece, 8), piece), :]
    wait_all(stores)


def mix(att, tokens, gain, offs, pieces, me):
    n, rows, feats = att.shape
    depth = tokens.shape[1]
    spans, shards = [p[0] for p in pieces], [p[1] for p in pieces]
    return pl.pallas_call(
        functools.partial(mix_kernel, spans),
        out_shape=(
            jax.ShapeDtypeStruct((rows, depth), bf),
            jax.ShapeDtypeStruct((rows // n, depth), f32),
            jax.ShapeDtypeStruct((depth, feats), bf),
        ),
        in_specs=[SM, SM, VM] + [HBM] * (2 + len(shards)),
        out_specs=(HBM, VM, HBM),
        scratch_shapes=[
            pltpu.VMEM((rows, n * feats), bf),
            pltpu.VMEM((rows, depth), bf),
            pltpu.VMEM((depth, n * feats), bf),
            pltpu.VMEM((rows, depth), f32),
            pltpu.VMEM((rows, depth), bf),
            pltpu.SemaphoreType.DMA((n, len(shards))),
            pltpu.SemaphoreType.DMA((n + 1,)),
            pltpu.SemaphoreType.DMA((1 + -(-rows // 128),)),
        ],
        compiler_params=params(56),
        cost_estimate=COST,
    )(me[None], offs, gain[None, :], att, tokens, *shards)


def grad_kernel(offs, a_ref, b_ref, keep_ref, send_ref, at_ref):
    at_ref[...] = a_ref[...].T
    block = keep_ref.shape[0] // 2
    for j in range(4):
        left = at_ref[pl.ds(pl.multiple_of(offs[j], 16), block), :]
        ref = send_ref if j % 2 else keep_ref
        ref[(j // 2) * block : (j // 2 + 1) * block, :] = dot(left, b_ref[...]).astype(bf)


def weight_grad(a, b, offs):
    rows, depth = a.shape
    feats = b.shape[1]
    half = jax.ShapeDtypeStruct((depth // 2, feats), bf)
    return pl.pallas_call(
        grad_kernel,
        out_shape=(half, half),
        in_specs=[SM, VM, VM],
        out_specs=(VM, VM),
        scratch_shapes=[pltpu.VMEM((depth, rows), bf)],
        compiler_params=params(20),
        cost_estimate=COST,
    )(offs, a, b)


def add_kernel(*refs):
    total = refs[0][...].astype(f32)
    for ref in refs[1:-1]:
        total = total + ref[...].astype(f32)
    refs[-1][...] = total.astype(bf)


def add_halves(pairs, others, half):
    rows, cols = pairs[0].shape[0] // 2, pairs[0].shape[1]
    steps = 4 if rows % 64 == 0 else 1
    block = (rows // steps, cols)
    picked = pl.BlockSpec(block, lambda i: (i + half * steps, 0))
    plain = pl.BlockSpec(block, lambda i: (i, 0))
    return pl.pallas_call(
        add_kernel,
        grid=(steps,),
        out_shape=jax.ShapeDtypeStruct((rows, cols), bf),
        in_specs=[picked] * len(pairs) + [plain] * len(others),
        out_specs=plain,
        compiler_params=params(16),
        cost_estimate=COST,
    )(*pairs, *others)


def widen_kernel(a_ref, o_ref):
    o_ref[...] = a_ref[...].astype(f32)


def widen(a):
    rows, cols = a.shape
    step = 128 if rows % 128 == 0 else rows
    block = pl.BlockSpec((step, cols), lambda i: (i, 0))
    return pl.pallas_call(
        widen_kernel,
        grid=(rows // step,),
        out_shape=jax.ShapeDtypeStruct((rows, cols), f32),
        in_specs=[block],
        out_specs=block,
        compiler_params=params(24),
        cost_estimate=COST,
    )(a)


def assemble_kernel(me_ref, *refs):
    out, parts = refs[-1], refs[:-1]
    n, rows = len(parts), parts[0].shape[0]
    for k, part in enumerate(parts):
        first = pl.multiple_of((me_ref[0] + n - k) % n * rows, 8)
        out[pl.ds(first, rows), :] = part[...].astype(f32)


def assemble(parts, me):
    rows, cols = parts[0].shape
    return pl.pallas_call(
        assemble_kernel,
        out_shape=jax.ShapeDtypeStruct((rows * len(parts), cols), f32),
        in_specs=[SM] + [VM] * len(parts),
        out_specs=VM,
        compiler_params=params(24),
        cost_estimate=COST,
    )(me[None], *parts)


def fill_bias(qseg_ref, qpos_ref, kseg_ref, kpos_ref, bias_ref):
    kseg = kseg_ref[...]
    allowed = ((kseg == qseg_ref[...]) | (kseg == 0)) & (kpos_ref[...] <= qpos_ref[...])
    bias_ref[...] = jnp.where(allowed, 0.0, NEG)


def attn_fwd_kernel(parts, heads, *refs):
    qseg, qpos = refs[:2]
    kseg, kpos = refs[2 : 2 + parts], refs[2 + parts : 2 + 2 * parts]
    rest = refs[2 + 2 * parts :]
    q_ref = rest[0]
    k_refs, v_refs = rest[1 : 1 + parts], rest[1 + parts : 1 + 2 * parts]
    o_ref, lse_ref = rest[1 + 2 * parts : 3 + 2 * parts]
    bias = rest[3 + 2 * parts : 3 + 3 * parts]
    ot_ref = rest[3 + 3 * parts]
    blk = pl.program_id(0)

    @pl.when(blk == 0)
    def _():
        for i in range(parts):
            fill_bias(qseg, qpos, kseg[i], kpos[i], bias[i])

    ot_ref[...] = jnp.zeros_like(ot_ref)
    lse_ref[...] = jnp.zeros_like(lse_ref)

    def one(sub):
        lane = lax.broadcasted_iota(jnp.int32, (1, LANES), 1)
        mine = (lane >= sub * HEAD) & (lane < (sub + 1) * HEAD)
        q = jnp.where(mine, q_ref[...] * 0.125, 0.0).astype(bf)
        scores = []
        best = None
        for i in range(parts):
            k = k_refs[i][...]
            s = dot(k, q, ((1,), (1,))) + bias[i][...]
            scores.append(s)
            top = jnp.max(s, axis=0, keepdims=True)
            best = top if best is None else jnp.maximum(best, top)
        total, acc = None, None
        for i in range(parts):
            p = jnp.exp(scores[i] - best)
            t = jnp.sum(p, axis=0, keepdims=True)
            v = v_refs[i][...]
            a = dot(v, p.astype(bf), ((0,), (0,)))
            total = t if total is None else total + t
            acc = a if acc is None else acc + a
        ot_ref[sub * HEAD : (sub + 1) * HEAD, :] = acc[sub * HEAD : (sub + 1) * HEAD, :] / total
        lse_ref[0, sub : sub + 1, :] = best + jnp.log(total)

    for sub in range(LANES // HEAD):
        pl.when(blk * (LANES // HEAD) + sub < heads)(functools.partial(one, sub))
    o_ref[...] = ot_ref[...].T.astype(bf)


def attn_specs(rows, key_rows, feats):
    blocks = -(-feats // LANES)
    row = pl.BlockSpec((1, rows), lambda h: (0, 0))
    cols = [pl.BlockSpec((n, 1), lambda h: (0, 0)) for n in key_rows]
    q = pl.BlockSpec((rows, LANES), lambda h: (0, h))
    ks = [pl.BlockSpec((n, LANES), lambda h: (0, h)) for n in key_rows]
    lse = pl.BlockSpec((1, 8, rows), lambda h: (h, 0, 0))
    return blocks, row, cols, q, ks, lse


def attention_fwd(q, keys, values, q_meta, k_metas, heads):
    rows, feats = q.shape
    parts = len(keys)
    key_rows = [k.shape[0] for k in keys]
    count = sum(key_rows)
    blocks, row, cols, qs, ks, lse = attn_specs(rows, key_rows, feats)
    return pl.pallas_call(
        functools.partial(attn_fwd_kernel, parts, heads),
        grid=(blocks,),
        out_shape=(
            jax.ShapeDtypeStruct((rows, feats), bf),
            jax.ShapeDtypeStruct((blocks, 8, rows), f32),
        ),
        in_specs=[row, row] + cols + cols + [qs] + ks + ks,
        out_specs=(qs, lse),
        scratch_shapes=[pltpu.VMEM((n, rows), f32) for n in key_rows] + [pltpu.VMEM((LANES, rows), f32)],
        compiler_params=pltpu.CompilerParams(vmem_limit_bytes=28 * MB),
        cost_estimate=COST,
    )(
        q_meta[0][None, :], q_meta[1][None, :],
        *[m[0][:, None] for m in k_metas], *[m[1][:, None] for m in k_metas],
        q, *keys, *values,
    )


def attn_bwd_kernel(parts, heads, *refs):
    qseg, qpos, qcos, qsin = refs[:4]
    refs = refs[4:]
    take = lambda n: (refs[:n], refs[n:])
    kseg, refs = take(parts)
    kpos, refs = take(parts)
    kcos, refs = take(parts)
    ksin, refs = take(parts)
    (q_ref, att_ref, do_ref, lse_ref), refs = take(4)
    k_refs, refs = take(parts)
    v_refs, refs = take(parts)
    (dq_ref,), refs = take(1)
    dk_refs, refs = take(parts)
    dv_refs, refs = take(parts)
    bias, refs = take(parts)
    dqt_ref, refs = refs[0], refs[1:]
    dka, refs = take(parts)
    dva, refs = take(parts)
    blk = pl.program_id(0)

    @pl.when(blk == 0)
    def _():
        for i in range(parts):
            fill_bias(qseg, qpos, kseg[i], kpos[i], bias[i])

    prod = (do_ref[...].astype(f32) * att_ref[...].astype(f32)).T
    dqt_ref[...] = jnp.zeros_like(dqt_ref)

    def one(sub):
        lane = lax.broadcasted_iota(jnp.int32, (1, LANES), 1)
        mine = (lane >= sub * HEAD) & (lane < (sub + 1) * HEAD)
        q = jnp.where(mine, q_ref[...] * 0.125, 0.0).astype(bf)
        do = jnp.where(mine, do_ref[...], 0.0).astype(bf)
        lse = lse_ref[0, sub : sub + 1, :]
        delta = jnp.sum(prod[sub * HEAD : (sub + 1) * HEAD, :], axis=0, keepdims=True)
        dqt = None
        for i in range(parts):
            k = k_refs[i][...]
            v = v_refs[i][...]
            p = jnp.exp(dot(k, q, ((1,), (1,))) + bias[i][...] - lse)
            dp = dot(v, do, ((1,), (1,)))
            ds = (p * (dp - delta)).astype(bf)
            dv = dot(p.astype(bf), do)
            dk = dot(ds, q)
            if sub == 0:
                dva[i][...] = dv
                dka[i][...] = dk
            else:
                dva[i][...] += dv
                dka[i][...] += dk
            d = dot(k, ds, ((0,), (0,)))
            dqt = d if dqt is None else dqt + d
        dqt_ref[sub * HEAD : (sub + 1) * HEAD, :] = dqt[sub * HEAD : (sub + 1) * HEAD, :] * 0.125

    for sub in range(LANES // HEAD):
        pl.when(blk * (LANES // HEAD) + sub < heads)(functools.partial(one, sub))
    dq_ref[...] = rope_block(dqt_ref[...].T, qcos[...], qsin[...], -1.0).astype(bf)
    for i in range(parts):
        dk_refs[i][...] = rope_block(dka[i][...], kcos[i][...], ksin[i][...], -1.0).astype(bf)
        dv_refs[i][...] = dva[i][...].astype(bf)


def attention_bwd(q, att, grad_att, lse, keys, values, q_meta, k_metas, heads):
    rows, feats = q.shape
    parts = len(keys)
    key_rows = [k.shape[0] for k in keys]
    count = sum(key_rows)
    blocks, row, cols, qs, ks, lses = attn_specs(rows, key_rows, feats)
    tab = pl.BlockSpec((rows, LANES), lambda h: (0, 0))
    tabs = [pl.BlockSpec((n, LANES), lambda h: (0, 0)) for n in key_rows]
    out = pl.pallas_call(
        functools.partial(attn_bwd_kernel, parts, heads),
        grid=(blocks,),
        out_shape=(jax.ShapeDtypeStruct((rows, feats), bf),)
        + tuple(jax.ShapeDtypeStruct((n, feats), bf) for n in key_rows) * 2,
        in_specs=[row, row, tab, tab] + cols + cols + tabs + tabs + [qs, qs, qs, lses] + ks + ks,
        out_specs=(qs,) + tuple(ks) + tuple(ks),
        scratch_shapes=[pltpu.VMEM((n, rows), f32) for n in key_rows]
        + [pltpu.VMEM((LANES, rows), f32)]
        + [pltpu.VMEM((n, LANES), f32) for n in key_rows] * 2,
        compiler_params=pltpu.CompilerParams(vmem_limit_bytes=40 * MB),
        cost_estimate=COST,
    )(
        q_meta[0][None, :], q_meta[1][None, :], q_meta[2], q_meta[3],
        *[m[0][:, None] for m in k_metas], *[m[1][:, None] for m in k_metas],
        *[m[2] for m in k_metas], *[m[3] for m in k_metas],
        q, att, grad_att, lse, *keys, *values,
    )
    return out[0], out[1 : 1 + parts], out[1 + parts :]


def swap(n, bit):
    return [(i, i ^ bit) for i in range(n)]


def power_of_two(n):
    return n & (n - 1) == 0


def sum_all(value, sizes):
    for axis, n in sizes:
        if power_of_two(n):
            bit = 1
            while bit < n:
                value = value + lax.ppermute(value, axis, swap(n, bit))
                bit *= 2
        else:
            value = lax.psum(value, axis)
    return value


def after(value, *others):
    return lax.optimization_barrier((value,) + others)[0]


def scatter_sum(array):
    return lax.psum_scatter(array, "tensor", scatter_dimension=0, tiled=True).astype(f32)


def gather_rows(array):
    return lax.all_gather(array, "tensor", axis=0, tiled=True)


def gather_weight(shard, n, offs, late=()):
    if n != 4:
        whole = lax.all_gather(shard, "dp", axis=0, tiled=True)
        return offs, [whole], whole
    raw = lax.ppermute(shard, "dp", swap(4, 2))
    far = after(raw, *late)
    near = lax.ppermute(shard, "dp", swap(4, 1))
    cross = lax.ppermute(far, "dp", swap(4, 1))
    return offs, [shard, near, far, cross], raw


def lockstep(items, waits):
    firsts, seconds, before = [], [], ()
    for step in range(len(items) + 1):
        now = []
        if step in waits:
            before += waits[step](firsts, seconds)
        if step > 0:
            seconds.append(lax.ppermute(after(firsts[-1], *before), "ctx", swap(2, 1)))
            now.append(seconds[-1])
        if step < len(items):
            firsts.append(lax.ppermute(after(items[step], *before), "dp", swap(4, 2)))
            now.append(firsts[-1])
        before = tuple(now)
    return firsts, seconds


def two_halves(shard, n, n_ctx, ctx, first, second, offs):
    half = shard.shape[1] // 2
    cross = lambda a: lax.ppermute(a, "dp", swap(4, 1))
    out = []
    for place, piece in ((ctx * half, first), ((1 - ctx) * half, second)):
        out += [(offs[2] + place, piece), (offs[3] + place, cross(piece))]
    return out


class WeightGrad:
    def __init__(self, n, n_ctx, offs):
        self.n, self.n_ctx, self.offs = n, n_ctx, offs

    def make(self, left, right):
        if self.n == 4:
            self.keep, self.first = weight_grad(left, right, self.offs)
        else:
            self.first = self.far = self.whole = dot(left, right, ((0,), (0,))).astype(bf)
        return self

    def trade(self, *late):
        if self.n == 4:
            self.got = lax.ppermute(after(self.first, *late), "dp", swap(4, 1))
            self.far = add_halves((self.keep, self.got), (), 1)
        return self

    def start(self, left, right):
        return self.make(left, right).trade()

    def start_x(self):
        if self.n == 4:
            self.raw = lax.ppermute(self.far, "dp", swap(4, 2))
        else:
            self.raw = lax.psum_scatter(self.whole, "dp", scatter_dimension=0, tiled=True)
        return self.raw

    def finish_x(self, *late):
        other = after(self.raw, *late)
        if self.n == 4:
            other = add_halves((self.keep, self.got), (other,), 0)
        self.total = lax.optimization_barrier(other)
        return self.total

    def along_x(self, *late):
        self.start_x()
        return self.finish_x(*late)

    def along_y(self, *late):
        if self.n_ctx == 2:
            self.other = lax.ppermute(after(self.total, *late), "ctx", swap(2, 1))
        else:
            self.other = lax.psum(self.total, "ctx")
        return self.other

    def along_y_halves(self, first, *late):
        if self.n_ctx != 2:
            return self.along_y()
        half = self.total.shape[0] // 2
        parts = [after(self.total[:half], *first), after(self.total[half:], *late)]
        parts = [lax.ppermute(p, "ctx", swap(2, 1)) for p in parts]
        self.other = jnp.concatenate(parts)
        return parts[0]

    def finish(self, size, *before):
        other = after(self.other, *before).astype(f32)
        out = self.total.astype(f32) + other if self.n_ctx == 2 else other
        return out[:, :size]


def per_device(
    n_dp, n_ctx, n_tp,
    tokens, segment, position, gain_attn, w_query, w_key, w_value, w_out, gain_ffn, w_gate, w_up, w_down, cotangent,
):
    dp, ctx, me = lax.axis_index("dp"), lax.axis_index("ctx"), lax.axis_index("tensor")
    rows = tokens.shape[0]
    piece = rows // n_tp
    shard = gain_attn.shape[0]
    feats, hidden_dev = w_query.shape[1], w_gate.shape[1]
    feats_pad, hidden_pad = up_to(feats, LANES), up_to(hidden_dev, 256)
    mine = functools.partial(lax.dynamic_slice_in_dim, start_index=me * piece, slice_size=piece, axis=0)
    offs = jnp.stack([(dp ^ j) * shard for j in range(4)]) if n_dp == 4 else jnp.zeros((4,), jnp.int32)

    def padded(w, width):
        return jnp.pad(w.astype(bf), ((0, 0), (0, width - w.shape[1])))

    wo_all = lax.all_gather(padded(w_out.T, feats_pad), "tensor", axis=0, tiled=False)
    wk_b = jnp.pad(w_key.astype(bf), ((0, 16), (0, feats_pad - feats)))
    gain_rows = jnp.pad(jnp.stack([gain_attn, gain_ffn]).astype(bf), ((0, 0), (0, feats_pad - shard)))
    wk_b = lax.dynamic_update_slice(wk_b, gain_rows, (shard, 0))
    v_cast, q_cast = padded(w_value, feats_pad), padded(w_query, feats_pad)
    _, wk_ext, raw_k = gather_weight(wk_b, n_dp, offs, (v_cast, q_cast))
    if n_dp == 4:
        own = jnp.stack([w[shard : shard + 2, :shard] for w in wk_ext])
        gains = jnp.zeros((2, n_dp * shard), f32)
        for j in range(4):
            gains = lax.dynamic_update_slice(gains, own[j].astype(f32), (0, offs[j]))
        wk = (offs, wk_ext)
    else:
        ext = wk_ext[0].reshape(n_dp, shard + 16, feats_pad)
        gains = ext[:, shard : shard + 2, :shard].transpose(1, 0, 2).reshape(2, n_dp * shard).astype(f32)
        wk = (offs, [ext[:, :shard].reshape(n_dp * shard, feats_pad)])
    gain1, gain2 = gains[0], gains[1]
    def meta(start, size):
        seg = lax.dynamic_slice_in_dim(segment, start, size)
        pos = lax.dynamic_slice_in_dim(position, start, size)
        return (seg, pos) + rope_tables(pos)

    q_meta = meta(ctx * rows, rows)
    cos_t, sin_t = q_meta[2:]
    inputs = tokens.astype(f32)
    scale1 = lax.rsqrt(jnp.mean(inputs * inputs, axis=-1, keepdims=True) + norm_eps)
    normed1 = (inputs * scale1 * gain1).astype(bf)
    keys = project(normed1, wk, cos_t, sin_t, True)
    *wv, raw_v = gather_weight(after(v_cast, raw_k), n_dp, offs, (keys,))
    values = project(normed1, wv, cos_t, sin_t, False)
    if n_ctx == 2:
        trade = lambda a: lax.ppermute(a, "ctx", swap(2, 1))
        keys_all = [keys, trade(keys)]
        values_all = [values, trade(after(values, keys_all[1]))]
        k_metas = [q_meta, meta((1 - ctx) * rows, rows)]
        early = (values_all[1],)
    else:
        spread = lambda a: [lax.all_gather(a, "ctx", axis=0, tiled=True)]
        keys_all, values_all = spread(keys), spread(values)
        k_metas = [meta(0, segment.shape[0])]
        early = (values,)
    wide = [padded(w, hidden_pad) for w in (w_down.T, w_gate, w_up)]
    half, mid = shard // 2, n_tp // 2
    items = []
    if n_dp == 4 and n_ctx == 2:
        cut = lambda a: lax.dynamic_slice_in_dim(a, ctx * half, half, a.ndim - 2)
        items = [cut(wide[0]), cut(wo_all[:mid]), cut(wo_all[mid:]), cut(wide[1]), cut(wide[2])]
    *wq, raw_q = gather_weight(after(q_cast, wv[1][-2] if n_dp == 4 else raw_v), n_dp, offs, early + tuple(wide) + tuple(t for m in k_metas for t in m[2:]))
    grad_ffn = (branch_scale * cotangent.astype(f32)).astype(bf)
    if n_dp == 4 and n_ctx == 2:
        near = lambda a: lax.ppermute(a, "dp", swap(4, 1))
        items[0] = after(items[0], raw_q)
        query = project(normed1, wq, cos_t, sin_t, True)
        early = []

        def shards_of(own, first, second):
            got = two_halves(own[None], n_dp, n_ctx, ctx, first, second, offs)
            places, pieces = zip((offs[0], own), (offs[1], near(own)), *got)
            return jnp.stack(places), list(pieces)

        def attend(firsts, seconds):
            early.append(attention_fwd(query, keys_all, values_all, q_meta, k_metas, feats // HEAD))
            return (early[0][0],)

        def work_ahead(firsts, seconds):
            wd = shards_of(wide[0], firsts[0], seconds[0])
            early.extend((wd, wide_matmul(after(grad_ffn, firsts[2]), wd, False, f32)))
            return (early[2],)

        waits = {1: lambda f, s: (query, values_all[1]), 2: attend, 4: work_ahead}
        firsts, seconds = lockstep(items, waits)
        att, lse = early.pop(0)
        wd, grad_hidden = early
        wg = shards_of(wide[1], firsts[3], seconds[3])
        places, wo_pieces = [offs[0], offs[1]], [((0, n_tp), wo_all), ((0, n_tp), near(wo_all))]
        for k, span in ((1, (0, mid)), (2, (mid, n_tp))):
            for place, got in two_halves(wo_all, n_dp, n_ctx, ctx, firsts[k], seconds[k], offs):
                places.append(place)
                wo_pieces.append((span, got))
        places = jnp.stack(places)
        late = (firsts[4], seconds[3])
    else:
        wd, wg, wu = [gather_weight(w, n_dp, offs)[:2] for w in wide]
        places, wo_pieces = offs[:1] * 0, [((0, n_tp), lax.all_gather(wo_all, "dp", axis=1, tiled=True))]
        late = ()
        query = project(normed1, wq, cos_t, sin_t, True)
        att, lse = attention_fwd(query, keys_all, values_all, q_meta, k_metas, feats // HEAD)
        grad_hidden = wide_matmul(grad_ffn, wd, False, f32)
    att_all = after(lax.all_gather(att, "tensor", axis=0, tiled=False), *late)
    my_in, my_scale = mine(tokens).astype(f32), mine(scale1)
    normed2, hidden_in, wo_dev = mix(att_all, tokens, gain2, places, wo_pieces, me)
    if n_dp == 4 and n_ctx == 2:
        wu = shards_of(wide[2], firsts[4], after(seconds[4], normed2))
    scale2 = lax.rsqrt(jnp.mean(hidden_in * hidden_in, axis=-1, keepdims=True) + norm_eps)

    hidden, grad_gate, grad_up, partial2 = ffn(normed2, grad_hidden, wg, wu)
    make = lambda: WeightGrad(n_dp, n_ctx, offs)
    grad_d = make().start(grad_ffn, hidden)
    ffn_part = wide_matmul(hidden, wd, True, bf)
    grad_g = make().start(after(normed2, grad_d.far, ffn_part), grad_gate)
    grad_norm2 = scatter_sum(partial2)
    grad_d.along_x(grad_norm2)
    grad_norm2 = after(grad_norm2, grad_d.raw, ffn_part, grad_g.first)
    part_g2 = jnp.sum(grad_norm2 * hidden_in * scale2, axis=0)
    grad_h = (
        mine(cotangent).astype(f32)
        + scale2 * gain2 * grad_norm2
        - hidden_in * scale2**3 * jnp.mean(hidden_in * gain2 * grad_norm2, axis=-1, keepdims=True)
    )
    local_mixed = (branch_scale * grad_h).astype(bf)
    grad_mixed = gather_rows(local_mixed)

    grad_u = make().start(after(normed2, local_mixed), grad_up)
    grad_mixed = after(grad_mixed, grad_d.along_y(), grad_g.along_x(), grad_u.far)
    ffn_part = scatter_sum(after(ffn_part, grad_mixed))

    grad_att = row_matmul(grad_mixed, wo_dev)
    back = lambda k, v, m: attention_bwd(query, att, grad_att, lse, k, v, q_meta, m, feats // HEAD)
    if n_ctx == 2:
        grad_q1, grad_k1, grad_v1 = back(keys_all[1:], values_all[1:], k_metas[1:])
        grad_o = make().start(after(grad_mixed, grad_q1), att)
        grad_att = after(grad_att, grad_o.got, grad_u.start_x())
        grad_q0, grad_k0, grad_v0 = back(keys_all[:1], values_all[:1], k_metas[:1])
        grad_q = (grad_q0.astype(f32) + grad_q1.astype(f32)).astype(bf)
        grad_ks, grad_vs = grad_k0 + grad_k1, grad_v0 + grad_v1
    else:
        grad_u.start_x()
        grad_q, grad_ks, grad_vs = back(keys_all, values_all, k_metas)
        grad_o = make().start(grad_mixed, att)
    if n_ctx == 2:
        merge = lambda pair: (pair[0].astype(f32) + trade(pair[1]).astype(f32)).astype(bf)
    else:
        merge = lambda whole: lax.psum_scatter(whole[0], "ctx", scatter_dimension=0, tiled=True)
    grad_k, grad_v = merge(grad_ks), merge(grad_vs)

    output = (hidden_in + branch_scale * after(ffn_part, grad_q)).astype(bf)
    rounds = [lax.optimization_barrier(output)]
    total_u, total_o = grad_u.finish_x(grad_q), grad_o.along_x()
    partial1, part_g1 = qkv_back((grad_q, grad_k, grad_v), (wq, wk, wv), tokens, scale1)
    ring = [(i, (i + 1) % n_tp) for i in range(n_tp)]
    step = lambda *before: rounds.append(lax.ppermute(after(rounds[-1], *before), "tensor", ring)) or rounds[-1]
    rest = n_tp - 1
    grad_norm1 = scatter_sum(after(partial1, *([step()] if rest > 0 else [])))
    grads_a = [make().start(normed1, g) for g in (grad_q, grad_k, grad_v)]
    totals = [g.along_x() for g in grads_a[:2]]
    grad_g.along_y(grad_k, grad_v)
    part_u = grad_u.along_y_halves((grad_g.other, grads_a[0].raw))
    beside = [step()] if rest > 1 else []
    grad_norm1 = after(grad_norm1, *totals, grad_g.other, part_u, *beside)
    grad_o.along_y()
    grad_in = (
        grad_h
        + my_scale * gain1 * grad_norm1
        - my_in * my_scale**3 * jnp.mean(my_in * gain1 * grad_norm1, axis=-1, keepdims=True)
    )
    local_in = lax.optimization_barrier(grad_in.astype(bf))
    grads_a[2].along_x(local_in)
    grad_in = widen(gather_rows(local_in))
    while len(rounds) < n_tp:
        step(local_in)
    output = assemble(rounds, me)
    gain_sum = after(jnp.concatenate([part_g1, part_g2[None, :]]), local_in)
    gain_sum = sum_all(gain_sum, (("tensor", n_tp), ("dp", n_dp)))
    gain_sum = sum_all(after(gain_sum, output), (("ctx", n_ctx),))
    gain_sum = lax.dynamic_slice_in_dim(gain_sum, dp * shard, shard, 1)

    for g in grads_a:
        g.along_y()
    sum_wd = grad_d.finish(hidden_dev, local_in).T
    sum_wg, sum_wu = grad_g.finish(hidden_dev, local_in), grad_u.finish(hidden_dev, local_in)
    sum_wo = grad_o.finish(feats, local_in, rounds[-1]).T
    sum_wq, sum_wk, sum_wv = [g.finish(feats, local_in) for g in grads_a]
    return (output, grad_in, gain_sum[0], sum_wq, sum_wk, sum_wv, sum_wo, gain_sum[1], sum_wg, sum_wu, sum_wd)


def solution(mesh):
    rows, col, row = P(("dp", "ctx"), None), P("dp", "tensor"), P("tensor", "dp")
    sizes = (mesh.shape["dp"], mesh.shape["ctx"], mesh.shape["tensor"])
    return jax.shard_map(
        functools.partial(per_device, *sizes),
        mesh=mesh,
        in_specs=(rows, P("dp"), P("dp"), P("dp"), col, col, col, row, P("dp"), col, col, row, rows),
        out_specs=(rows, rows, P("dp"), col, col, col, row, P("dp"), col, col, row),
        check_vma=False,
    )
```
